32 devices in a mesh: dp: 16 (over z, y, x), tensor: 2 (over core).
Axes of the slice: x: 2, y: 2, z: 4, core: 2. Of those that a mesh axis runs over, the one named last changes fastest.
Arguments:
- inputs: bfloat16 [16384, 768], P(('dp', 'tensor')), may hold values from -9 to 9, as said below
- row_lengths: int32 [128], P('dp'), may hold values from 0 to 512, as said below
- project_weight: bfloat16 [768, 3, 768], P(None, None, 'tensor'), may hold values from -0.21875 to 0.21875
- merge_weight: bfloat16 [768, 768], P('tensor'), may hold values from -1.75 to 1.75
- up_weight: bfloat16 [768, 3072], P(None, 'tensor'), may hold values from -0.21875 to 0.21875
- down_weight: bfloat16 [3072, 768], P('tensor'), may hold values from -0.109375 to 0.109375
- query_value_bias: float32 [2, 768], P(None, 'tensor'), may hold values from -1.5 to 1.5
- merge_bias: float32 [768], replicated, may hold values from -1.5 to 1.5
- up_bias: float32 [3072], P('tensor'), may hold values from -1.5 to 1.5
- down_bias: float32 [768], replicated, may hold values from -1.5 to 1.5
- norm_gains: float32 [2, 768], replicated, may hold values from 0.5 to 1.5
- norm_shifts: float32 [2, 768], replicated, may hold values from -1 to 1
- clip_scales: float32 [3], replicated, may hold values from 2 to 5
- cotangent: bfloat16 [16384, 768], P(('dp', 'tensor')), may hold values from -6 to 6
Outputs:
- output: bfloat16 [16384, 768], P(('dp', 'tensor'))
- input_grad: float32 [16384, 768], P(('dp', 'tensor'))
- project_grad: float32 [768, 3, 768], P(None, None, 'tensor')
- merge_grad: float32 [768, 768], P('tensor')
- up_grad: float32 [768, 3072], P(None, 'tensor')
- down_grad: float32 [3072, 768], P('tensor')
- query_value_bias_grad: float32 [2, 768], P(None, 'tensor')
- merge_bias_grad: float32 [768], replicated
- up_bias_grad: float32 [3072], P('tensor')
- down_bias_grad: float32 [768], replicated
- gain_grad: float32 [2, 768], replicated
- shift_grad: float32 [2, 768], replicated
- new_scales: float32 [3], replicated
The draws below stay inside these ranges and needn't reach their ends.
Inputs may be any that keep to these rules, and one draw needn't show every extreme that they name: `row_lengths`: each aligned block of 512 entries-worth of slots (4 entries) holds either one row, whose length (more than 128) is in its first entry with zeros in the others, or 4 rows whose lengths (at least 1) are in their entries. Some row has 512 tokens. `inputs`: activations of order one.
All inputs are finite; a program needn't handle non-finite values.
Results may differ from the reference program's by a relative error of at most 0.014.
The reference program's roundings to bfloat16 on the way count: a program that leaves them out, or rounds other values in their place, can miss the bound.
Values may be sent and summed in bfloat16 or wider, within the bound.
No kernel may reach another device: no remote copies, remote signals or barrier semaphores. Data moves between devices by JAX's collectives and lax.ppermute only.
A program may use at most 128 MiB of HBM per device.

```python
import math
import jax
import jax.numpy as jnp
from jax import lax

D = 768
HEADS = 12
HEAD = 64
FF = 3072
LONG = 512
SHORT = 128
TOK_DEV = 1024
TOKENS = 16384


def draw_inputs(key, part):
    key = jax.random.fold_in(key, 11)
    base_key, rough_key = jax.random.split(key)
    place = jnp.arange(TOKENS, dtype=jnp.float32) / max(TOKENS - 1, 1)
    rise = 0.6 * jnp.power(3.0, place)
    rough = jax.random.uniform(rough_key, (TOKENS, 1), jnp.float32, 0.8, 1.2)
    base = jnp.clip(jax.random.normal(base_key, (TOKENS, D), jnp.float32), -4.0, 4.0)
    return (base * rise[:, None] * rough).astype(jnp.bfloat16)


def draw_row_lengths(key, part):
    key = jax.random.fold_in(key, 5)
    kind_key, forced_key, long_key, short_key = jax.random.split(key, 4)
    blocks = TOKENS // LONG
    slots = LONG // SHORT
    numbers = jnp.arange(blocks, dtype=jnp.int32)
    forced = jax.random.randint(forced_key, (), 0, blocks)
    single = (jax.random.randint(kind_key, (blocks,), 0, 4) == 0) | (numbers == forced)
    long_length = jax.random.randint(long_key, (blocks,), LONG // 2, LONG + 1)
    long_length = jnp.where(numbers == forced, LONG, long_length)
    short_length = jax.random.randint(short_key, (blocks, slots), SHORT // 2, SHORT + 1)
    slot_place = jnp.arange(slots, dtype=jnp.int32)
    long_rows = jnp.where(slot_place[None, :] == 0, long_length[:, None], 0)
    return jnp.where(single[:, None], long_rows, short_length).reshape(-1).astype(jnp.int32)


def block_scale(stream_key, dims, pieces, least, high):
    loudness, own = 1.0, jax.random.fold_in(stream_key, 6)
    for dim, blocks in pieces:
        heights = jnp.exp(jax.random.uniform(jax.random.fold_in(own, dim), (blocks,), jnp.float32, least / len(pieces), high / len(pieces)))
        loudness = loudness * jnp.repeat(heights, dims[dim] // blocks).reshape([-1 if axis == dim else 1 for axis in range(len(dims))])
    return loudness


def bell_draw(stream_key, extent, width, most, cuts=(), held_as=jnp.bfloat16):
    values = width * jax.random.normal(stream_key, extent, jnp.float32)
    if cuts:
        values = values * block_scale(stream_key, extent, cuts, -0.22, 0.18)
    return jnp.clip(values, -most, most).astype(held_as)


def setup_inputs(seed: int = 0) -> dict:
    splits = jax.random.split(jax.random.key(seed), 15)
    inputs = draw_inputs(jax.random.fold_in(splits[14], 71), 0)
    row_lengths = draw_row_lengths(jax.random.fold_in(splits[14], 71), 0)
    project_weight = bell_draw(splits[2], (D, 3, D), D ** -0.5, 0.21875, ((2, 2),))
    merge_weight = bell_draw(splits[3], (D, D), (D // 64) ** -0.5, 1.75, ((0, 2),))
    up_weight = bell_draw(splits[4], (D, FF), D ** -0.5, 0.21875, ((1, 2),))
    down_weight = bell_draw(splits[5], (FF, D), FF ** -0.5, 0.109375, ((0, 2),))
    query_value_bias = bell_draw(splits[6], (2, D), 0.3, 1.5, ((1, 2),), jnp.float32)
    merge_bias = bell_draw(splits[7], (D,), 0.3, 1.5, (), jnp.float32)
    up_bias = bell_draw(splits[8], (FF,), 0.3, 1.5, ((0, 2),), jnp.float32)
    down_bias = bell_draw(splits[9], (D,), 0.3, 1.5, (), jnp.float32)
    norm_gains = jnp.clip(1.0 + 0.1 * jax.random.normal(splits[10], (2, D), jnp.float32), 0.5, 1.5)
    norm_shifts = bell_draw(splits[11], (2, D), 0.2, 1.0, (), jnp.float32)
    clip_scales = jnp.clip(jnp.exp(jax.random.uniform(splits[12], (3,), jnp.float32, math.log(2.0), math.log(5.0))), 2.0, 5.0)
    cotangent = bell_draw(splits[13], (TOKENS, D), 1.0, 6.0, ((0, 32),))
    return {"inputs": inputs, "row_lengths": row_lengths, "project_weight": project_weight, "merge_weight": merge_weight, "up_weight": up_weight, "down_weight": down_weight, "query_value_bias": query_value_bias, "merge_bias": merge_bias, "up_bias": up_bias, "down_bias": down_bias, "norm_gains": norm_gains, "norm_shifts": norm_shifts, "clip_scales": clip_scales, "cotangent": cotangent}


@jax.custom_vjp
def low(v):
    return lax.optimization_barrier(v.astype(jnp.bfloat16)).astype(jnp.float32)

@jax.custom_vjp
def low_back(v):
    return v

def low_keep(v):
    return (low(v), None)

def low_pass(kept, grad):
    return (grad,)

def back_keep(v):
    return (v, None)

def back_low(kept, grad):
    return (low(grad),)
low.defvjp(low_keep, low_pass)
low_back.defvjp(back_keep, back_low)
EPSILON = 1e-12
DECAY = 0.9
HIGHEST = lax.Precision.HIGHEST

def softclip(value, scale):
    return scale * jnp.tanh(value / scale)

def layer_norm(value, gain, shift):
    mean = lax.optimization_barrier(jnp.mean(value, axis=-1, keepdims=True))
    centred = value - mean
    spread = lax.optimization_barrier(jnp.mean(centred * centred, axis=-1, keepdims=True))
    return centred * lax.rsqrt(spread + EPSILON) * gain + shift

def block_mask(lengths):
    places = jnp.arange(LONG, dtype=jnp.int32)
    single = lengths[0] > SHORT
    per_slot = jnp.repeat(lengths, SHORT, total_repeat_length=LONG)
    member = jnp.where(single, 0, places // SHORT)
    inner = jnp.where(single, places, places % SHORT)
    limit = jnp.where(single, lengths[0], per_slot)
    usable = inner < limit
    return (member[:, None] == member[None, :]) & usable[None, :]

def attend_block(parts):
    queries, key_rows, values, lengths = parts
    scores = jnp.einsum('qhd,khd->hqk', queries, key_rows, precision=HIGHEST) * 0.125
    scores = low_back(scores)
    masked = jnp.where(block_mask(lengths)[None], scores, -1e+30)
    weights = low(jax.nn.softmax(masked, axis=-1))
    return jnp.einsum('hqk,khd->qhd', weights, values, precision=HIGHEST)

def group_forward(params, rows, lengths, weight_scales, clip_scales):
    project, merge, upward, downward, qv_bias, merge_bias, up_bias, down_bias, gains, shifts = params
    project_q = low(softclip(project, weight_scales[0:3][None, :, None]))
    merge_q = low(softclip(merge, weight_scales[3]))
    up_q = low(softclip(upward, weight_scales[4]))
    down_q = low(softclip(downward, weight_scales[5]))
    quantized = low(softclip(rows, clip_scales[0]))
    projected = jnp.einsum('td,dcf->tcf', quantized, project_q, precision=HIGHEST)
    queries = low_back(low(projected[:, 0] + qv_bias[0]))
    key_rows = low_back(low(projected[:, 1]))
    values = low_back(low(projected[:, 2] + qv_bias[1]))
    count = rows.shape[0]
    blocks = count // LONG
    block_shape = (blocks, LONG, HEADS, HEAD)
    context = lax.map(jax.checkpoint(attend_block), (queries.reshape(block_shape), key_rows.reshape(block_shape), values.reshape(block_shape), lengths.reshape(blocks, LONG // SHORT)))
    context = low_back(low(context.reshape(count, D)))
    branch = low_back(jnp.dot(context, merge_q, precision=HIGHEST))
    normed = layer_norm(rows + branch + merge_bias, gains[0], shifts[0])
    normed_q = low(softclip(normed, clip_scales[1]))
    hidden = low_back(jnp.dot(normed_q, up_q, precision=HIGHEST) + up_bias)
    active = jax.nn.gelu(hidden, approximate=False)
    active_q = low(softclip(active, clip_scales[2]))
    feed = low_back(jnp.dot(active_q, down_q, precision=HIGHEST))
    result = layer_norm(normed + feed + down_bias, gains[1], shifts[1])
    peaks = jnp.stack([jnp.max(jnp.abs(rows)), jnp.max(jnp.abs(normed)), jnp.max(jnp.abs(active))])
    return (result, peaks)

def reference(inputs, row_lengths, project_weight, merge_weight, up_weight, down_weight, query_value_bias, merge_bias, up_bias, down_bias, norm_gains, norm_shifts, clip_scales, cotangent):
    params = tuple((array.astype(jnp.float32) for array in (project_weight, merge_weight, up_weight, down_weight, query_value_bias, merge_bias, up_bias, down_bias, norm_gains, norm_shifts)))
    weight_scales = 0.5 * jnp.stack([jnp.max(jnp.abs(params[0][:, 0])), jnp.max(jnp.abs(params[0][:, 1])), jnp.max(jnp.abs(params[0][:, 2])), jnp.max(jnp.abs(params[1])), jnp.max(jnp.abs(params[2])), jnp.max(jnp.abs(params[3]))])
    groups = TOKENS // TOK_DEV
    rows_all = inputs.astype(jnp.float32).reshape(groups, TOK_DEV, D)
    grads_all = cotangent.astype(jnp.float32).reshape(groups, TOK_DEV, D)
    lengths_all = row_lengths.reshape(groups, TOK_DEV // SHORT)

    def step(carry, item):
        totals, peaks = carry
        rows, lengths, upstream = item

        def forward(weights, values):
            return group_forward(weights, values, lengths, weight_scales, clip_scales)
        result, pullback, group_peaks = jax.vjp(forward, params, rows, has_aux=True)
        param_grads, row_grad = pullback(upstream)
        totals = jax.tree.map(jnp.add, totals, param_grads)
        return ((totals, jnp.maximum(peaks, group_peaks)), (result.astype(jnp.bfloat16), row_grad))
    zeros = jax.tree.map(jnp.zeros_like, params)
    (totals, peaks), (outputs, row_grads) = lax.scan(step, (zeros, jnp.zeros((3,), jnp.float32)), (rows_all, lengths_all, grads_all))
    new_scales = DECAY * clip_scales + (1.0 - DECAY) * peaks
    return (outputs.reshape(TOKENS, D), row_grads.reshape(TOKENS, D), totals[0], totals[1], totals[2], totals[3], totals[4], totals[5], totals[6], totals[7], totals[8], totals[9], new_scales)
```

```python
from functools import partial

import jax
import jax.numpy as jnp
from jax import lax
from jax.experimental import pallas as pl
from jax.experimental.pallas import tpu as pltpu
from jax.sharding import PartitionSpec as P

HEAD = 64
LONG = 512
SHORT = 128
EPSILON = 1e-12
DECAY = 0.9
F32 = jnp.float32
BF16 = jnp.bfloat16
VMEM = pl.BlockSpec(memory_space=pltpu.VMEM)
SMEM = pl.BlockSpec(memory_space=pltpu.SMEM)
LANES = 384
TILE = 64


def dot(a, b, ca, cb):
    return lax.dot_general(a, b, (((ca,), (cb,)), ((), ())), preferred_element_type=F32)


def shaped(shape, dtype):
    return jax.ShapeDtypeStruct(shape, dtype)


def call(body, out_shape, ins, flops, scratch=(), grid_spec=None, in_specs=None, out_specs=None):
    nbytes = sum(a.size * a.dtype.itemsize for a in ins)
    nbytes += sum(o.size * o.dtype.itemsize for o in jax.tree.leaves(out_shape))
    params = dict(
        out_shape=out_shape,
        compiler_params=pltpu.CompilerParams(vmem_limit_bytes=56 << 20),
        cost_estimate=pl.CostEstimate(flops=int(flops), bytes_accessed=nbytes, transcendentals=0),
    )
    if grid_spec is not None:
        return pl.pallas_call(body, grid_spec=grid_spec, **params)(*ins)
    return pl.pallas_call(
        body, in_specs=in_specs, out_specs=out_specs, scratch_shapes=list(scratch), **params
    )(*ins)


def peaks_body(project, merge, up, down, qv_bias, up_bias, pack):
    step = pl.program_id(0)

    @pl.when(step == 0)
    def _():
        pack[...] = jnp.zeros_like(pack)
        pack[0:1, :] = up_bias[...]
        pack[1:3, 0:LANES] = qv_bias[...]

    def peak(value):
        top = jnp.max(jnp.abs(value.astype(F32)), axis=0, keepdims=True)
        return jnp.max(top, axis=1, keepdims=True)

    parts = [peak(project[0]), peak(project[1]), peak(project[2])]
    parts += [peak(merge[...]), peak(up[...]), peak(down[...])]
    for row, part in enumerate(parts):
        at = slice(8 + row, 9 + row)
        pack[at, :] = jnp.maximum(pack[at, :], part)


def scale_row(own, other, row, width):
    at = slice(8 + row, 9 + row)
    return 0.5 * jnp.maximum(own[at, 0:width], other[at, 0:width])


def clip_tile(value, scale):
    return (scale * jnp.tanh(value.astype(F32) / scale)).astype(BF16)


def clip_project_body(own, other, project, out):
    for part in range(3):
        scale = scale_row(own, other, part, LANES)
        out[part] = clip_tile(project[part], scale)


def clip_rest_body(own, other, merge, up, down, merge_q, up_q, down_q):
    for row, (src, dst) in enumerate(((merge, merge_q), (up, up_q), (down, down_q))):
        dst[...] = clip_tile(src[...], scale_row(own, other, 3 + row, src.shape[1]))


def key_bias(lengths, first):
    key = lax.broadcasted_iota(jnp.int32, (LONG, 1), 0)
    query = lax.broadcasted_iota(jnp.int32, (1, LONG), 1)
    single = lengths[first] > SHORT
    limit = jnp.full((LONG, 1), lengths[first], jnp.int32)
    for slot in range(1, LONG // SHORT):
        own = jnp.where(single, lengths[first], slot * SHORT + lengths[first + slot])
        limit = jnp.where(key >= slot * SHORT, own, limit)
    key_row = jnp.where(single, 0, key // SHORT)
    query_row = jnp.where(single, 0, query // SHORT)
    key_row = jnp.where(key < limit, key_row, -1)
    return jnp.where(key_row == query_row, 0.0, -1e30).astype(F32)


def qkv_into(xq, weight, bias_pack, q_ref, k_ref, v_ref):
    for part, ref in enumerate((q_ref, k_ref, v_ref)):
        value = dot(xq, weight[part], 1, 0)
        if part == 0:
            value = value + bias_pack[1:2, 0:LANES]
        if part == 2:
            value = value + bias_pack[2:3, 0:LANES]
        value = value.astype(BF16)
        if part == 0:
            value = value * jnp.asarray(0.125, BF16)
        ref[...] = value.T


def attend(lengths, first, q_ref, k_ref, v_ref, c_ref, lse_ref, bias_ref):
    bias_ref[...] = key_bias(lengths, first)

    def head(index, carry):
        at = pl.ds(pl.multiple_of(index * HEAD, HEAD), HEAD)
        scores = dot(k_ref[at, :], q_ref[at, :], 0, 0) + bias_ref[...]
        top = jnp.max(scores, axis=0, keepdims=True)
        prob = jnp.exp(scores - top)
        total = jnp.sum(prob, axis=0, keepdims=True)
        mixed = dot(v_ref[at, :], prob.astype(BF16), 1, 0)
        c_ref[at, :] = (mixed * (1.0 / total)).astype(BF16)
        lse_ref[pl.ds(index, 1), :] = top + jnp.log(total)
        return carry

    lax.fori_loop(0, q_ref.shape[0] // HEAD, head, 0)


def forward_first_body(
    ids, lengths, clips, inputs, weight, pack, xq, q_ref, k_ref, v_ref, c_ref, lse_ref, bias_ref
):
    scale = clips[0]
    xq[...] = (scale * jnp.tanh(inputs[...].astype(F32) / scale)).astype(BF16)
    qkv_into(xq[...], weight, pack, q_ref, k_ref, v_ref)
    attend(lengths, ids[2], q_ref, k_ref, v_ref, c_ref, lse_ref, bias_ref)


def forward_second_body(
    ids, lengths, xq, weight, pack, q_ref, k_ref, v_ref, c_ref, lse_ref, bias_ref
):
    qkv_into(xq[...], weight, pack, q_ref, k_ref, v_ref)
    attend(lengths, ids[2], q_ref, k_ref, v_ref, c_ref, lse_ref, bias_ref)


def backward_heads_body(
    ids,
    lengths,
    which,
    xq,
    q_ref,
    k_ref,
    v_ref,
    c_ref,
    lse_ref,
    merge_q,
    grad_branch,
    chunk,
    d_ref,
    qv_row,
    bias_ref,
    g_ref,
    x_t,
):
    rel = ids[which[0]]
    blocks = chunk.shape[0]
    bias_ref[...] = key_bias(lengths, ids[2])
    x_t[...] = xq[...].T
    g_ref[...] = dot(merge_q[...], grad_branch[...], 1, 1).astype(BF16)
    width = q_ref.shape[0]

    def head(index, carry):
        at = pl.ds(pl.multiple_of(index * HEAD, HEAD), HEAD)
        q, k, v, g = q_ref[at, :], k_ref[at, :], v_ref[at, :], g_ref[at, :]
        scores = dot(k, q, 0, 0) + bias_ref[...]
        prob = jnp.exp(scores - lse_ref[pl.ds(index, 1), :])
        grad_prob = dot(v, g, 0, 0)
        inner = jnp.sum(g.astype(F32) * c_ref[at, :].astype(F32), axis=0, keepdims=True)
        grad_score = (prob * (grad_prob - inner)).astype(BF16)
        d_ref[2, at, :] = dot(g, prob.astype(BF16), 1, 1).astype(BF16)
        d_ref[0, at, :] = (dot(k, grad_score, 1, 0) * 0.125).astype(BF16)
        d_ref[1, at, :] = dot(q, grad_score, 1, 1).astype(BF16)
        return carry

    lax.fori_loop(0, width // HEAD, head, 0)
    rows = x_t.shape[0] // blocks
    base = 3 * rows
    for part in range(3):
        grad = dot(x_t[...], d_ref[part], 1, 1)
        for block in range(blocks):
            piece = grad[block * rows : (block + 1) * rows, :]
            chunk[block ^ rel, part * rows : (part + 1) * rows, :] = piece.astype(BF16)
    ones = jnp.ones((8, xq.shape[0]), BF16)
    qv_row[:, 0:LANES] = dot(ones, d_ref[0], 1, 1)
    qv_row[:, LANES : 2 * LANES] = dot(ones, d_ref[2], 1, 1)
    grad = dot(c_ref[...], grad_branch[...], 1, 0)
    step = width // blocks
    for block in range(blocks):
        piece = grad[block * step : (block + 1) * step, :]
        piece = jnp.concatenate([piece[:, :LANES], piece[:, LANES:]], axis=0)
        chunk[block ^ rel, base : base + 2 * step, :] = piece.astype(BF16)


ERF_P = 0.3275911 * 0.7071067811865476
ERF_A = (0.254829592, -0.284496736, 1.421413741, -1.453152027, 1.061405429)


def gelu_parts(hidden, scale):
    bell = jnp.exp(-0.5 * hidden * hidden)
    t = 1.0 / (1.0 + ERF_P * jnp.abs(hidden))
    poly = ERF_A[4]
    for coefficient in (ERF_A[3], ERF_A[2], ERF_A[1], ERF_A[0]):
        poly = poly * t + coefficient
    tail = 0.5 * poly * t * bell
    area = jnp.where(hidden >= 0.0, 1.0 - tail, tail)
    active = hidden * area
    slope = area + hidden * bell * 0.3989422804014327
    bent = jnp.tanh(active / scale)
    return (scale * bent).astype(BF16), ((1.0 - bent * bent) * slope).astype(BF16), active


def fold(value, op):
    rows, lanes = value.shape
    return op(value.reshape(rows // 8, 8, lanes), axis=0)


def middle_body(
    clips,
    c_own,
    c_other,
    merge_own,
    merge_other,
    inputs,
    up_own,
    up_other,
    down_own,
    down_other,
    pack_own,
    pack_other,
    vectors,
    cotangent,
    unit_out,
    inverse_out,
    normed_q,
    active_own,
    active_other,
    factor_own,
    factor_other,
    output,
    grad_sum,
    grad_feed,
    sums,
    work,
    hidden_ref,
    tops,
    sum_ref,
):
    total = inputs.shape[0]
    work[...] = dot(c_own[...], merge_own[...], 0, 0) + dot(c_other[...], merge_other[...], 0, 0)
    tops[...] = jnp.zeros_like(tops)
    sum_ref[...] = jnp.zeros_like(sum_ref)
    clip_first, clip_second = clips[1], clips[2]

    def first_norm(index, carry):
        at = pl.ds(pl.multiple_of(index * TILE, TILE), TILE)
        rows = inputs[at, :].astype(F32)
        value = rows + work[at, :] + vectors[0:1, :]
        mean = jnp.mean(value, axis=-1, keepdims=True)
        centred = value - mean
        inverse = lax.rsqrt(jnp.mean(centred * centred, axis=-1, keepdims=True) + EPSILON)
        unit = centred * inverse
        normed = unit * vectors[2:3, :] + vectors[4:5, :]
        unit_out[at, :] = unit
        inverse_out[at, :] = jnp.broadcast_to(inverse, (TILE, 128))
        normed_q[at, :] = (clip_first * jnp.tanh(normed / clip_first)).astype(BF16)
        tops[0] = jnp.maximum(tops[0], fold(jnp.abs(rows), jnp.max))
        tops[1] = jnp.maximum(tops[1], fold(jnp.abs(normed), jnp.max))
        work[at, :] = normed
        return carry

    lax.fori_loop(0, total // TILE, first_norm, 0)
    span = hidden_ref.shape[1]
    for weight, pack, active_ref, factor_ref in (
        (up_own, pack_own, active_own, factor_own),
        (up_other, pack_other, active_other, factor_other),
    ):

        def columns(index, carry):
            cols = pl.ds(pl.multiple_of(index * span, span), span)
            hidden_ref[...] = dot(normed_q[...], weight[:, cols], 1, 0)
            bias = pack[0:1, cols]

            def rows(row, carry):
                at = pl.ds(pl.multiple_of(row * TILE, TILE), TILE)
                clipped, factor, active = gelu_parts(hidden_ref[at, :] + bias, clip_second)
                active_ref[at, cols] = clipped
                factor_ref[at, cols] = factor
                tops[2, :, 0:span] = jnp.maximum(tops[2, :, 0:span], fold(jnp.abs(active), jnp.max))
                return carry

            lax.fori_loop(0, total // TILE, rows, 0)
            return carry

        lax.fori_loop(0, weight.shape[1] // span, columns, 0)
    work[...] += dot(active_own[...], down_own[...], 1, 0) + dot(
        active_other[...], down_other[...], 1, 0
    )

    def second_norm(index, carry):
        at = pl.ds(pl.multiple_of(index * TILE, TILE), TILE)
        value = work[at, :] + vectors[1:2, :]
        mean = jnp.mean(value, axis=-1, keepdims=True)
        centred = value - mean
        inverse = lax.rsqrt(jnp.mean(centred * centred, axis=-1, keepdims=True) + EPSILON)
        unit = centred * inverse
        output[at, :] = (unit * vectors[3:4, :] + vectors[5:6, :]).astype(BF16)
        upstream = cotangent[at, :].astype(F32)
        scaled = upstream * vectors[3:4, :]
        grad = inverse * (
            scaled
            - jnp.mean(scaled, axis=-1, keepdims=True)
            - unit * jnp.mean(scaled * unit, axis=-1, keepdims=True)
        )
        grad_sum[at, :] = grad
        grad_feed[at, :] = grad.astype(BF16)
        sum_ref[0] += fold(upstream * unit, jnp.sum)
        sum_ref[1] += fold(upstream, jnp.sum)
        sum_ref[2] += fold(grad, jnp.sum)
        return carry

    lax.fori_loop(0, total // TILE, second_norm, 0)
    for row in range(3):
        sums[row : row + 1, :] = jnp.sum(sum_ref[row], axis=0, keepdims=True)
    for row in range(3):
        top = jnp.max(jnp.max(tops[row], axis=0, keepdims=True), axis=1, keepdims=True)
        sums[3 + row : 4 + row, :] = jnp.broadcast_to(top, (1, sums.shape[1]))
    sums[6:8, :] = jnp.zeros((2, sums.shape[1]), F32)


def down_grad_body(ids, which, active, grad_feed, chunk):
    rel = ids[which[0]]
    blocks = chunk.shape[0]
    rows = active.shape[1] // blocks
    per = blocks // 4

    def tile(index, carry):
        cols = pl.ds(pl.multiple_of(index * per * rows, per * rows), per * rows)
        grad = dot(active[:, cols], grad_feed[...], 0, 0)
        for block in range(per):
            piece = grad[block * rows : (block + 1) * rows, :].astype(BF16)
            to = (index * per + block) ^ rel
            chunk[to, 0:rows, :] = piece[:, :LANES]
            chunk[to, rows : 2 * rows, :] = piece[:, LANES:]
        return carry

    lax.fori_loop(0, 4, tile, 0)


def up_grad_body(
    ids, which, grad_feed, down, up, factor, normed_q, before, chunk, bias_row, grad_normed, g_ref
):
    rel = ids[which[0]]
    blocks = chunk.shape[0]
    span = 512

    def columns(index, carry):
        cols = pl.ds(pl.multiple_of(index * span, span), span)
        grad = dot(grad_feed[...], down[cols, :], 1, 1) * factor[:, cols].astype(F32)
        grad = grad.astype(BF16)
        g_ref[:, cols] = grad
        bias_row[0:1, cols] = jnp.sum(grad.astype(F32), axis=0, keepdims=True)
        return carry

    lax.fori_loop(0, g_ref.shape[1] // span, columns, 0)
    rows = normed_q.shape[1] // blocks
    per = 8

    def tile(index, carry):
        cols = pl.ds(pl.multiple_of(index * per * rows, per * rows), per * rows)
        grad = dot(normed_q[:, cols], g_ref[...], 0, 0)
        for block in range(per):
            to = (index * per + block) ^ rel
            for part in range(grad.shape[1] // LANES):
                piece = grad[block * rows : (block + 1) * rows, part * LANES : (part + 1) * LANES]
                chunk[to, part * rows : (part + 1) * rows, :] = piece.astype(BF16)
        return carry

    lax.fori_loop(0, blocks // per, tile, 0)
    result = dot(g_ref[...], up[...], 1, 1)
    if before is not None:
        result = result + before[...]
    grad_normed[...] = result


def up_grad_first_body(
    ids, which, grad_feed, down, up, factor, normed_q, chunk, bias_row, grad_normed, g_ref
):
    up_grad_body(
        ids, which, grad_feed, down, up, factor, normed_q, None, chunk, bias_row, grad_normed, g_ref
    )


def first_norm_back_body(
    clips,
    grad_normed,
    grad_sum,
    unit_ref,
    inverse_ref,
    vectors,
    sums,
    bias_other,
    bias_own,
    grad_first,
    grad_branch,
    pack_other,
    pack_own,
    sum_ref,
):
    clip_first = clips[1]
    sum_ref[...] = jnp.zeros_like(sum_ref)

    def rows(index, carry):
        at = pl.ds(pl.multiple_of(index * TILE, TILE), TILE)
        unit = unit_ref[at, :]
        bent = jnp.tanh((unit * vectors[2:3, :] + vectors[4:5, :]) / clip_first)
        grad = grad_normed[at, :] * (1.0 - bent * bent) + grad_sum[at, :]
        scaled = grad * vectors[2:3, :]
        back = inverse_ref[at, 0:1] * (
            scaled
            - jnp.mean(scaled, axis=-1, keepdims=True)
            - unit * jnp.mean(scaled * unit, axis=-1, keepdims=True)
        )
        grad_first[at, :] = back
        grad_branch[at, :] = back.astype(BF16)
        sum_ref[0] += fold(grad * unit, jnp.sum)
        sum_ref[1] += fold(grad, jnp.sum)
        sum_ref[2] += fold(back, jnp.sum)
        return carry

    lax.fori_loop(0, unit_ref.shape[0] // TILE, rows, 0)
    width = unit_ref.shape[1]
    for pack, bias in ((pack_other, bias_other), (pack_own, bias_own)):
        pack[...] = jnp.zeros_like(pack)
        for row, source in ((0, 0), (2, 1), (4, 2)):
            pack[row : row + 1, :] = jnp.sum(sum_ref[source], axis=0, keepdims=True)
        pack[1:2, :] = sums[0:1, :]
        pack[3:4, :] = sums[1:2, :]
        pack[5:6, :] = sums[2:3, :]
        pack[6:7, :] = bias[0:1, 0:width]
        pack[7:8, :] = bias[0:1, width : 2 * width]
        pack[12:15, :] = sums[3:6, :]


def input_grad_body(clips, inputs, d_own, d_other, w_own, w_other, grad_first, out):
    total = None
    for d_ref, weight in ((d_own, w_own), (d_other, w_other)):
        for part in range(3):
            term = dot(d_ref[part], weight[part], 0, 1)
            total = term if total is None else total + term
    bent = jnp.tanh(inputs[...].astype(F32) / clips[0])
    out[...] = total * (1.0 - bent * bent) + grad_first[...]


def slope_of(weight, scale):
    bent = jnp.tanh(weight.astype(F32) / scale)
    return 1.0 - bent * bent


def down_final_body(ids, own, other, chunk, weight, out):
    rows = weight.shape[0]
    value = chunk[0].astype(F32)
    slope = slope_of(weight[...], scale_row(own, other, 5, weight.shape[1]))
    out[:, :LANES] = value[:rows] * slope[:, :LANES]
    out[:, LANES:] = value[rows:] * slope[:, LANES:]


def up_final_body(ids, own, other, chunk, weight, out):
    rows = weight.shape[0]
    value = chunk[0].astype(F32)
    slope = slope_of(weight[...], scale_row(own, other, 4, weight.shape[1]))
    for part in range(weight.shape[1] // LANES):
        cols = slice(part * LANES, (part + 1) * LANES)
        out[:, cols] = value[part * rows : (part + 1) * rows] * slope[:, cols]


def rest_final_body(ids, own, other, chunk, project, merge, project_out, merge_out):
    rows = project.shape[1]
    step = merge.shape[1]
    value = chunk[0].astype(F32)
    for part in range(3):
        slope = slope_of(project[part], scale_row(own, other, part, LANES))
        project_out[part] = value[part * rows : (part + 1) * rows] * slope
    slope = slope_of(merge[0], scale_row(own, other, 3, merge.shape[2]))
    base = 3 * rows
    merge_out[0, :, :LANES] = value[base : base + step] * slope[:, :LANES]
    merge_out[0, :, LANES:] = value[base + step : base + 2 * step] * slope[:, LANES:]


class Exchange:
    def __init__(self, size):
        self.bits = size.bit_length() - 1
        assert 1 << self.bits == size
        self.size = size
        order = list(range(self.bits))
        turned = order[:]
        if self.bits > 1:
            turned[0], turned[1] = 1, 0
        self.orders = (order, turned)
        self.halvings = min(self.bits, 4)
        self.blocks = 1 << self.halvings

    def relative(self, position, core):
        total = 0
        for stage in range(self.halvings):
            bit = (position >> self.orders[core][stage]) & 1
            total = total + (bit << (self.halvings - 1 - stage))
        return total

    def swap(self, value, stage, same=False):
        pairs = []
        for index in range(self.size):
            for core in range(2):
                to = index ^ (1 << self.orders[0 if same else core][stage])
                pairs.append((2 * index + core, 2 * to + core))
        return lax.ppermute(value, ("dp", "tensor"), pairs)

    def core_swap(self, value):
        return lax.ppermute(value, "tensor", [(0, 1), (1, 0)])

    def reduce(self, mine, received):
        terms = [mine, received]
        count = self.blocks

        def add(lo, hi):
            total = terms[0][lo:hi].astype(F32)
            for term in terms[1:]:
                total = total + term[lo:hi].astype(F32)
            return total.astype(BF16)

        for stage in range(self.halvings):
            count //= 2
            terms.append(self.swap(add(count, 2 * count), stage))
        value = add(0, 1)
        for stage in range(self.halvings, self.bits):
            value = (value.astype(F32) + self.swap(value, stage).astype(F32)).astype(BF16)
        for stage in reversed(range(self.halvings)):
            value = jnp.concatenate([value, self.swap(value, stage)], axis=0)
        return value


def local(
    inputs,
    row_lengths,
    project_weight,
    merge_weight,
    up_weight,
    down_weight,
    query_value_bias,
    merge_bias,
    up_bias,
    down_bias,
    norm_gains,
    norm_shifts,
    clip_scales,
    cotangent,
):
    exchange = Exchange(lax.axis_size("dp"))
    blocks = exchange.blocks
    member = lax.axis_index("tensor")
    place = lax.axis_index("dp")
    rel0, rel1 = exchange.relative(place, 0), exchange.relative(place, 1)
    own_rel = jnp.where(member == 0, rel0, rel1)
    other_rel = jnp.where(member == 0, rel1, rel0)
    ids = jnp.stack([own_rel, other_rel, member * (LONG // SHORT)]).astype(jnp.int32)
    own_id = jnp.zeros((1,), jnp.int32)
    other_id = jnp.ones((1,), jnp.int32)
    total, width = inputs.shape
    hidden = up_weight.shape[1]
    project = jnp.transpose(project_weight, (1, 0, 2))

    steps = 4
    own_pack = pl.pallas_call(
        peaks_body,
        grid=(steps,),
        in_specs=[
            pl.BlockSpec((3, width // steps, LANES), lambda i: (0, i, 0)),
            pl.BlockSpec((LANES // steps, width), lambda i: (i, 0)),
            pl.BlockSpec((width // steps, hidden), lambda i: (i, 0)),
            pl.BlockSpec((hidden // steps, width), lambda i: (i, 0)),
            pl.BlockSpec((2, LANES), lambda i: (0, 0)),
            pl.BlockSpec((1, hidden), lambda i: (0, 0)),
        ],
        out_specs=pl.BlockSpec((16, hidden), lambda i: (0, 0)),
        out_shape=shaped((16, hidden), F32),
    )(project, merge_weight, up_weight, down_weight, query_value_bias, up_bias[None])
    other_pack = exchange.core_swap(own_pack)
    pack_spec = pl.BlockSpec((16, hidden), lambda i: (0, 0))
    project_block = pl.BlockSpec((3, width // steps, LANES), lambda i: (0, i, 0))
    project_own = pl.pallas_call(
        clip_project_body,
        grid=(steps,),
        in_specs=[pack_spec, pack_spec, project_block],
        out_specs=project_block,
        out_shape=shaped(project.shape, BF16),
    )(own_pack, other_pack, project)
    project_other = exchange.core_swap(project_own)
    rest_blocks = [
        pl.BlockSpec((LANES // steps, width), lambda i: (i, 0)),
        pl.BlockSpec((width // steps, hidden), lambda i: (i, 0)),
        pl.BlockSpec((hidden // steps, width), lambda i: (i, 0)),
    ]
    merge_own, up_own, down_own = pl.pallas_call(
        clip_rest_body,
        grid=(steps,),
        in_specs=[pack_spec, pack_spec] + rest_blocks,
        out_specs=rest_blocks,
        out_shape=[shaped(a.shape, BF16) for a in (merge_weight, up_weight, down_weight)],
    )(own_pack, other_pack, merge_weight, up_weight, down_weight)
    merge_other = exchange.core_swap(merge_own)
    up_other = exchange.core_swap(up_own)
    down_other = exchange.core_swap(down_own)

    head_shape = shaped((LANES, total), BF16)
    heads_out = [head_shape] * 4 + [shaped((8, total), F32)]
    mask_scratch = pltpu.VMEM((LONG, LONG), F32)
    heads_flops = 2 * total * width * 3 * LANES * 4
    xq, *own_heads = call(
        forward_first_body,
        [shaped((total, width), BF16)] + heads_out,
        (ids, row_lengths, clip_scales, inputs, project_own, own_pack),
        heads_flops,
        [mask_scratch],
        in_specs=[SMEM] * 3 + [VMEM] * 3,
        out_specs=[VMEM] * 6,
    )
    other_heads = call(
        forward_second_body,
        heads_out,
        (ids, row_lengths, xq, project_other, other_pack),
        heads_flops,
        [mask_scratch],
        in_specs=[SMEM] * 2 + [VMEM] * 3,
        out_specs=[VMEM] * 5,
    )

    vectors = jnp.concatenate([merge_bias[None], down_bias[None], norm_gains, norm_shifts], axis=0)
    rows_f32 = shaped((total, width), F32)
    rows_bf16 = shaped((total, width), BF16)
    wide = shaped((total, hidden), BF16)
    (
        unit,
        inverse,
        normed_q,
        active_own,
        active_other,
        factor_own,
        factor_other,
        output,
        grad_sum,
        grad_feed,
        sums,
    ) = call(
        middle_body,
        [
            rows_f32,
            shaped((total, 128), F32),
            rows_bf16,
            wide,
            wide,
            wide,
            wide,
            rows_bf16,
            rows_f32,
            rows_bf16,
            shaped((8, width), F32),
        ],
        (
            clip_scales,
            own_heads[3],
            other_heads[3],
            merge_own,
            merge_other,
            inputs,
            up_own,
            up_other,
            down_own,
            down_other,
            own_pack,
            other_pack,
            vectors,
            cotangent,
        ),
        2 * total * width * 4 * hidden * 3,
        [
            pltpu.VMEM((total, width), F32),
            pltpu.VMEM((total, 256), F32),
            pltpu.VMEM((3, 8, width), F32),
            pltpu.VMEM((3, 8, width), F32),
        ],
        in_specs=[SMEM] + [VMEM] * 13,
        out_specs=[VMEM] * 11,
    )

    chunk_shape = shaped((blocks, 2 * hidden // blocks, LANES), BF16)

    def down_half(which, active):
        return call(
            down_grad_body,
            chunk_shape,
            (ids, which, active, grad_feed),
            2 * total * width * hidden,
            in_specs=[SMEM] * 2 + [VMEM] * 2,
            out_specs=VMEM,
        )

    down_got = exchange.core_swap(down_half(other_id, active_other))
    down_rel = exchange.reduce(down_half(own_id, active_own), down_got)

    def up_half(body, which, down, up, factor, *before):
        return call(
            body,
            [chunk_shape, shaped((1, hidden), F32), rows_f32],
            (ids, which, grad_feed, down, up, factor, normed_q) + before,
            2 * total * width * hidden * 3,
            [pltpu.VMEM((total, hidden), BF16)],
            in_specs=[SMEM] * 2 + [VMEM] * (5 + len(before)),
            out_specs=[VMEM] * 3,
        )

    up_theirs, bias_other, partial_normed = up_half(
        up_grad_first_body, other_id, down_other, up_other, factor_other
    )
    up_got = exchange.core_swap(up_theirs)
    up_mine, bias_own, grad_normed = up_half(
        up_grad_body, own_id, down_own, up_own, factor_own, partial_normed
    )
    up_rel = exchange.reduce(up_mine, up_got)

    small = shaped((16, width), F32)
    grad_first, grad_branch, small_theirs, small_mine = call(
        first_norm_back_body,
        [rows_f32, rows_bf16, small, small],
        (clip_scales, grad_normed, grad_sum, unit, inverse, vectors, sums, bias_other, bias_own),
        2 * total * width * 1000,
        [pltpu.VMEM((3, 8, width), F32)],
        in_specs=[SMEM] + [VMEM] * 8,
        out_specs=[VMEM] * 4,
    )

    def heads_half(which, heads, merge_q):
        return call(
            backward_heads_body,
            [
                chunk_shape,
                shaped((3, LANES, total), BF16),
                shaped((8, 2 * LANES), F32),
            ],
            (ids, row_lengths, which, xq) + tuple(heads) + (merge_q, grad_branch),
            heads_flops * 2,
            [
                mask_scratch,
                pltpu.VMEM((LANES, total), BF16),
                pltpu.VMEM((width, total), BF16),
            ],
            in_specs=[SMEM] * 3 + [VMEM] * 8,
            out_specs=[VMEM] * 3,
        )

    rest_theirs, d_other, qv_other = heads_half(other_id, other_heads, merge_other)
    rest_got = exchange.core_swap(rest_theirs)
    rest_mine, d_own, qv_own = heads_half(own_id, own_heads, merge_own)
    rest_rel = exchange.reduce(rest_mine, rest_got)
    input_grad = call(
        input_grad_body,
        rows_f32,
        (clip_scales, inputs, d_own, d_other, project_own, project_other, grad_first),
        2 * total * width * 6 * LANES,
        in_specs=[SMEM] + [VMEM] * 6,
        out_specs=VMEM,
    )

    def joined(sums_part, qv_row):
        return jnp.concatenate([sums_part[:8], qv_row[:1], sums_part[12:15]], axis=0)

    row = lax.broadcasted_iota(jnp.int32, (12, width), 0)

    def merge_small(a, b):
        return jnp.where(row < 9, a + b, jnp.maximum(a, b))

    small_all = joined(small_mine, qv_own)
    small_all = merge_small(small_all, exchange.core_swap(joined(small_theirs, qv_other)))
    for stage in range(exchange.bits):
        small_all = merge_small(small_all, exchange.swap(small_all, stage, same=True))

    def final(body, rel, weights, weight_specs, out_shapes, out_specs):
        spec = pltpu.PrefetchScalarGridSpec(
            num_scalar_prefetch=1,
            grid=(blocks,),
            in_specs=[
                pl.BlockSpec((16, hidden), lambda i, s: (0, 0)),
                pl.BlockSpec((16, hidden), lambda i, s: (0, 0)),
                pl.BlockSpec((1,) + rel.shape[1:], lambda i, s: (i ^ s[0], 0, 0)),
            ]
            + weight_specs,
            out_specs=out_specs,
        )
        return call(
            body,
            out_shapes,
            (ids, own_pack, other_pack, rel) + weights,
            1,
            grid_spec=spec,
        )

    down_spec = pl.BlockSpec((hidden // blocks, width), lambda i, s: (i, 0))
    down_grad = final(
        down_final_body,
        down_rel,
        (down_weight,),
        [down_spec],
        shaped(down_weight.shape, F32),
        down_spec,
    )
    up_spec = pl.BlockSpec((width // blocks, hidden), lambda i, s: (i, 0))
    up_grad = final(
        up_final_body, up_rel, (up_weight,), [up_spec], shaped(up_weight.shape, F32), up_spec
    )
    project_spec = pl.BlockSpec((3, width // blocks, LANES), lambda i, s: (0, i, 0))
    merge_spec = pl.BlockSpec((1, LANES // blocks, width), lambda i, s: (i, 0, 0))
    merge_parts = merge_weight.reshape(blocks, LANES // blocks, width)
    project_grad, merge_grad = final(
        rest_final_body,
        rest_rel,
        (project, merge_parts),
        [project_spec, merge_spec],
        [shaped(project.shape, F32), shaped(merge_parts.shape, F32)],
        [project_spec, merge_spec],
    )
    peaks = small_all[9:12, 0]
    return (
        output,
        input_grad,
        jnp.transpose(project_grad, (1, 0, 2)),
        merge_grad.reshape(merge_weight.shape),
        up_grad,
        down_grad,
        small_all[8].reshape(2, LANES),
        small_all[4],
        small_all[6:8].reshape(hidden),
        small_all[5],
        small_all[0:2],
        small_all[2:4],
        DECAY * clip_scales + (1.0 - DECAY) * peaks,
    )


def solution(mesh):
    return jax.shard_map(
        local,
        mesh=mesh,
        in_specs=(
            P(("dp", "tensor"), None),
            P("dp"),
            P(None, None, "tensor"),
            P("tensor", None),
            P(None, "tensor"),
            P("tensor", None),
            P(None, "tensor"),
            P(),
            P("tensor"),
            P(),
            P(),
            P(),
            P(),
            P(("dp", "tensor"), None),
        ),
        out_specs=(
            P(("dp", "tensor"), None),
            P(("dp", "tensor"), None),
            P(None, None, "tensor"),
            P("tensor", None),
            P(None, "tensor"),
            P("tensor", None),
            P(None, "tensor"),
            P(),
            P("tensor"),
            P(),
            P(),
            P(),
            P(),
        ),
        check_vma=False,
    )
```

```python
from functools import partial

import jax
import jax.numpy as jnp
from jax import lax
from jax.experimental import pallas as pl
from jax.experimental.pallas import tpu as pltpu
from jax.sharding import PartitionSpec as P

HEAD = 64
LONG = 512
SHORT = 128
EPSILON = 1e-12
DECAY = 0.9
F32 = jnp.float32
BF16 = jnp.bfloat16
VMEM = pl.BlockSpec(memory_space=pltpu.VMEM)
SMEM = pl.BlockSpec(memory_space=pltpu.SMEM)
SPANS = ((0, 4), (4, 2))
ORDER = (
    "down.theirs",
    "down.mine",
    "down.add0",
    "up.theirs",
    "up.mine",
    "down.add1",
    "up.add0",
    "norm",
    "heads0",
    "down.add2",
    "heads1",
    "up.add1",
    "down.add3",
    "rest1.add0",
    "rest0.add0",
    "up.add2",
    "down.sum",
    "input",
    "up.add3",
    "down.join3",
    "rest0.add1",
    "rest1.add1",
    "small.theirs",
    "up.sum",
    "rest0.add2",
    "down.join2",
    "rest1.add2",
    "small.mine",
    "up.join3",
    "rest0.add3",
    "down.join1",
    "small.sum0",
    "rest1.add3",
    "rest0.sum",
    "up.join2",
    "rest1.sum",
    "small.sum1",
    "rest0.join3",
    "small.sum2",
    "rest1.join3",
    "rest0.join2",
    "small.sum3",
    "up.join1",
    "rest1.join2",
    "rest0.join1",
    "down.final",
    "rest1.join1",
    "up.final",
    "rest.final",
)
LANES = 384
TILE = 64


def dot(a, b, ca, cb):
    return lax.dot_general(a, b, (((ca,), (cb,)), ((), ())), preferred_element_type=F32)


def shaped(shape, dtype):
    return jax.ShapeDtypeStruct(shape, dtype)


def call(
    body, out_shape, ins, flops, scratch=(), grid_spec=None, in_specs=None, out_specs=None, limit=None
):
    nbytes = sum(a.size * a.dtype.itemsize for a in ins)
    nbytes += sum(o.size * o.dtype.itemsize for o in jax.tree.leaves(out_shape))
    params = dict(
        out_shape=out_shape,
        compiler_params=pltpu.CompilerParams(vmem_limit_bytes=limit or (nbytes + (6 << 20))),
        cost_estimate=pl.CostEstimate(flops=int(flops), bytes_accessed=nbytes, transcendentals=0),
    )
    if grid_spec is not None:
        return pl.pallas_call(body, grid_spec=grid_spec, **params)(*ins)
    return pl.pallas_call(
        body, in_specs=in_specs, out_specs=out_specs, scratch_shapes=list(scratch), **params
    )(*ins)


def peaks_body(project, merge, up, down, qv_bias, up_bias, pack):
    step = pl.program_id(0)

    @pl.when(step == 0)
    def _():
        pack[...] = jnp.zeros_like(pack)
        pack[0:1, :] = up_bias[...]
        pack[1:3, 0:LANES] = qv_bias[...]

    def peak(value):
        top = jnp.max(jnp.abs(value.astype(F32)), axis=0, keepdims=True)
        return jnp.max(top, axis=1, keepdims=True)

    parts = [peak(project[0]), peak(project[1]), peak(project[2])]
    parts += [peak(merge[...]), peak(up[...]), peak(down[...])]
    for row, part in enumerate(parts):
        at = slice(8 + row, 9 + row)
        pack[at, :] = jnp.maximum(pack[at, :], part)


def scale_row(own, other, row, width):
    at = slice(8 + row, 9 + row)
    return 0.5 * jnp.maximum(own[at, 0:width], other[at, 0:width])


def clip_tile(value, scale):
    return (scale * jnp.tanh(value.astype(F32) / scale)).astype(BF16)


def clip_project_body(own, other, project, out):
    for part in range(3):
        scale = scale_row(own, other, part, LANES)
        out[part] = clip_tile(project[part], scale)


def clip_rest_body(own, other, merge, up, down, merge_q, up_q, down_q):
    for row, (src, dst) in enumerate(((merge, merge_q), (up, up_q), (down, down_q))):
        dst[...] = clip_tile(src[...], scale_row(own, other, 3 + row, src.shape[1]))


def key_bias(lengths, first):
    key = lax.broadcasted_iota(jnp.int32, (LONG, 1), 0)
    query = lax.broadcasted_iota(jnp.int32, (1, LONG), 1)
    single = lengths[first] > SHORT
    limit = jnp.full((LONG, 1), lengths[first], jnp.int32)
    for slot in range(1, LONG // SHORT):
        own = jnp.where(single, lengths[first], slot * SHORT + lengths[first + slot])
        limit = jnp.where(key >= slot * SHORT, own, limit)
    key_row = jnp.where(single, 0, key // SHORT)
    query_row = jnp.where(single, 0, query // SHORT)
    key_row = jnp.where(key < limit, key_row, -1)
    return jnp.where(key_row == query_row, 0.0, -1e30).astype(F32)


def qkv_into(xq, weight, bias_pack, q_ref, k_ref, v_ref):
    for part, ref in enumerate((q_ref, k_ref, v_ref)):
        value = dot(xq, weight[part], 1, 0)
        if part == 0:
            value = value + bias_pack[1:2, 0:LANES]
        if part == 2:
            value = value + bias_pack[2:3, 0:LANES]
        value = value.astype(BF16)
        if part == 0:
            value = value * jnp.asarray(0.125, BF16)
        ref[...] = value.T


def attend(lengths, first, q_ref, k_ref, v_ref, c_ref, lse_ref, bias_ref):
    bias_ref[...] = key_bias(lengths, first)

    def head(index, carry):
        at = pl.ds(pl.multiple_of(index * HEAD, HEAD), HEAD)
        scores = dot(k_ref[at, :], q_ref[at, :], 0, 0) + bias_ref[...]
        top = jnp.max(scores, axis=0, keepdims=True)
        prob = jnp.exp(scores - top)
        total = jnp.sum(prob, axis=0, keepdims=True)
        mixed = dot(v_ref[at, :], prob.astype(BF16), 1, 0)
        c_ref[at, :] = (mixed * (1.0 / total)).astype(BF16)
        lse_ref[pl.ds(index, 1), :] = top + jnp.log(total)
        return carry

    lax.fori_loop(0, q_ref.shape[0] // HEAD, head, 0)


def forward_first_body(
    ids, lengths, clips, inputs, weight, pack, xq, q_ref, k_ref, v_ref, c_ref, lse_ref, bias_ref
):
    scale = clips[0]
    xq[...] = (scale * jnp.tanh(inputs[...].astype(F32) / scale)).astype(BF16)
    qkv_into(xq[...], weight, pack, q_ref, k_ref, v_ref)
    attend(lengths, ids[2], q_ref, k_ref, v_ref, c_ref, lse_ref, bias_ref)


def forward_second_body(
    ids, lengths, xq, weight, pack, q_ref, k_ref, v_ref, c_ref, lse_ref, bias_ref
):
    qkv_into(xq[...], weight, pack, q_ref, k_ref, v_ref)
    attend(lengths, ids[2], q_ref, k_ref, v_ref, c_ref, lse_ref, bias_ref)


def backward_heads_body(
    heads,
    which,
    ids,
    lengths,
    xq,
    grad_branch,
    other_half,
    own_half,
    theirs,
    mine,
    d_other,
    d_own,
    qv_other,
    qv_own,
    bias_ref,
    g_ref,
    x_t,
):
    bias_ref[...] = key_bias(lengths, ids[2])
    x_t[...] = xq[...].T
    ones = jnp.ones((8, xq.shape[0]), BF16)
    start, count = heads
    width = count * HEAD
    for half, rel, chunk, d_ref, qv_row in (
        (other_half, ids[which[1]], theirs, d_other, qv_other),
        (own_half, ids[which[0]], mine, d_own, qv_own),
    ):
        q_ref, k_ref, v_ref, c_ref, lse_ref, merge_q = half
        blocks = chunk.shape[0]
        span = slice(start * HEAD, start * HEAD + width)
        g_ref[...] = dot(merge_q[span, :], grad_branch[...], 1, 1).astype(BF16)

        def head(index, carry):
            to = pl.ds(pl.multiple_of(index * HEAD, HEAD), HEAD)
            at = pl.ds(pl.multiple_of((index + start) * HEAD, HEAD), HEAD)
            q, k, v, g = q_ref[at, :], k_ref[at, :], v_ref[at, :], g_ref[to, :]
            scores = dot(k, q, 0, 0) + bias_ref[...]
            prob = jnp.exp(scores - lse_ref[pl.ds(index + start, 1), :])
            grad_prob = dot(v, g, 0, 0)
            inner = jnp.sum(g.astype(F32) * c_ref[at, :].astype(F32), axis=0, keepdims=True)
            grad_score = (prob * (grad_prob - inner)).astype(BF16)
            d_ref[2, to, :] = dot(g, prob.astype(BF16), 1, 1).astype(BF16)
            d_ref[0, to, :] = (dot(k, grad_score, 1, 0) * 0.125).astype(BF16)
            d_ref[1, to, :] = dot(q, grad_score, 1, 1).astype(BF16)
            return carry

        lax.fori_loop(0, count, head, 0)
        rows = x_t.shape[0] // blocks
        for part in range(3):
            grad = dot(x_t[...], d_ref[part], 1, 1)
            for block in range(blocks):
                piece = grad[block * rows : (block + 1) * rows, :]
                chunk[block ^ rel, part * rows : (part + 1) * rows, :] = piece.astype(BF16)
        qv_row[:, 0:width] = dot(ones, d_ref[0], 1, 1)
        qv_row[:, width : 2 * width] = dot(ones, d_ref[2], 1, 1)
        grad = dot(c_ref[span, :], grad_branch[...], 1, 0)
        step = width // blocks
        for block in range(blocks):
            piece = grad[block * step : (block + 1) * step, :]
            pieces = [piece[:, i * width : (i + 1) * width] for i in range(piece.shape[1] // width)]
            piece = jnp.concatenate(pieces, axis=0)
            chunk[block ^ rel, 3 * rows : 3 * rows + piece.shape[0], :] = piece.astype(BF16)


def backward_heads(heads, which, *refs):
    ids, lengths, xq, grad_branch = refs[:4]
    backward_heads_body(heads, which, ids, lengths, xq, grad_branch, refs[4:10], refs[10:16], *refs[16:])


ERF_P = 0.3275911 * 0.7071067811865476
ERF_A = (0.254829592, -0.284496736, 1.421413741, -1.453152027, 1.061405429)


def gelu_parts(hidden, scale):
    bell = jnp.exp(-0.5 * hidden * hidden)
    t = 1.0 / (1.0 + ERF_P * jnp.abs(hidden))
    poly = ERF_A[4]
    for coefficient in (ERF_A[3], ERF_A[2], ERF_A[1], ERF_A[0]):
        poly = poly * t + coefficient
    tail = 0.5 * poly * t * bell
    area = jnp.where(hidden >= 0.0, 1.0 - tail, tail)
    active = hidden * area
    slope = area + hidden * bell * 0.3989422804014327
    bent = jnp.tanh(active / scale)
    return (scale * bent).astype(BF16), ((1.0 - bent * bent) * slope).astype(BF16), active


def fold(value, op):
    rows, lanes = value.shape
    return op(value.reshape(rows // 8, 8, lanes), axis=0)


def middle_body(
    clips,
    c_own,
    c_other,
    merge_own,
    merge_other,
    inputs,
    up_own,
    up_other,
    down_own,
    down_other,
    pack_own,
    pack_other,
    vectors,
    cotangent,
    unit_out,
    inverse_out,
    normed_q,
    active_own,
    active_other,
    factor_own,
    factor_other,
    output,
    grad_sum,
    grad_feed,
    sums,
    work,
    hidden_ref,
    tops,
    sum_ref,
):
    total = inputs.shape[0]
    work[...] = dot(c_own[...], merge_own[...], 0, 0) + dot(c_other[...], merge_other[...], 0, 0)
    tops[...] = jnp.zeros_like(tops)
    sum_ref[...] = jnp.zeros_like(sum_ref)
    clip_first, clip_second = clips[1], clips[2]

    def first_norm(index, carry):
        at = pl.ds(pl.multiple_of(index * TILE, TILE), TILE)
        rows = inputs[at, :].astype(F32)
        value = rows + work[at, :] + vectors[0:1, :]
        mean = jnp.mean(value, axis=-1, keepdims=True)
        centred = value - mean
        inverse = lax.rsqrt(jnp.mean(centred * centred, axis=-1, keepdims=True) + EPSILON)
        unit = centred * inverse
        normed = unit * vectors[2:3, :] + vectors[4:5, :]
        unit_out[at, :] = unit
        inverse_out[at, :] = jnp.broadcast_to(inverse, (TILE, 128))
        normed_q[at, :] = (clip_first * jnp.tanh(normed / clip_first)).astype(BF16)
        tops[0] = jnp.maximum(tops[0], fold(jnp.abs(rows), jnp.max))
        tops[1] = jnp.maximum(tops[1], fold(jnp.abs(normed), jnp.max))
        work[at, :] = normed
        return carry

    lax.fori_loop(0, total // TILE, first_norm, 0)
    span = hidden_ref.shape[1]
    for weight, pack, active_ref, factor_ref in (
        (up_own, pack_own, active_own, factor_own),
        (up_other, pack_other, active_other, factor_other),
    ):

        def columns(index, carry):
            cols = pl.ds(pl.multiple_of(index * span, span), span)
            hidden_ref[...] = dot(normed_q[...], weight[:, cols], 1, 0)
            bias = pack[0:1, cols]

            def rows(row, carry):
                at = pl.ds(pl.multiple_of(row * TILE, TILE), TILE)
                clipped, factor, active = gelu_parts(hidden_ref[at, :] + bias, clip_second)
                active_ref[at, cols] = clipped
                factor_ref[at, cols] = factor
                tops[2, :, 0:span] = jnp.maximum(tops[2, :, 0:span], fold(jnp.abs(active), jnp.max))
                return carry

            lax.fori_loop(0, total // TILE, rows, 0)
            return carry

        lax.fori_loop(0, weight.shape[1] // span, columns, 0)
    work[...] += dot(active_own[...], down_own[...], 1, 0) + dot(
        active_other[...], down_other[...], 1, 0
    )

    def second_norm(index, carry):
        at = pl.ds(pl.multiple_of(index * TILE, TILE), TILE)
        value = work[at, :] + vectors[1:2, :]
        mean = jnp.mean(value, axis=-1, keepdims=True)
        centred = value - mean
        inverse = lax.rsqrt(jnp.mean(centred * centred, axis=-1, keepdims=True) + EPSILON)
        unit = centred * inverse
        output[at, :] = (unit * vectors[3:4, :] + vectors[5:6, :]).astype(BF16)
        upstream = cotangent[at, :].astype(F32)
        scaled = upstream * vectors[3:4, :]
        grad = inverse * (
            scaled
            - jnp.mean(scaled, axis=-1, keepdims=True)
            - unit * jnp.mean(scaled * unit, axis=-1, keepdims=True)
        )
        grad_sum[at, :] = grad
        grad_feed[at, :] = grad.astype(BF16)
        sum_ref[0] += fold(upstream * unit, jnp.sum)
        sum_ref[1] += fold(upstream, jnp.sum)
        sum_ref[2] += fold(grad, jnp.sum)
        return carry

    lax.fori_loop(0, total // TILE, second_norm, 0)
    for row in range(3):
        sums[row : row + 1, :] = jnp.sum(sum_ref[row], axis=0, keepdims=True)
    for row in range(3):
        top = jnp.max(jnp.max(tops[row], axis=0, keepdims=True), axis=1, keepdims=True)
        sums[3 + row : 4 + row, :] = jnp.broadcast_to(top, (1, sums.shape[1]))
    sums[6:8, :] = jnp.zeros((2, sums.shape[1]), F32)


def down_grad_body(which, ids, active, grad_feed, chunk):
    rel = ids[which]
    blocks = chunk.shape[0]
    rows = active.shape[1] // blocks
    per = blocks // 4

    def tile(index, carry):
        cols = pl.ds(pl.multiple_of(index * per * rows, per * rows), per * rows)
        grad = dot(active[:, cols], grad_feed[...], 0, 0)
        for block in range(per):
            piece = grad[block * rows : (block + 1) * rows, :].astype(BF16)
            to = (index * per + block) ^ rel
            chunk[to, 0:rows, :] = piece[:, :LANES]
            chunk[to, rows : 2 * rows, :] = piece[:, LANES:]
        return carry

    lax.fori_loop(0, 4, tile, 0)


def up_grad_body(
    which, ids, grad_feed, down, up, factor, normed_q, before, chunk, bias_row, grad_normed, g_ref
):
    rel = ids[which]
    blocks = chunk.shape[0]
    span = 512

    def columns(index, carry):
        cols = pl.ds(pl.multiple_of(index * span, span), span)
        grad = dot(grad_feed[...], down[cols, :], 1, 1) * factor[:, cols].astype(F32)
        grad = grad.astype(BF16)
        g_ref[:, cols] = grad
        bias_row[0:1, cols] = jnp.sum(grad.astype(F32), axis=0, keepdims=True)
        return carry

    lax.fori_loop(0, g_ref.shape[1] // span, columns, 0)
    rows = normed_q.shape[1] // blocks
    per = 8

    def tile(index, carry):
        cols = pl.ds(pl.multiple_of(index * per * rows, per * rows), per * rows)
        grad = dot(normed_q[:, cols], g_ref[...], 0, 0)
        for block in range(per):
            to = (index * per + block) ^ rel
            for part in range(grad.shape[1] // LANES):
                piece = grad[block * rows : (block + 1) * rows, part * LANES : (part + 1) * LANES]
                chunk[to, part * rows : (part + 1) * rows, :] = piece.astype(BF16)
        return carry

    lax.fori_loop(0, blocks // per, tile, 0)
    result = dot(g_ref[...], up[...], 1, 1)
    if before is not None:
        result = result + before[...]
    grad_normed[...] = result


def up_grad_first_body(
    which, ids, grad_feed, down, up, factor, normed_q, chunk, bias_row, grad_normed, g_ref
):
    up_grad_body(
        which, ids, grad_feed, down, up, factor, normed_q, None, chunk, bias_row, grad_normed, g_ref
    )


def first_norm_back_body(
    clips,
    grad_normed,
    grad_sum,
    unit_ref,
    inverse_ref,
    vectors,
    sums,
    bias_other,
    bias_own,
    grad_first,
    grad_branch,
    pack_other,
    pack_own,
    sum_ref,
):
    clip_first = clips[1]
    sum_ref[...] = jnp.zeros_like(sum_ref)

    def rows(index, carry):
        at = pl.ds(pl.multiple_of(index * TILE, TILE), TILE)
        unit = unit_ref[at, :]
        bent = jnp.tanh((unit * vectors[2:3, :] + vectors[4:5, :]) / clip_first)
        grad = grad_normed[at, :] * (1.0 - bent * bent) + grad_sum[at, :]
        scaled = grad * vectors[2:3, :]
        back = inverse_ref[at, 0:1] * (
            scaled
            - jnp.mean(scaled, axis=-1, keepdims=True)
            - unit * jnp.mean(scaled * unit, axis=-1, keepdims=True)
        )
        grad_first[at, :] = back
        grad_branch[at, :] = back.astype(BF16)
        sum_ref[0] += fold(grad * unit, jnp.sum)
        sum_ref[1] += fold(grad, jnp.sum)
        sum_ref[2] += fold(back, jnp.sum)
        return carry

    lax.fori_loop(0, unit_ref.shape[0] // TILE, rows, 0)
    width = unit_ref.shape[1]
    for pack, bias in ((pack_other, bias_other), (pack_own, bias_own)):
        pack[...] = jnp.zeros_like(pack)
        for row, source in ((0, 0), (2, 1), (4, 2)):
            pack[row : row + 1, :] = jnp.sum(sum_ref[source], axis=0, keepdims=True)
        pack[1:2, :] = sums[0:1, :]
        pack[3:4, :] = sums[1:2, :]
        pack[5:6, :] = sums[2:3, :]
        pack[6:7, :] = bias[0:1, 0:width]
        pack[7:8, :] = bias[0:1, width : 2 * width]
        pack[12:15, :] = sums[3:6, :]


def input_grad_body(spans, clips, inputs, grad_first, w_own, w_other, *refs):
    out = refs[-1]
    total = None
    for (start, count), d_own, d_other in zip(spans, refs[0:-1:2], refs[1:-1:2]):
        span = slice(start * HEAD, (start + count) * HEAD)
        for d_ref, weight in ((d_own, w_own), (d_other, w_other)):
            for part in range(3):
                term = dot(d_ref[part], weight[part, :, span], 0, 1)
                total = term if total is None else total + term
    bent = jnp.tanh(inputs[...].astype(F32) / clips[0])
    out[...] = total * (1.0 - bent * bent) + grad_first[...]


def slope_of(weight, scale):
    bent = jnp.tanh(weight.astype(F32) / scale)
    return 1.0 - bent * bent


def pieces_of(rel, lows, highs, per, body):
    step = pl.program_id(0)
    half = lows[0].shape[0]

    def block(index, carry):
        at = (step * per + index) ^ rel
        low = jnp.minimum(at, half - 1)
        high = jnp.maximum(at - half, 0)
        first = at < half
        values = []
        for lo, hi in zip(lows, highs):
            values.append(jnp.where(first, lo[low].astype(F32), hi[high].astype(F32)))
        body(index, values)
        return carry

    lax.fori_loop(0, per, block, 0)


def down_final_body(per, which, ids, own, other, *refs):
    weight, out = refs[-2:]
    rows = weight.shape[0] // per
    scale = scale_row(own, other, 5, weight.shape[1])

    def block(index, values):
        at = pl.ds(pl.multiple_of(index * rows, 16), rows)
        slope = slope_of(weight[at, :], scale)
        value = jnp.concatenate(values, axis=0)
        out[at, :LANES] = value[:rows] * slope[:, :LANES]
        out[at, LANES:] = value[rows:] * slope[:, LANES:]

    pieces_of(ids[which], refs[0:-2:2], refs[1:-2:2], per, block)


def up_final_body(per, which, ids, own, other, *refs):
    weight, out = refs[-2:]
    rows = weight.shape[0] // per
    scale = scale_row(own, other, 4, weight.shape[1])

    def block(index, values):
        at = pl.ds(pl.multiple_of(index * rows, 16), rows)
        slope = slope_of(weight[at, :], scale)
        value = jnp.concatenate(values, axis=0)
        for part in range(weight.shape[1] // LANES):
            cols = slice(part * LANES, (part + 1) * LANES)
            out[at, cols] = value[part * rows : (part + 1) * rows] * slope[:, cols]

    pieces_of(ids[which], refs[0:-2:2], refs[1:-2:2], per, block)


def rest_final_body(per, spans, which, ids, own, other, *refs):
    groups = len(spans)
    lows, highs = refs[0 : 2 * groups : 2], refs[1 : 2 * groups : 2]
    project = refs[2 * groups]
    merges = refs[2 * groups + 1 : 3 * groups + 1]
    project_out = refs[3 * groups + 1]
    merge_outs = refs[3 * groups + 2 :]
    rows = project.shape[1] // per
    project_scales = [scale_row(own, other, part, LANES) for part in range(3)]
    merge_scale = scale_row(own, other, 3, merges[0].shape[2])

    def block(index, values):
        at = pl.ds(pl.multiple_of(index * rows, 16), rows)
        slopes = [slope_of(project[part, at, :], project_scales[part]) for part in range(3)]
        for (start, count), value, merge, merge_out in zip(spans, values, merges, merge_outs):
            cols = slice(start * HEAD, (start + count) * HEAD)
            for part in range(3):
                piece = value[part * rows : (part + 1) * rows]
                project_out[part, at, cols] = piece * slopes[part][:, cols]
            slope = slope_of(merge[index], merge_scale)
            step, width = merge.shape[1], count * HEAD
            for part in range(merge.shape[2] // width):
                piece = value[3 * rows + part * step : 3 * rows + (part + 1) * step]
                across = slice(part * width, (part + 1) * width)
                merge_out[index, :, across] = piece * slope[:, across]

    pieces_of(ids[which], lows, highs, per, block)


class Exchange:
    def __init__(self, size, first):
        self.bits = size.bit_length() - 1
        assert 1 << self.bits == size and self.bits >= 4
        self.size = size
        self.orders = [list(order) + list(range(4, self.bits)) for order in first]
        self.blocks = 16

    def relative(self, position, core):
        total = 0
        for stage in range(4):
            bit = (position >> self.orders[core][stage]) & 1
            total = total + (bit << (3 - stage))
        return total

    def swap(self, value, stage):
        pairs = []
        for index in range(self.size):
            for core in range(2):
                to = index ^ (1 << self.orders[core][stage])
                pairs.append((2 * index + core, 2 * to + core))
        return lax.ppermute(value, ("dp", "tensor"), pairs)

    def core_swap(self, value):
        return lax.ppermute(value, "tensor", [(0, 1), (1, 0)])


class Task:
    def __init__(self, body, deps):
        self.body, self.deps, self.sends = body, list(deps), []


class Plan:
    def __init__(self):
        self.tasks = {}
        self.values = {}
        self.source = {}

    def given(self, name, value):
        self.values[name] = value
        return name

    def core(self, name, body, deps):
        self.tasks[name] = Task(body, deps)
        return name

    def send(self, name, source, body):
        self.tasks[source].sends.append((name, body))
        self.source[name] = source
        return name

    def run(self):
        values, last = dict(self.values), None

        def take(name):
            nonlocal last
            if name in values:
                return
            if name in self.source:
                take(self.source[name])
                return
            task = self.tasks[name]
            for dep in task.deps:
                take(dep)
            inputs = [values[dep] for dep in task.deps]
            if last is not None:
                inputs, last = lax.optimization_barrier((inputs, last))
            with jax.named_scope(name.replace(".", "_")):
                result = task.body(*inputs)
            values[name] = result
            last = jax.tree.leaves(result)[0]
            for sent, body in task.sends:
                with jax.named_scope(sent.replace(".", "_")):
                    values[sent] = body(result)

        for name in ORDER:
            if name in self.tasks:
                take(name)
        for name in self.tasks:
            take(name)
        return values

    def reduce(self, name, way, mine, theirs, pick_mine, pick_theirs):
        half = way.blocks // 2
        high = self.send(name + ".high", theirs, lambda v: way.core_swap(pick_theirs(v)[half:]))
        low = self.send(name + ".low", theirs, lambda v: way.core_swap(pick_theirs(v)[:half]))

        def total(values):
            out = values[0].astype(F32)
            for value in values[1:]:
                out = out + value.astype(F32)
            return out.astype(BF16)

        def cut(lo, hi):
            def body(mine, *others):
                return total([pick_mine(mine)[lo:hi]] + [other[lo:hi] for other in others])

            return body

        def first(mine, high):
            return total([pick_mine(mine)[half:], high])

        def join(value, other):
            return jnp.concatenate([value, other], axis=0)

        def swap(stage):
            return lambda value: way.swap(value, stage)

        terms, count = [mine, low], half
        value = self.core(f"{name}.add0", first, [mine, high])
        for stage in range(4):
            if stage > 0:
                value = self.core(f"{name}.add{stage}", cut(count, 2 * count), terms)
            terms.append(self.send(f"{name}.in{stage}", value, swap(stage)))
            count //= 2
        value = self.core(f"{name}.sum", cut(0, 1), terms)
        for stage in range(4, way.bits):
            sent = self.send(f"{name}.in{stage}", value, swap(stage))
            value = self.core(f"{name}.sum{stage}", lambda a, b: total([a, b]), [value, sent])
        for stage in reversed(range(4)):
            sent = self.send(f"{name}.out{stage}", value, swap(stage))
            if stage > 0:
                value = self.core(f"{name}.join{stage}", join, [value, sent])
        return [value, sent]


def local(
    inputs,
    row_lengths,
    project_weight,
    merge_weight,
    up_weight,
    down_weight,
    query_value_bias,
    merge_bias,
    up_bias,
    down_bias,
    norm_gains,
    norm_shifts,
    clip_scales,
    cotangent,
):
    size = lax.axis_size("dp")
    exchange = Exchange(size, ((0, 1, 2, 3), (1, 0, 2, 3)))
    same_way = Exchange(size, ((0, 1, 2, 3), (0, 1, 2, 3)))
    blocks = exchange.blocks
    member = lax.axis_index("tensor")
    place = lax.axis_index("dp")
    rel0, rel1 = exchange.relative(place, 0), exchange.relative(place, 1)
    own_rel = jnp.where(member == 0, rel0, rel1)
    other_rel = jnp.where(member == 0, rel1, rel0)
    ids = jnp.stack([own_rel, other_rel, member * (LONG // SHORT)]).astype(jnp.int32)
    total, width = inputs.shape
    hidden = up_weight.shape[1]
    project = jnp.transpose(project_weight, (1, 0, 2))

    steps = 4
    own_pack = pl.pallas_call(
        peaks_body,
        grid=(steps,),
        in_specs=[
            pl.BlockSpec((3, width // steps, LANES), lambda i: (0, i, 0)),
            pl.BlockSpec((LANES // steps, width), lambda i: (i, 0)),
            pl.BlockSpec((width // steps, hidden), lambda i: (i, 0)),
            pl.BlockSpec((hidden // steps, width), lambda i: (i, 0)),
            pl.BlockSpec((2, LANES), lambda i: (0, 0)),
            pl.BlockSpec((1, hidden), lambda i: (0, 0)),
        ],
        out_specs=pl.BlockSpec((16, hidden), lambda i: (0, 0)),
        out_shape=shaped((16, hidden), F32),
        compiler_params=pltpu.CompilerParams(vmem_limit_bytes=16 << 20),
    )(project, merge_weight, up_weight, down_weight, query_value_bias, up_bias[None])
    other_pack = exchange.core_swap(own_pack)
    pack_spec = pl.BlockSpec((16, hidden), lambda i: (0, 0))
    project_block = pl.BlockSpec((3, width // steps, LANES), lambda i: (0, i, 0))
    project_own = pl.pallas_call(
        clip_project_body,
        grid=(steps,),
        in_specs=[pack_spec, pack_spec, project_block],
        out_specs=project_block,
        out_shape=shaped(project.shape, BF16),
        compiler_params=pltpu.CompilerParams(vmem_limit_bytes=16 << 20),
    )(own_pack, other_pack, project)
    project_other = exchange.core_swap(project_own)
    rest_blocks = [
        pl.BlockSpec((LANES // steps, width), lambda i: (i, 0)),
        pl.BlockSpec((width // steps, hidden), lambda i: (i, 0)),
        pl.BlockSpec((hidden // steps, width), lambda i: (i, 0)),
    ]
    merge_own, up_own, down_own = pl.pallas_call(
        clip_rest_body,
        grid=(steps,),
        in_specs=[pack_spec, pack_spec] + rest_blocks,
        out_specs=rest_blocks,
        out_shape=[shaped(a.shape, BF16) for a in (merge_weight, up_weight, down_weight)],
        compiler_params=pltpu.CompilerParams(vmem_limit_bytes=20 << 20),
    )(own_pack, other_pack, merge_weight, up_weight, down_weight)
    merge_other = exchange.core_swap(merge_own)
    up_other = exchange.core_swap(up_own)
    down_other = exchange.core_swap(down_own)

    head_shape = shaped((LANES, total), BF16)
    heads_out = [head_shape] * 4 + [shaped((8, total), F32)]
    mask_scratch = pltpu.VMEM((LONG, LONG), F32)
    heads_flops = 2 * total * width * 3 * LANES * 4
    xq, *own_heads = call(
        forward_first_body,
        [shaped((total, width), BF16)] + heads_out,
        (ids, row_lengths, clip_scales, inputs, project_own, own_pack),
        heads_flops,
        [mask_scratch],
        in_specs=[SMEM] * 3 + [VMEM] * 3,
        out_specs=[VMEM] * 6,
        limit=16 << 20,
    )
    other_heads = call(
        forward_second_body,
        heads_out,
        (ids, row_lengths, xq, project_other, other_pack),
        heads_flops,
        [mask_scratch],
        in_specs=[SMEM] * 2 + [VMEM] * 3,
        out_specs=[VMEM] * 5,
        limit=16 << 20,
    )

    vectors = jnp.concatenate([merge_bias[None], down_bias[None], norm_gains, norm_shifts], axis=0)
    rows_f32 = shaped((total, width), F32)
    rows_bf16 = shaped((total, width), BF16)
    wide = shaped((total, hidden), BF16)
    (
        unit,
        inverse,
        normed_q,
        active_own,
        active_other,
        factor_own,
        factor_other,
        output,
        grad_sum,
        grad_feed,
        sums,
    ) = call(
        middle_body,
        [
            rows_f32,
            shaped((total, 128), F32),
            rows_bf16,
            wide,
            wide,
            wide,
            wide,
            rows_bf16,
            rows_f32,
            rows_bf16,
            shaped((8, width), F32),
        ],
        (
            clip_scales,
            own_heads[3],
            other_heads[3],
            merge_own,
            merge_other,
            inputs,
            up_own,
            up_other,
            down_own,
            down_other,
            own_pack,
            other_pack,
            vectors,
            cotangent,
        ),
        2 * total * width * 4 * hidden * 3,
        [
            pltpu.VMEM((total, width), F32),
            pltpu.VMEM((total, 256), F32),
            pltpu.VMEM((3, 8, width), F32),
            pltpu.VMEM((3, 8, width), F32),
        ],
        in_specs=[SMEM] + [VMEM] * 13,
        out_specs=[VMEM] * 11,
        limit=40 << 20,
    )

    plan = Plan()
    chunk_shape = (blocks, 2 * hidden // blocks, LANES)
    chunk = shaped(chunk_shape, BF16)

    def down_half(which, active, grad):
        return call(
            partial(down_grad_body, which),
            chunk,
            (ids, active, grad),
            2 * total * width * hidden,
            in_specs=[SMEM] + [VMEM] * 2,
            out_specs=VMEM,
        )

    feed = plan.given("feed", grad_feed)
    down_theirs = plan.core(
        "down.theirs",
        lambda grad: down_half(1, active_other, grad),
        [feed],
    )
    down_mine = plan.core(
        "down.mine", lambda grad: down_half(0, active_own, grad), [feed]
    )

    def same(value):
        return value

    def take(index):
        return lambda values: values[index]

    down_out = plan.reduce("down", exchange, down_mine, down_theirs, same, same)

    def up_half(body, which, grad, down, up, factor, *before):
        return call(
            partial(body, which),
            [chunk, shaped((1, hidden), F32), rows_f32],
            (ids, grad, down, up, factor, normed_q) + before,
            2 * total * width * hidden * 3,
            [pltpu.VMEM((total, hidden), BF16)],
            in_specs=[SMEM] + [VMEM] * (5 + len(before)),
            out_specs=[VMEM] * 3,
            limit=22 << 20,
        )

    up_theirs = plan.core(
        "up.theirs",
        lambda grad: up_half(
            up_grad_first_body, 1, grad, down_other, up_other, factor_other
        ),
        [feed],
    )
    up_mine = plan.core(
        "up.mine",
        lambda grad, before: up_half(
            up_grad_body, 0, grad, down_own, up_own, factor_own, before[2]
        ),
        [feed, up_theirs],
    )
    up_out = plan.reduce("up", exchange, up_mine, up_theirs, take(0), take(0))

    small = shaped((16, width), F32)

    def norm_back(theirs, mine):
        ins = (clip_scales, mine[2], grad_sum, unit, inverse, vectors, sums, theirs[1], mine[1])
        return call(
            first_norm_back_body,
            [rows_f32, rows_bf16, small, small],
            ins,
            2 * total * width * 1000,
            [pltpu.VMEM((3, 8, width), F32)],
            in_specs=[SMEM] + [VMEM] * 8,
            out_specs=[VMEM] * 4,
        )

    first_back = plan.core("norm", norm_back, [up_theirs, up_mine])

    spans = SPANS
    groups = []
    for group, (start, count) in enumerate(spans):
        span_width = count * HEAD
        group_shape = (blocks, 3 * width // blocks + LANES * 2 // blocks, span_width)

        def heads_back(back, heads=(start, count), group_shape=group_shape):
            grads = shaped((3, group_shape[2], total), BF16)
            row = shaped((8, 2 * group_shape[2]), F32)
            travel = shaped(group_shape, BF16)
            halves = tuple(other_heads) + (merge_other,) + tuple(own_heads) + (merge_own,)
            return call(
                partial(backward_heads, heads, (0, 1)),
                [travel, travel, grads, grads, row, row],
                (ids, row_lengths, xq, back[1]) + halves,
                heads_flops * 4,
                [
                    mask_scratch,
                    pltpu.VMEM((group_shape[2], total), BF16),
                    pltpu.VMEM((width, total), BF16),
                ],
                in_specs=[SMEM] * 2 + [VMEM] * 14,
                out_specs=[VMEM] * 6,
                limit=24 << 20,
            )

        heads_task = plan.core(f"heads{group}", heads_back, [first_back])
        groups.append(heads_task)
    outs = []
    for group, task in enumerate(groups):
        outs += plan.reduce(f"rest{group}", exchange, task, task, take(1), take(0))

    def input_part(back, *results):
        pairs = []
        for result in results:
            pairs += [result[3], result[2]]
        return call(
            partial(input_grad_body, spans),
            rows_f32,
            (clip_scales, inputs, back[0], project_own, project_other) + tuple(pairs),
            2 * total * width * 6 * LANES,
            in_specs=[SMEM] + [VMEM] * (4 + len(pairs)),
            out_specs=VMEM,
            limit=20 << 20,
        )

    input_task = plan.core("input", input_part, [first_back] + groups)

    def joined(sums_part, rows):
        qv = [row[0:1, : row.shape[1] // 2] for row in rows]
        qv += [row[0:1, row.shape[1] // 2 :] for row in rows]
        return jnp.concatenate(
            [sums_part[:8], jnp.concatenate(qv, axis=1), sums_part[12:15]], axis=0
        )

    small_row = lax.broadcasted_iota(jnp.int32, (12, width), 0)

    def merge_small(a, b):
        return jnp.where(small_row < 9, a + b, jnp.maximum(a, b))

    theirs_small = plan.core(
        "small.theirs",
        lambda back, *results: joined(back[2], [result[4] for result in results]),
        [first_back] + groups,
    )
    small_got = plan.send("small.got", theirs_small, exchange.core_swap)
    small_value = plan.core(
        "small.mine",
        lambda got, back, *results: merge_small(
            joined(back[3], [result[5] for result in results]), got
        ),
        [small_got, first_back] + groups,
    )
    for stage in range(exchange.bits):
        swap = partial(same_way.swap, stage=stage)
        small_in = plan.send(f"small.in{stage}", small_value, swap)
        small_value = plan.core(f"small.sum{stage}", merge_small, [small_value, small_in])

    final_steps = 4
    per = blocks // final_steps

    def final(body, parts, weights, weight_specs, out_shapes, out_specs):
        part_specs = [pl.BlockSpec(part.shape, lambda i, s: (0, 0, 0)) for part in parts]
        spec = pltpu.PrefetchScalarGridSpec(
            num_scalar_prefetch=1,
            grid=(final_steps,),
            in_specs=[pl.BlockSpec((16, hidden), lambda i, s: (0, 0))] * 2
            + part_specs
            + weight_specs,
            out_specs=out_specs,
        )
        ins = (ids, own_pack, other_pack) + tuple(parts) + weights
        return call(body, out_shapes, ins, 1, grid_spec=spec, limit=16 << 20)

    down_spec = pl.BlockSpec((hidden // final_steps, width), lambda i, s: (i, 0))

    def down_final(*parts):
        return final(
            partial(down_final_body, per, 0),
            parts,
            (down_weight,),
            [down_spec],
            shaped(down_weight.shape, F32),
            down_spec,
        )

    up_spec = pl.BlockSpec((width // final_steps, hidden), lambda i, s: (i, 0))

    def up_final(*parts):
        return final(
            partial(up_final_body, per, 0),
            parts,
            (up_weight,),
            [up_spec],
            shaped(up_weight.shape, F32),
            up_spec,
        )

    project_spec = pl.BlockSpec((3, width // final_steps, LANES), lambda i, s: (0, i, 0))
    merges, merge_specs = [], []
    for start, count in spans:
        part = merge_weight[start * HEAD : (start + count) * HEAD]
        merges.append(part.reshape(blocks, count * HEAD // blocks, width))
        merge_specs.append(
            pl.BlockSpec((per, count * HEAD // blocks, width), lambda i, s: (i, 0, 0))
        )

    def rest_final(*parts):
        return final(
            partial(rest_final_body, per, spans, 0),
            parts,
            (project,) + tuple(merges),
            [project_spec] + merge_specs,
            [shaped(project.shape, F32)] + [shaped(part.shape, F32) for part in merges],
            [project_spec] + merge_specs,
        )

    plan.core("down.final", down_final, down_out)
    plan.core("up.final", up_final, up_out)
    plan.core("rest.final", rest_final, outs)
    values = plan.run()
    small_all = values[small_value]
    project_grad, *merge_grads = values["rest.final"]
    merge_grads = [part.reshape(-1, width) for part in merge_grads]
    peaks = small_all[9:12, 0]
    return (
        output,
        values[input_task],
        jnp.transpose(project_grad, (1, 0, 2)),
        jnp.concatenate(merge_grads, axis=0),
        values["up.final"],
        values["down.final"],
        small_all[8].reshape(2, LANES),
        small_all[4],
        small_all[6:8].reshape(hidden),
        small_all[5],
        small_all[0:2],
        small_all[2:4],
        DECAY * clip_scales + (1.0 - DECAY) * peaks,
    )


def solution(mesh):
    return jax.shard_map(
        local,
        mesh=mesh,
        in_specs=(
            P(("dp", "tensor"), None),
            P("dp"),
            P(None, None, "tensor"),
            P("tensor", None),
            P(None, "tensor"),
            P("tensor", None),
            P(None, "tensor"),
            P(),
            P("tensor"),
            P(),
            P(),
            P(),
            P(),
            P(("dp", "tensor"), None),
        ),
        out_specs=(
            P(("dp", "tensor"), None),
            P(("dp", "tensor"), None),
            P(None, None, "tensor"),
            P("tensor", None),
            P(None, "tensor"),
            P("tensor", None),
            P(None, "tensor"),
            P(),
            P("tensor"),
            P(),
            P(),
            P(),
            P(),
        ),
        check_vma=False,
    )
```

```python
from functools import partial

import jax
import jax.numpy as jnp
from jax import lax
from jax.experimental import pallas as pl
from jax.experimental.pallas import tpu as pltpu
from jax.sharding import PartitionSpec as P

HEAD = 64
LONG = 512
SHORT = 128
EPSILON = 1e-12
DECAY = 0.9
F32 = jnp.float32
BF16 = jnp.bfloat16
VMEM = pl.BlockSpec(memory_space=pltpu.VMEM)
SMEM = pl.BlockSpec(memory_space=pltpu.SMEM)
ORDER = (
    "down.theirshigh",
    "down.minehigh",
    "down.add0",
    "down.theirslow",
    "down.minelow",
    "up.theirs",
    "up.mine",
    "down.add1",
    "up.add0",
    "norm",
    "heads.theirs",
    "heads.mine",
    "rest.add0",
    "down.add2",
    "up.add1",
    "small.theirs",
    "input",
    "down.add3",
    "down.sum",
    "up.add2",
    "rest.add1",
    "down.join3",
    "up.add3",
    "rest.add2",
    "small.mine",
    "down.join2",
    "up.sum",
    "rest.add3",
    "small.sum0",
    "down.join1",
    "up.join3",
    "small.sum1",
    "rest.sum",
    "up.join2",
    "rest.join3",
    "small.sum2",
    "down.final",
    "rest.join2",
    "up.join1",
    "small.sum3",
    "rest.join1",
    "up.final",
    "rest.final",
)
COST = 1
LANES = 384
TILE = 64


def dot(a, b, ca, cb):
    return lax.dot_general(a, b, (((ca,), (cb,)), ((), ())), preferred_element_type=F32)


def shaped(shape, dtype):
    return jax.ShapeDtypeStruct(shape, dtype)


def call(
    body, out_shape, ins, scratch=(), in_specs=None, out_specs=None, limit=None
):
    nbytes = sum(a.size * a.dtype.itemsize for a in ins)
    nbytes += sum(o.size * o.dtype.itemsize for o in jax.tree.leaves(out_shape))
    params = dict(
        out_shape=out_shape,
        compiler_params=pltpu.CompilerParams(vmem_limit_bytes=limit or (nbytes + (6 << 20))),
        cost_estimate=pl.CostEstimate(flops=1, bytes_accessed=COST, transcendentals=0),
    )
    return pl.pallas_call(
        body, in_specs=in_specs, out_specs=out_specs, scratch_shapes=list(scratch), **params
    )(*ins)


def peak(value):
    top = jnp.max(jnp.abs(value.astype(F32)), axis=0, keepdims=True)
    return jnp.max(top, axis=1, keepdims=True)


def raise_peaks(pack, tiles):
    for row, tile in enumerate(tiles):
        at = slice(8 + row, 9 + row)
        pack[at, :] = jnp.maximum(pack[at, :], peak(tile))


def project_peaks_body(project, qv_bias, pack):
    @pl.when(pl.program_id(0) == 0)
    def _():
        pack[...] = jnp.zeros_like(pack)
        pack[0:2, :] = qv_bias[...]

    raise_peaks(pack, [project[0], project[1], project[2]])


def rest_peaks_body(merge, up, down, up_bias, pack):
    @pl.when(pl.program_id(0) == 0)
    def _():
        pack[...] = jnp.zeros_like(pack)
        pack[0:1, :] = up_bias[...]

    raise_peaks(pack, [merge[...], up[...], down[...]])


def scale_row(own, other, row, width):
    at = slice(8 + row, 9 + row)
    return 0.5 * jnp.maximum(own[at, 0:width], other[at, 0:width])


def clip_tile(value, scale):
    return (scale * jnp.tanh(value.astype(F32) * (1.0 / scale))).astype(BF16)


def clip_project_body(own, other, project, out):
    for part in range(3):
        out[part] = clip_tile(project[part], scale_row(own, other, part, LANES))


def clip_rest_body(own, other, merge, up, down, merge_q, up_q, down_q):
    for row, (src, dst) in enumerate(((merge, merge_q), (up, up_q), (down, down_q))):
        dst[...] = clip_tile(src[...], scale_row(own, other, row, src.shape[1]))


def key_bias(lengths, first):
    key = lax.broadcasted_iota(jnp.int32, (LONG, 1), 0)
    query = lax.broadcasted_iota(jnp.int32, (1, LONG), 1)
    single = lengths[first] > SHORT
    limit = jnp.full((LONG, 1), lengths[first], jnp.int32)
    for slot in range(1, LONG // SHORT):
        own = jnp.where(single, lengths[first], slot * SHORT + lengths[first + slot])
        limit = jnp.where(key >= slot * SHORT, own, limit)
    key_row = jnp.where(single, 0, key // SHORT)
    query_row = jnp.where(single, 0, query // SHORT)
    key_row = jnp.where(key < limit, key_row, -1)
    return jnp.where(key_row == query_row, 0.0, -1e30).astype(F32)


def qkv_into(xq, weight, bias_pack, q_ref, k_ref, v_ref):
    for part, ref in enumerate((q_ref, k_ref, v_ref)):
        value = dot(xq, weight[part], 1, 0)
        if part == 0:
            value = value + bias_pack[0:1, :]
        if part == 2:
            value = value + bias_pack[1:2, :]
        value = value.astype(BF16)
        if part == 0:
            value = value * jnp.asarray(0.125, BF16)
        ref[...] = value.T


def attend(lengths, first, q_ref, k_ref, v_ref, c_ref, lse_ref, bias_ref):
    bias_ref[...] = key_bias(lengths, first)

    def head(index, carry):
        at = pl.ds(pl.multiple_of(index * HEAD, HEAD), HEAD)
        scores = dot(k_ref[at, :], q_ref[at, :], 0, 0) + bias_ref[...]
        top = jnp.max(scores, axis=0, keepdims=True)
        prob = jnp.exp(scores - top)
        total = jnp.sum(prob, axis=0, keepdims=True)
        mixed = dot(v_ref[at, :], prob.astype(BF16), 1, 0)
        c_ref[at, :] = (mixed * (1.0 / total)).astype(BF16)
        lse_ref[pl.ds(index, 1), :] = top + jnp.log(total)
        return carry

    lax.fori_loop(0, q_ref.shape[0] // HEAD, head, 0)


def forward_first_body(
    ids, lengths, clips, inputs, weight, pack, xq, q_ref, k_ref, v_ref, c_ref, lse_ref, bias_ref
):
    scale = clips[0]
    xq[...] = clip_tile(inputs[...], scale)
    qkv_into(xq[...], weight, pack, q_ref, k_ref, v_ref)
    attend(lengths, ids[2], q_ref, k_ref, v_ref, c_ref, lse_ref, bias_ref)


def forward_second_body(
    ids, lengths, xq, weight, pack, q_ref, k_ref, v_ref, c_ref, lse_ref, bias_ref
):
    qkv_into(xq[...], weight, pack, q_ref, k_ref, v_ref)
    attend(lengths, ids[2], q_ref, k_ref, v_ref, c_ref, lse_ref, bias_ref)


def backward_heads_body(
    which,
    ids,
    lengths,
    xq,
    grad_branch,
    q_ref,
    k_ref,
    v_ref,
    c_ref,
    lse_ref,
    merge_q,
    *refs,
):
    *outs, d_ref, qv_row, bias_ref, g_ref, x_t = refs
    bias_ref[...] = key_bias(lengths, ids[2])
    x_t[...] = xq[...].T
    count, rel = outs[0].shape[0], ids[which]
    width = q_ref.shape[0]
    g_ref[...] = dot(merge_q[...], grad_branch[...], 1, 1).astype(BF16)

    def head(index, carry):
        at = pl.ds(pl.multiple_of(index * HEAD, HEAD), HEAD)
        q, k, v, g = q_ref[at, :], k_ref[at, :], v_ref[at, :], g_ref[at, :]
        scores = dot(k, q, 0, 0) + bias_ref[...]
        prob = jnp.exp(scores - lse_ref[pl.ds(index, 1), :])
        grad_prob = dot(v, g, 0, 0)
        inner = jnp.sum(g.astype(F32) * c_ref[at, :].astype(F32), axis=0, keepdims=True)
        grad_score = (prob * (grad_prob - inner)).astype(BF16)
        d_ref[2, at, :] = dot(g, prob.astype(BF16), 1, 1).astype(BF16)
        d_ref[0, at, :] = (dot(k, grad_score, 1, 0) * 0.125).astype(BF16)
        d_ref[1, at, :] = dot(q, grad_score, 1, 1).astype(BF16)
        return carry

    lax.fori_loop(0, width // HEAD, head, 0)
    rows, step = x_t.shape[0] // (2 * count), width // (2 * count)
    if len(outs) == 2:
        outs = [out.at[:, at * rows : (at + 1) * rows, :] for out in outs for at in range(4)]
    for half, parts in ((1, outs[:4]), (0, outs[4:])):
        base = half_base(rel, half, 2 * count)
        at = pl.ds(pl.multiple_of(base * rows, count * rows), count * rows)
        for part in range(3):
            grad = dot(x_t[at, :], d_ref[part], 1, 1).astype(BF16)
            for block in range(count):
                to = ((base + block) ^ rel) % count
                piece = grad[block * rows : (block + 1) * rows, :]
                parts[part][to] = piece
        at = pl.ds(pl.multiple_of(base * step, count * step), count * step)
        grad = dot(c_ref[at, :], grad_branch[...], 1, 0)
        for block in range(count):
            to = ((base + block) ^ rel) % count
            piece = grad[block * step : (block + 1) * step, :]
            piece = jnp.concatenate([piece[:, :width], piece[:, width:]], axis=0)
            parts[3][to] = piece.astype(BF16)
    ones = jnp.ones((8, xq.shape[0]), BF16)
    qv_row[:, 0:width] = dot(ones, d_ref[0], 1, 1)
    qv_row[:, width : 2 * width] = dot(ones, d_ref[2], 1, 1)


def gelu_parts(hidden, scale):
    area = 0.5 + 0.5 * lax.erf(hidden * 0.7071067811865476)
    bell = jnp.exp(-0.5 * hidden * hidden)
    active = hidden * area
    slope = area + hidden * bell * 0.3989422804014327
    bent = jnp.tanh(active * (1.0 / scale))
    return (scale * bent).astype(BF16), ((1.0 - bent * bent) * slope).astype(BF16), active


def fold(value, op):
    rows, lanes = value.shape
    return op(value.reshape(rows // 8, 8, lanes), axis=0)


def middle_body(
    clips,
    c_own,
    c_other,
    merge_own,
    merge_other,
    inputs,
    up_own,
    up_other,
    down_own,
    down_other,
    pack_own,
    pack_other,
    vectors,
    cotangent,
    unit_out,
    inverse_out,
    normed_q,
    active_own,
    active_other,
    factor_own,
    factor_other,
    output,
    grad_sum,
    grad_feed,
    sums,
    work,
    hidden_ref,
    tops,
    sum_ref,
):
    total = inputs.shape[0]
    work[...] = dot(c_own[...], merge_own[...], 0, 0) + dot(c_other[...], merge_other[...], 0, 0)
    tops[...] = jnp.zeros_like(tops)
    sum_ref[...] = jnp.zeros_like(sum_ref)
    clip_first, clip_second = clips[1], clips[2]

    def first_norm(index, carry):
        at = pl.ds(pl.multiple_of(index * TILE, TILE), TILE)
        rows = inputs[at, :].astype(F32)
        value = rows + work[at, :] + vectors[0:1, :]
        mean = jnp.mean(value, axis=-1, keepdims=True)
        centred = value - mean
        inverse = lax.rsqrt(jnp.mean(centred * centred, axis=-1, keepdims=True) + EPSILON)
        unit = centred * inverse
        normed = unit * vectors[2:3, :] + vectors[4:5, :]
        unit_out[at, :] = unit
        inverse_out[at, :] = jnp.broadcast_to(inverse, (TILE, 128))
        normed_q[at, :] = clip_tile(normed, clip_first)
        tops[0] = jnp.maximum(tops[0], fold(jnp.abs(rows), jnp.max))
        tops[1] = jnp.maximum(tops[1], fold(jnp.abs(normed), jnp.max))
        work[at, :] = normed
        return carry

    lax.fori_loop(0, total // TILE, first_norm, 0)
    span = hidden_ref.shape[1]
    for weight, pack, active_ref, factor_ref in (
        (up_own, pack_own, active_own, factor_own),
        (up_other, pack_other, active_other, factor_other),
    ):

        def columns(index, carry):
            cols = pl.ds(pl.multiple_of(index * span, span), span)
            hidden_ref[...] = dot(normed_q[...], weight[:, cols], 1, 0)
            bias = pack[0:1, cols]

            def rows(row, carry):
                at = pl.ds(pl.multiple_of(row * TILE, TILE), TILE)
                clipped, factor, active = gelu_parts(hidden_ref[at, :] + bias, clip_second)
                active_ref[at, cols] = clipped
                factor_ref[at, cols] = factor
                tops[2, :, 0:span] = jnp.maximum(tops[2, :, 0:span], fold(jnp.abs(active), jnp.max))
                return carry

            lax.fori_loop(0, total // TILE, rows, 0)
            return carry

        lax.fori_loop(0, weight.shape[1] // span, columns, 0)
    work[...] += dot(active_own[...], down_own[...], 1, 0) + dot(
        active_other[...], down_other[...], 1, 0
    )

    def second_norm(index, carry):
        at = pl.ds(pl.multiple_of(index * TILE, TILE), TILE)
        value = work[at, :] + vectors[1:2, :]
        mean = jnp.mean(value, axis=-1, keepdims=True)
        centred = value - mean
        inverse = lax.rsqrt(jnp.mean(centred * centred, axis=-1, keepdims=True) + EPSILON)
        unit = centred * inverse
        output[at, :] = (unit * vectors[3:4, :] + vectors[5:6, :]).astype(BF16)
        upstream = cotangent[at, :].astype(F32)
        scaled = upstream * vectors[3:4, :]
        grad = inverse * (
            scaled
            - jnp.mean(scaled, axis=-1, keepdims=True)
            - unit * jnp.mean(scaled * unit, axis=-1, keepdims=True)
        )
        grad_sum[at, :] = grad
        grad_feed[at, :] = grad.astype(BF16)
        sum_ref[0] += fold(upstream * unit, jnp.sum)
        sum_ref[1] += fold(upstream, jnp.sum)
        sum_ref[2] += fold(grad, jnp.sum)
        return carry

    lax.fori_loop(0, total // TILE, second_norm, 0)
    for row in range(3):
        sums[row : row + 1, :] = jnp.sum(sum_ref[row], axis=0, keepdims=True)
    for row in range(3):
        top = jnp.max(jnp.max(tops[row], axis=0, keepdims=True), axis=1, keepdims=True)
        sums[3 + row : 4 + row, :] = jnp.broadcast_to(top, (1, sums.shape[1]))
    sums[6:8, :] = jnp.zeros((2, sums.shape[1]), F32)


def half_base(rel, half, blocks):
    return (half ^ (rel // (blocks // 2))) * (blocks // 2)


def down_grad_body(which, half, ids, active, grad_feed, chunk):
    rel = ids[which]
    count = chunk.shape[0]
    rows = active.shape[1] // (2 * count)
    base = half_base(rel, half, 2 * count)
    per = count // 2
    for tile in range(2):
        first = base + tile * per
        cols = pl.ds(pl.multiple_of(first * rows, per * rows), per * rows)
        grad = dot(active[:, cols], grad_feed[...], 0, 0)
        for block in range(per):
            piece = grad[block * rows : (block + 1) * rows, :].astype(BF16)
            to = ((first + block) ^ rel) % count
            chunk[to, 0:rows, :] = piece[:, :LANES]
            chunk[to, rows : 2 * rows, :] = piece[:, LANES:]


def up_grad_body(
    which, ids, grad_feed, down, up, factor, normed_q, before, high, low, bias_row, grad_normed, g_ref
):
    rel = ids[which]
    count = high.shape[0]
    span = 512

    def columns(index, carry):
        cols = pl.ds(pl.multiple_of(index * span, span), span)
        grad = dot(grad_feed[...], down[cols, :], 1, 1) * factor[:, cols].astype(F32)
        grad = grad.astype(BF16)
        g_ref[:, cols] = grad
        bias_row[0:1, cols] = jnp.sum(grad.astype(F32), axis=0, keepdims=True)
        return carry

    lax.fori_loop(0, g_ref.shape[1] // span, columns, 0)
    rows = normed_q.shape[1] // (2 * count)
    for half, chunk in ((1, high), (0, low)):
        base = half_base(rel, half, 2 * count)
        cols = pl.ds(pl.multiple_of(base * rows, count * rows), count * rows)
        grad = dot(normed_q[:, cols], g_ref[...], 0, 0)
        for block in range(count):
            to = ((base + block) ^ rel) % count
            for part in range(grad.shape[1] // LANES):
                piece = grad[block * rows : (block + 1) * rows, part * LANES : (part + 1) * LANES]
                chunk[to, part * rows : (part + 1) * rows, :] = piece.astype(BF16)
    result = dot(g_ref[...], up[...], 1, 1)
    if before is not None:
        result = result + before[...]
    grad_normed[...] = result


def up_grad_first_body(which, ids, grad_feed, down, up, factor, normed_q, *outs):
    up_grad_body(which, ids, grad_feed, down, up, factor, normed_q, None, *outs)


def first_norm_back_body(
    clips,
    grad_normed,
    grad_sum,
    unit_ref,
    inverse_ref,
    vectors,
    sums,
    bias_other,
    bias_own,
    grad_first,
    grad_branch,
    pack_other,
    pack_own,
    sum_ref,
):
    clip_first = clips[1]
    sum_ref[...] = jnp.zeros_like(sum_ref)

    def rows(index, carry):
        at = pl.ds(pl.multiple_of(index * TILE, TILE), TILE)
        unit = unit_ref[at, :]
        bent = jnp.tanh((unit * vectors[2:3, :] + vectors[4:5, :]) * (1.0 / clip_first))
        grad = grad_normed[at, :] * (1.0 - bent * bent) + grad_sum[at, :]
        scaled = grad * vectors[2:3, :]
        back = inverse_ref[at, 0:1] * (
            scaled
            - jnp.mean(scaled, axis=-1, keepdims=True)
            - unit * jnp.mean(scaled * unit, axis=-1, keepdims=True)
        )
        grad_first[at, :] = back
        grad_branch[at, :] = back.astype(BF16)
        sum_ref[0] += fold(grad * unit, jnp.sum)
        sum_ref[1] += fold(grad, jnp.sum)
        sum_ref[2] += fold(back, jnp.sum)
        return carry

    lax.fori_loop(0, unit_ref.shape[0] // TILE, rows, 0)
    width = unit_ref.shape[1]
    for pack, bias in ((pack_other, bias_other), (pack_own, bias_own)):
        pack[...] = jnp.zeros_like(pack)
        for row, source in ((0, 0), (2, 1), (4, 2)):
            pack[row : row + 1, :] = jnp.sum(sum_ref[source], axis=0, keepdims=True)
        pack[1:2, :] = sums[0:1, :]
        pack[3:4, :] = sums[1:2, :]
        pack[5:6, :] = sums[2:3, :]
        pack[6:7, :] = bias[0:1, 0:width]
        pack[7:8, :] = bias[0:1, width : 2 * width]
        pack[12:15, :] = sums[3:6, :]


def input_grad_body(clips, inputs, grad_first, w_own, w_other, d_own, d_other, out):
    terms = []
    for d_ref, weight in ((d_own, w_own), (d_other, w_other)):
        for part in range(3):
            terms.append(dot(d_ref[part], weight[part], 0, 1))
    bent = jnp.tanh(inputs[...].astype(F32) * (1.0 / clips[0]))
    out[...] = sum(terms[1:], terms[0]) * (1.0 - bent * bent) + grad_first[...]


def slope_of(weight, scale):
    bent = jnp.tanh(weight.astype(F32) * (1.0 / scale))
    return 1.0 - bent * bent


def block_value(rel, low, high, at):
    half = low.shape[0]
    at = at ^ rel
    first = low[jnp.minimum(at, half - 1)].astype(F32)
    return jnp.where(at < half, first, high[jnp.maximum(at - half, 0)].astype(F32))


def down_final_body(per, ids, own, other, low, high, weight, out):
    rows = weight.shape[0] // per
    slope = slope_of(weight[...], scale_row(own, other, 2, weight.shape[1]))
    for index in range(per):
        value = block_value(ids[0], low, high, pl.program_id(0) * per + index)
        at = slice(index * rows, (index + 1) * rows)
        out[at, :LANES] = value[:rows] * slope[at, :LANES]
        out[at, LANES:] = value[rows:] * slope[at, LANES:]


def up_final_body(per, ids, own, other, low, high, weight, out):
    rows = weight.shape[0] // per
    slope = slope_of(weight[...], scale_row(own, other, 1, weight.shape[1]))
    for index in range(per):
        value = block_value(ids[0], low, high, pl.program_id(0) * per + index)
        at = slice(index * rows, (index + 1) * rows)
        for part in range(weight.shape[1] // LANES):
            cols = slice(part * LANES, (part + 1) * LANES)
            out[at, cols] = value[part * rows : (part + 1) * rows] * slope[at, cols]


def rest_final_body(
    per, ids, own, other, low, high, p_own, p_other, project, merge, project_out, merge_out
):
    rows = project.shape[1] // per
    slopes = []
    for part in range(3):
        slopes.append(slope_of(project[part], scale_row(p_own, p_other, part, LANES)))
    scale = scale_row(own, other, 0, merge.shape[1])
    values = []
    for index in range(per):
        value = block_value(ids[0], low, high, pl.program_id(0) * per + index)
        values.append(value[3 * rows :])
        at = slice(index * rows, (index + 1) * rows)
        for part in range(3):
            project_out[part, at, :] = value[part * rows : (part + 1) * rows] * slopes[part][at]
    step = merge.shape[0] // per
    slope = slope_of(merge[...], scale)
    for part in range(2):
        across = slice(part * LANES, (part + 1) * LANES)
        piece = jnp.concatenate([v[part * step : (part + 1) * step] for v in values], axis=0)
        merge_out[:, across] = piece * slope[:, across]


class Exchange:
    def __init__(self, size, first):
        self.bits = size.bit_length() - 1
        assert 1 << self.bits == size and self.bits >= 4
        self.size = size
        self.orders = [list(order) + list(range(4, self.bits)) for order in first]
        self.blocks = 16

    def relative(self, position, core):
        total = 0
        for stage in range(4):
            bit = (position >> self.orders[core][stage]) & 1
            total = total + (bit << (3 - stage))
        return total

    def swap(self, value, stage):
        pairs = []
        for index in range(self.size):
            for core in range(2):
                to = index ^ (1 << self.orders[core][stage])
                pairs.append((2 * index + core, 2 * to + core))
        return lax.ppermute(value, ("dp", "tensor"), pairs)

    def core_swap(self, value):
        return lax.ppermute(value, "tensor", [(0, 1), (1, 0)])


class Task:
    def __init__(self, body, deps):
        self.body, self.deps, self.sends = body, list(deps), []


class Plan:
    def __init__(self):
        self.tasks = {}
        self.values = {}
        self.source = {}

    def given(self, name, value):
        self.values[name] = value
        return name

    def core(self, name, body, deps):
        self.tasks[name] = Task(body, deps)
        return name

    def send(self, name, source, body):
        self.tasks[source].sends.append((name, body))
        self.source[name] = source
        return name

    def run(self):
        values, last = dict(self.values), None

        def take(name):
            nonlocal last
            if name in values:
                return
            if name in self.source:
                take(self.source[name])
                return
            task = self.tasks[name]
            for dep in task.deps:
                take(dep)
            inputs = [values[dep] for dep in task.deps]
            if last is not None:
                inputs, last = lax.optimization_barrier((inputs, last))
            with jax.named_scope(name.replace(".", "_")):
                result = task.body(*inputs)
            values[name] = result
            last = jax.tree.leaves(result)[0]
            for sent, body in task.sends:
                with jax.named_scope(sent.replace(".", "_")):
                    values[sent] = body(result)

        for name in ORDER:
            if name in self.tasks:
                take(name)
        for name in self.tasks:
            take(name)
        return values

    def swap(self, name, source, way, stage, pick=lambda value: value):
        return self.send(name, source, lambda value: way.swap(pick(value), stage))

    def reduce(self, name, way, mine, theirs, pick):
        def swapped(index):
            return lambda v: [way.core_swap(value) for value in pick(v, index)]

        def whole(values):
            return values[0] if len(values) == 1 else jnp.concatenate(values, axis=1)

        high = self.send(name + ".high", theirs[0], swapped(0))
        low = self.send(name + ".low", theirs[1], swapped(1))
        value = self.core(
            f"{name}.add0",
            lambda mine, high: total([whole(pick(mine, 0)), whole(high)]),
            [mine[0], high],
        )
        got = self.swap(f"{name}.in0", value, way, 0)

        def second(mine, low, got):
            return split_in_two([whole(pick(mine, 1)), whole(low), got])

        def more(kept, got):
            return split_in_two([kept[0], got])

        value = self.core(f"{name}.add1", second, [mine[1], low, got])
        for stage in (1, 2, 3):
            got = self.swap(f"{name}.in{stage}", value, way, stage, second_of)
            if stage < 3:
                value = self.core(f"{name}.add{stage + 1}", more, [value, got])
        value = self.core(f"{name}.sum", lambda kept, got: total([kept[0], got]), [value, got])
        for stage in range(4, way.bits):
            sent = self.swap(f"{name}.in{stage}", value, way, stage)
            value = self.core(f"{name}.sum{stage}", lambda a, b: total([a, b]), [value, sent])
        for stage in reversed(range(4)):
            sent = self.swap(f"{name}.out{stage}", value, way, stage)
            if stage > 0:
                value = self.core(
                    f"{name}.join{stage}",
                    lambda a, b: jnp.concatenate([a, b], axis=0),
                    [value, sent],
                )
        return [value, sent]


def total(values):
    out = values[0].astype(F32)
    for value in values[1:]:
        out = out + value.astype(F32)
    return out.astype(BF16)


def split_in_two(values):
    half = values[0].shape[0] // 2
    return total([value[:half] for value in values]), total([value[half:] for value in values])


def second_of(value):
    return value[1]


def local(
    inputs,
    row_lengths,
    project_weight,
    merge_weight,
    up_weight,
    down_weight,
    query_value_bias,
    merge_bias,
    up_bias,
    down_bias,
    norm_gains,
    norm_shifts,
    clip_scales,
    cotangent,
):
    size = lax.axis_size("dp")
    exchange = Exchange(size, ((0, 1, 2, 3), (1, 0, 2, 3)))
    same_way = Exchange(size, ((0, 1, 2, 3), (0, 1, 2, 3)))
    blocks = exchange.blocks
    member = lax.axis_index("tensor")
    place = lax.axis_index("dp")
    rel0, rel1 = exchange.relative(place, 0), exchange.relative(place, 1)
    own_rel = jnp.where(member == 0, rel0, rel1)
    other_rel = jnp.where(member == 0, rel1, rel0)
    ids = jnp.stack([own_rel, other_rel, member * (LONG // SHORT)]).astype(jnp.int32)
    total, width = inputs.shape
    hidden = up_weight.shape[1]
    project = jnp.transpose(project_weight, (1, 0, 2))

    steps = 4
    small_grid = pltpu.CompilerParams(vmem_limit_bytes=12 << 20)
    project_block = pl.BlockSpec((3, width // steps, LANES), lambda i: (0, i, 0))
    rest_blocks = [
        pl.BlockSpec((LANES // steps, width), lambda i: (i, 0)),
        pl.BlockSpec((width // steps, hidden), lambda i: (i, 0)),
        pl.BlockSpec((hidden // steps, width), lambda i: (i, 0)),
    ]
    project_pack_spec = pl.BlockSpec((16, LANES), lambda i: (0, 0))
    pack_spec = pl.BlockSpec((16, hidden), lambda i: (0, 0))
    rest_weights = (merge_weight, up_weight, down_weight)

    def project_peaks():
        return pl.pallas_call(
            project_peaks_body,
            grid=(steps,),
            in_specs=[project_block, pl.BlockSpec((2, LANES), lambda i: (0, 0))],
            out_specs=project_pack_spec,
            out_shape=shaped((16, LANES), F32),
            compiler_params=small_grid,
        )(project, query_value_bias)

    def rest_peaks(weights):
        return pl.pallas_call(
            rest_peaks_body,
            grid=(steps,),
            in_specs=rest_blocks + [pl.BlockSpec((1, hidden), lambda i: (0, 0))],
            out_specs=pack_spec,
            out_shape=shaped((16, hidden), F32),
            compiler_params=small_grid,
        )(*weights, up_bias[None])

    def clip_project(own, other):
        return pl.pallas_call(
            clip_project_body,
            grid=(steps,),
            in_specs=[project_pack_spec, project_pack_spec, project_block],
            out_specs=project_block,
            out_shape=shaped(project.shape, BF16),
            compiler_params=small_grid,
        )(own, other, project)

    def clip_rest(own, other):
        return pl.pallas_call(
            clip_rest_body,
            grid=(steps,),
            in_specs=[pack_spec, pack_spec] + rest_blocks,
            out_specs=rest_blocks,
            out_shape=[shaped(a.shape, BF16) for a in rest_weights],
            compiler_params=small_grid,
        )(own, other, *rest_weights)

    project_own_pack = project_peaks()
    project_other_pack = exchange.core_swap(project_own_pack)
    project_own = clip_project(project_own_pack, project_other_pack)
    project_other = exchange.core_swap(project_own)
    tied, project_own = lax.optimization_barrier((rest_weights, project_own))
    own_pack = rest_peaks(tied)
    other_pack = exchange.core_swap(own_pack)
    other_pack, project_other = lax.optimization_barrier((other_pack, project_other))
    merge_own, up_own, down_own = clip_rest(own_pack, other_pack)
    merge_other = exchange.core_swap(merge_own)
    up_other = exchange.core_swap(up_own)
    down_other = exchange.core_swap(down_own)
    project_own, merge_own = lax.optimization_barrier((project_own, merge_own))

    head_shape = shaped((LANES, total), BF16)
    heads_out = [head_shape] * 4 + [shaped((8, total), F32)]
    mask_scratch = pltpu.VMEM((LONG, LONG), F32)
    xq, *own_heads = call(
        forward_first_body,
        [shaped((total, width), BF16)] + heads_out,
        (ids, row_lengths, clip_scales, inputs, project_own, project_own_pack),
        [mask_scratch],
        in_specs=[SMEM] * 3 + [VMEM] * 3,
        out_specs=[VMEM] * 6,
        limit=16 << 20,
    )
    other_heads = call(
        forward_second_body,
        heads_out,
        (ids, row_lengths, xq, project_other, project_other_pack),
        [mask_scratch],
        in_specs=[SMEM] * 2 + [VMEM] * 3,
        out_specs=[VMEM] * 5,
        limit=16 << 20,
    )

    vectors = jnp.concatenate([merge_bias[None], down_bias[None], norm_gains, norm_shifts], axis=0)
    rows_f32 = shaped((total, width), F32)
    rows_bf16 = shaped((total, width), BF16)
    wide = shaped((total, hidden), BF16)
    (
        unit,
        inverse,
        normed_q,
        active_own,
        active_other,
        factor_own,
        factor_other,
        output,
        grad_sum,
        grad_feed,
        sums,
    ) = call(
        middle_body,
        [
            rows_f32,
            shaped((total, 128), F32),
            rows_bf16,
            wide,
            wide,
            wide,
            wide,
            rows_bf16,
            rows_f32,
            rows_bf16,
            shaped((8, width), F32),
        ],
        (
            clip_scales,
            own_heads[3],
            other_heads[3],
            merge_own,
            merge_other,
            inputs,
            up_own,
            up_other,
            down_own,
            down_other,
            own_pack,
            other_pack,
            vectors,
            cotangent,
        ),
        [
            pltpu.VMEM((total, width), F32),
            pltpu.VMEM((total, 256), F32),
            pltpu.VMEM((3, 8, width), F32),
            pltpu.VMEM((3, 8, width), F32),
        ],
        in_specs=[SMEM] + [VMEM] * 13,
        out_specs=[VMEM] * 11,
        limit=32 << 20,
    )

    plan = Plan()
    chunk = shaped((blocks // 2, 2 * hidden // blocks, LANES), BF16)

    def down_half(which, half, active, grad):
        return call(
            partial(down_grad_body, which, half),
            chunk,
            (ids, active, grad),
            in_specs=[SMEM] + [VMEM] * 2,
            out_specs=VMEM,
            limit=9 << 20,
        )

    feed = plan.given("feed", grad_feed)
    down_tasks = {}
    for half, word in ((1, "high"), (0, "low")):
        for which, active in ((1, active_other), (0, active_own)):
            down_tasks[which, half] = plan.core(
                ("down.mine", "down.theirs")[which] + word,
                lambda grad, which=which, half=half, active=active: down_half(
                    which, half, active, grad
                ),
                [feed],
            )

    def take(index):
        return lambda values: values[index]

    def part(values, index):
        return values[index]

    def one(values, index):
        return [values[index]]

    down_out = plan.reduce(
        "down",
        exchange,
        (down_tasks[0, 1], down_tasks[0, 0]),
        (down_tasks[1, 1], down_tasks[1, 0]),
        lambda value, index: [value],
    )

    def up_half(body, which, grad, down, up, factor, *before):
        return call(
            partial(body, which),
            [chunk, chunk, shaped((1, hidden), F32), rows_f32],
            (ids, grad, down, up, factor, normed_q) + before,
            [pltpu.VMEM((total, hidden), BF16)],
            in_specs=[SMEM] + [VMEM] * (5 + len(before)),
            out_specs=[VMEM] * 4,
            limit=20 << 20,
        )

    up_theirs = plan.core(
        "up.theirs",
        lambda grad: up_half(
            up_grad_first_body, 1, grad, down_other, up_other, factor_other
        ),
        [feed],
    )
    up_mine = plan.core(
        "up.mine",
        lambda grad, before: up_half(
            up_grad_body, 0, grad, down_own, up_own, factor_own, before[3]
        ),
        [feed, up_theirs],
    )
    up_out = plan.reduce("up", exchange, (up_mine, up_mine), (up_theirs, up_theirs), one)

    small = shaped((16, width), F32)

    def norm_back(theirs, mine):
        ins = (clip_scales, mine[3], grad_sum, unit, inverse, vectors, sums, theirs[2], mine[2])
        return call(
            first_norm_back_body,
            [rows_f32, rows_bf16, small, small],
            ins,
            [pltpu.VMEM((3, 8, width), F32)],
            in_specs=[SMEM] + [VMEM] * 8,
            out_specs=[VMEM] * 4,
        )

    first_back = plan.core("norm", norm_back, [up_theirs, up_mine])

    def heads_back(which, back, heads, merge_q):
        count = (1, 4)[which]
        parts = [shaped((chunk.shape[0], chunk.shape[1] // count, LANES), BF16)] * count
        *outs, grads, row = call(
            partial(backward_heads_body, which),
            parts + parts + [shaped((3, LANES, total), BF16), shaped((8, 2 * LANES), F32)],
            (ids, row_lengths, xq, back[1]) + tuple(heads) + (merge_q,),
            [
                mask_scratch,
                pltpu.VMEM((LANES, total), BF16),
                pltpu.VMEM((width, total), BF16),
            ],
            in_specs=[SMEM] * 2 + [VMEM] * 8,
            out_specs=[VMEM] * (2 * count + 2),
            limit=18 << 20,
        )
        return outs[:count], outs[count:], grads, row

    heads_theirs = plan.core(
        "heads.theirs", lambda back: heads_back(1, back, other_heads, merge_other), [first_back]
    )
    heads_mine = plan.core(
        "heads.mine", lambda back: heads_back(0, back, own_heads, merge_own), [first_back]
    )
    rest_out = plan.reduce(
        "rest", exchange, (heads_mine, heads_mine), (heads_theirs, heads_theirs), part
    )

    def input_part(back, theirs, mine):
        return call(
            input_grad_body,
            rows_f32,
            (clip_scales, inputs, back[0], project_own, project_other, mine[2], theirs[2]),
            in_specs=[SMEM] + [VMEM] * 6,
            out_specs=VMEM,
            limit=16 << 20,
        )

    input_task = plan.core("input", input_part, [first_back, heads_theirs, heads_mine])

    def joined(sums_part, row):
        return jnp.concatenate([sums_part[:8], row[0:1], sums_part[12:15]], axis=0)

    small_row = lax.broadcasted_iota(jnp.int32, (12, width), 0)

    def merge_small(a, b):
        return jnp.where(small_row < 9, a + b, jnp.maximum(a, b))

    theirs_small = plan.core(
        "small.theirs", lambda back, heads: joined(back[2], heads[3]), [first_back, heads_theirs]
    )
    small_got = plan.send("small.got", theirs_small, exchange.core_swap)
    small_value = plan.core(
        "small.mine",
        lambda got, back, heads: merge_small(joined(back[3], heads[3]), got),
        [small_got, first_back, heads_mine],
    )
    for stage in range(exchange.bits):
        swap = partial(same_way.swap, stage=stage)
        small_in = plan.send(f"small.in{stage}", small_value, swap)
        small_value = plan.core(f"small.sum{stage}", merge_small, [small_value, small_in])

    final_steps = 4
    per = blocks // final_steps

    def final(body, parts, weights, specs, packs=()):
        part_specs = [pl.BlockSpec(part.shape, lambda i, s: (0, 0, 0)) for part in parts]
        pack = pl.BlockSpec((16, hidden), lambda i, s: (0, 0))
        ins = (ids, own_pack, other_pack) + tuple(parts) + tuple(packs) + weights
        return pl.pallas_call(
            partial(body, per),
            grid_spec=pltpu.PrefetchScalarGridSpec(
                num_scalar_prefetch=1,
                grid=(final_steps,),
                in_specs=[pack, pack]
                + part_specs
                + [pl.BlockSpec((16, LANES), lambda i, s: (0, 0))] * len(packs)
                + specs,
                out_specs=specs,
            ),
            out_shape=[shaped(weight.shape, F32) for weight in weights],
            compiler_params=pltpu.CompilerParams(vmem_limit_bytes=10 << 20),
            cost_estimate=pl.CostEstimate(flops=1, bytes_accessed=1, transcendentals=0),
        )(*ins)

    down_spec = pl.BlockSpec((hidden // final_steps, width), lambda i, s: (i, 0))
    plan.core(
        "down.final",
        lambda *parts: final(down_final_body, parts, (down_weight,), [down_spec])[0],
        down_out,
    )
    up_spec = pl.BlockSpec((width // final_steps, hidden), lambda i, s: (i, 0))
    plan.core(
        "up.final",
        lambda *parts: final(up_final_body, parts, (up_weight,), [up_spec])[0],
        up_out,
    )
    project_spec = pl.BlockSpec((3, width // final_steps, LANES), lambda i, s: (0, i, 0))
    merge_spec = pl.BlockSpec((LANES // final_steps, width), lambda i, s: (i, 0))
    plan.core(
        "rest.final",
        lambda *parts: final(
            rest_final_body,
            parts,
            (project, merge_weight),
            [project_spec, merge_spec],
            (project_own_pack, project_other_pack),
        ),
        rest_out,
    )
    values = plan.run()
    small_all = values[small_value]
    project_grad, merge_grad = values["rest.final"]
    peaks = small_all[9:12, 0]
    return (
        output,
        values[input_task],
        jnp.transpose(project_grad, (1, 0, 2)),
        merge_grad,
        values["up.final"],
        values["down.final"],
        small_all[8].reshape(2, LANES),
        small_all[4],
        small_all[6:8].reshape(hidden),
        small_all[5],
        small_all[0:2],
        small_all[2:4],
        DECAY * clip_scales + (1.0 - DECAY) * peaks,
    )


def solution(mesh):
    return jax.shard_map(
        local,
        mesh=mesh,
        in_specs=(
            P(("dp", "tensor"), None),
            P("dp"),
            P(None, None, "tensor"),
            P("tensor", None),
            P(None, "tensor"),
            P("tensor", None),
            P(None, "tensor"),
            P(),
            P("tensor"),
            P(),
            P(),
            P(),
            P(),
            P(("dp", "tensor"), None),
        ),
        out_specs=(
            P(("dp", "tensor"), None),
            P(("dp", "tensor"), None),
            P(None, None, "tensor"),
            P("tensor", None),
            P(None, "tensor"),
            P("tensor", None),
            P(None, "tensor"),
            P(),
            P("tensor"),
            P(),
            P(),
            P(),
            P(),
        ),
        check_vma=False,
    )
```

```python
from functools import partial

import jax
import jax.numpy as jnp
from jax import lax
from jax.experimental import pallas as pl
from jax.experimental.pallas import tpu as pltpu
from jax.sharding import PartitionSpec as P

HEAD = 64
LONG = 512
SHORT = 128
EPSILON = 1e-12
DECAY = 0.9
F32 = jnp.float32
BF16 = jnp.bfloat16
VMEM = pl.BlockSpec(memory_space=pltpu.VMEM)
SMEM = pl.BlockSpec(memory_space=pltpu.SMEM)
ORDER = (
    "down.theirshigh",
    "down.minehigh",
    "down.add0",
    "down.theirslow",
    "down.minelow",
    "up.theirs",
    "up.mine",
    "down.add1",
    "up.add0",
    "norm",
    "heads.theirs",
    "heads.mine",
    "down.add2",
    "up.add1",
    "rest.add0",
    "input",
    "down.add3",
    "small.theirs",
    "down.sum",
    "up.add2",
    "rest.add1",
    "small.mine",
    "down.join3",
    "up.add3",
    "rest.add2",
    "down.join2",
    "up.sum",
    "rest.add3",
    "small.sum0",
    "down.join1",
    "up.join3",
    "small.sum1",
    "rest.sum",
    "small.sum2",
    "up.join2",
    "rest.join3",
    "down.final",
    "rest.join2",
    "up.join1",
    "small.sum3",
    "rest.join1",
    "rest.half",
    "up.final",
    "rest.final",
)
COST = 1
LANES = 384
TILE = 128
GELU_TILE = 32


def dot(a, b, ca, cb):
    return lax.dot_general(a, b, (((ca,), (cb,)), ((), ())), preferred_element_type=F32)


def shaped(shape, dtype):
    return jax.ShapeDtypeStruct(shape, dtype)


def call(
    body, out_shape, ins, scratch=(), in_specs=None, out_specs=None, limit=None
):
    nbytes = sum(a.size * a.dtype.itemsize for a in ins)
    nbytes += sum(o.size * o.dtype.itemsize for o in jax.tree.leaves(out_shape))
    params = dict(
        out_shape=out_shape,
        compiler_params=pltpu.CompilerParams(vmem_limit_bytes=limit or (nbytes + (6 << 20))),
        cost_estimate=pl.CostEstimate(flops=1, bytes_accessed=COST, transcendentals=0),
    )
    return pl.pallas_call(
        body, in_specs=in_specs, out_specs=out_specs, scratch_shapes=list(scratch), **params
    )(*ins)


def peak(value):
    top = jnp.max(jnp.abs(value.astype(F32)), axis=0, keepdims=True)
    return jnp.max(top, axis=1, keepdims=True)


def raise_peaks(pack, tiles):
    for row, tile in enumerate(tiles):
        at = slice(8 + row, 9 + row)
        pack[at, :] = jnp.maximum(pack[at, :], peak(tile))


def project_peaks_body(project, qv_bias, pack):
    @pl.when(pl.program_id(0) == 0)
    def _():
        pack[...] = jnp.zeros_like(pack)
        pack[0:2, :] = qv_bias[...]

    raise_peaks(pack, [project[0], project[1], project[2]])


def rest_peaks_body(merge, up, down, up_bias, pack):
    @pl.when(pl.program_id(0) == 0)
    def _():
        pack[...] = jnp.zeros_like(pack)
        pack[0:1, :] = up_bias[...]

    raise_peaks(pack, [merge[...], up[...], down[...]])


def scale_row(own, other, row, width):
    at = slice(8 + row, 9 + row)
    return 0.5 * jnp.maximum(own[at, 0:width], other[at, 0:width])


def clip_tile(value, scale):
    return (scale * jnp.tanh(value.astype(F32) * (1.0 / scale))).astype(BF16)


def clip_project_body(own, other, project, out):
    for part in range(3):
        out[part] = clip_tile(project[part], scale_row(own, other, part, LANES))


def clip_rest_body(own, other, merge, up, down, merge_q, up_q, down_q):
    for row, (src, dst) in enumerate(((merge, merge_q), (up, up_q), (down, down_q))):
        dst[...] = clip_tile(src[...], scale_row(own, other, row, src.shape[1]))


def key_bias(lengths, first):
    key = lax.broadcasted_iota(jnp.int32, (LONG, 1), 0)
    query = lax.broadcasted_iota(jnp.int32, (1, LONG), 1)
    single = lengths[first] > SHORT
    limit = jnp.full((LONG, 1), lengths[first], jnp.int32)
    for slot in range(1, LONG // SHORT):
        own = jnp.where(single, lengths[first], slot * SHORT + lengths[first + slot])
        limit = jnp.where(key >= slot * SHORT, own, limit)
    key_row = jnp.where(single, 0, key // SHORT)
    query_row = jnp.where(single, 0, query // SHORT)
    key_row = jnp.where(key < limit, key_row, -1)
    return jnp.where(key_row == query_row, 0.0, -1e30).astype(F32)


def qkv_into(xq, weight, bias_pack, q_ref, k_ref, v_ref):
    for part, ref in enumerate((q_ref, k_ref, v_ref)):
        value = dot(xq, weight[part], 1, 0)
        if part == 0:
            value = value + bias_pack[0:1, :]
        if part == 2:
            value = value + bias_pack[1:2, :]
        value = value.astype(BF16)
        if part == 0:
            value = value * jnp.asarray(0.125, BF16)
        ref[...] = value.T


def attend(lengths, first, q_ref, k_ref, v_ref, c_ref, lse_ref, bias_ref):
    bias_ref[...] = key_bias(lengths, first)

    def head(index, carry):
        at = pl.ds(pl.multiple_of(index * HEAD, HEAD), HEAD)
        scores = dot(k_ref[at, :], q_ref[at, :], 0, 0) + bias_ref[...]
        top = jnp.max(scores, axis=0, keepdims=True)
        prob = jnp.exp(scores - top)
        total = jnp.sum(prob, axis=0, keepdims=True)
        mixed = dot(v_ref[at, :], prob.astype(BF16), 1, 0)
        c_ref[at, :] = (mixed * (1.0 / total)).astype(BF16)
        lse_ref[pl.ds(index, 1), :] = top + jnp.log(total)
        return carry

    lax.fori_loop(0, q_ref.shape[0] // HEAD, head, 0, unroll=True)


def forward_first_body(
    ids, lengths, clips, inputs, weight, pack, xq, q_ref, k_ref, v_ref, c_ref, lse_ref, bias_ref
):
    scale = clips[0]
    xq[...] = clip_tile(inputs[...], scale)
    qkv_into(xq[...], weight, pack, q_ref, k_ref, v_ref)
    attend(lengths, ids[2], q_ref, k_ref, v_ref, c_ref, lse_ref, bias_ref)


def forward_second_body(
    ids, lengths, xq, weight, pack, q_ref, k_ref, v_ref, c_ref, lse_ref, bias_ref
):
    qkv_into(xq[...], weight, pack, q_ref, k_ref, v_ref)
    attend(lengths, ids[2], q_ref, k_ref, v_ref, c_ref, lse_ref, bias_ref)


def backward_heads_body(
    which,
    ids,
    lengths,
    xq,
    grad_branch,
    q_ref,
    k_ref,
    v_ref,
    c_ref,
    lse_ref,
    merge_q,
    *refs,
):
    *outs, d_ref, qv_row, bias_ref, g_ref, x_t = refs
    bias_ref[...] = key_bias(lengths, ids[2])
    x_t[...] = xq[...].T
    count, rel = outs[0].shape[0], ids[which]
    width = q_ref.shape[0]
    g_ref[...] = dot(merge_q[...], grad_branch[...], 1, 1).astype(BF16)

    def head(index, carry):
        at = pl.ds(pl.multiple_of(index * HEAD, HEAD), HEAD)
        q, k, v, g = q_ref[at, :], k_ref[at, :], v_ref[at, :], g_ref[at, :]
        scores = dot(k, q, 0, 0) + bias_ref[...]
        prob = jnp.exp(scores - lse_ref[pl.ds(index, 1), :])
        grad_prob = dot(v, g, 0, 0)
        inner = jnp.sum(g.astype(F32) * c_ref[at, :].astype(F32), axis=0, keepdims=True)
        grad_score = (prob * (grad_prob - inner)).astype(BF16)
        d_ref[2, at, :] = dot(g, prob.astype(BF16), 1, 1).astype(BF16)
        d_ref[0, at, :] = (dot(k, grad_score, 1, 0) * 0.125).astype(BF16)
        d_ref[1, at, :] = dot(q, grad_score, 1, 1).astype(BF16)
        return carry

    lax.fori_loop(0, width // HEAD, head, 0, unroll=True)
    rows, step = x_t.shape[0] // (2 * count), width // (2 * count)
    if len(outs) == 2:
        outs = [out.at[:, at * rows : (at + 1) * rows, :] for out in outs for at in range(4)]
    for half, parts in ((1, outs[:4]), (0, outs[4:])):
        base = half_base(rel, half, 2 * count)
        at = pl.ds(pl.multiple_of(base * rows, count * rows), count * rows)
        for part in range(3):
            grad = dot(x_t[at, :], d_ref[part], 1, 1).astype(BF16)
            for block in range(count):
                to = ((base + block) ^ rel) % count
                piece = grad[block * rows : (block + 1) * rows, :]
                parts[part][to] = piece
        at = pl.ds(pl.multiple_of(base * step, count * step), count * step)
        grad = dot(c_ref[at, :], grad_branch[...], 1, 0)
        for block in range(count):
            to = ((base + block) ^ rel) % count
            piece = grad[block * step : (block + 1) * step, :]
            piece = jnp.concatenate([piece[:, :width], piece[:, width:]], axis=0)
            parts[3][to] = piece.astype(BF16)
    ones = jnp.ones((8, xq.shape[0]), BF16)
    qv_row[:, 0:width] = dot(ones, d_ref[0], 1, 1)
    qv_row[:, width : 2 * width] = dot(ones, d_ref[2], 1, 1)


def gelu_parts(hidden, scale):
    area = 0.5 + 0.5 * lax.erf(hidden * 0.7071067811865476)
    bell = jnp.exp(-0.5 * hidden * hidden)
    active = hidden * area
    slope = area + hidden * bell * 0.3989422804014327
    bent = jnp.tanh(active * (1.0 / scale))
    return (scale * bent).astype(BF16), ((1.0 - bent * bent) * slope).astype(BF16), active


def fold(value, op):
    rows, lanes = value.shape
    return op(value.reshape(rows // 8, 8, lanes), axis=0)


def middle_body(
    clips,
    c_own,
    c_other,
    merge_own,
    merge_other,
    inputs,
    up_own,
    up_other,
    down_own,
    down_other,
    pack_own,
    pack_other,
    vectors,
    cotangent,
    unit_out,
    inverse_out,
    normed_q,
    active_own,
    active_other,
    factor_own,
    factor_other,
    output,
    grad_sum,
    grad_feed,
    sums,
    work,
    hidden_ref,
    second_ref,
    tops,
    sum_ref,
):
    total = inputs.shape[0]
    work[...] = dot(c_own[...], merge_own[...], 0, 0) + dot(c_other[...], merge_other[...], 0, 0)
    tops[...] = jnp.zeros_like(tops)
    sum_ref[...] = jnp.zeros_like(sum_ref)
    clip_first, clip_second = clips[1], clips[2]

    def first_norm(index, carry):
        at = pl.ds(pl.multiple_of(index * TILE, TILE), TILE)
        rows = inputs[at, :].astype(F32)
        value = rows + work[at, :] + vectors[0:1, :]
        mean = jnp.mean(value, axis=-1, keepdims=True)
        centred = value - mean
        inverse = lax.rsqrt(jnp.mean(centred * centred, axis=-1, keepdims=True) + EPSILON)
        unit = centred * inverse
        normed = unit * vectors[2:3, :] + vectors[4:5, :]
        unit_out[at, :] = unit
        inverse_out[at, :] = jnp.broadcast_to(inverse, (TILE, 128))
        normed_q[at, :] = clip_tile(normed, clip_first)
        tops[0] = jnp.maximum(tops[0], fold(jnp.abs(rows), jnp.max))
        tops[1] = jnp.maximum(tops[1], fold(jnp.abs(normed), jnp.max))
        work[at, :] = normed
        return carry

    lax.fori_loop(0, total // TILE, first_norm, 0)
    span = hidden_ref.shape[1]
    for weight, pack, active_ref, factor_ref in (
        (up_own, pack_own, active_own, factor_own),
        (up_other, pack_other, active_other, factor_other),
    ):

        def gelu_chunk(source, index):
            cols = pl.ds(pl.multiple_of(index * span, span), span)
            bias = pack[0:1, cols]
            top = tops[2, :, 0:span]
            for row in range(total // GELU_TILE):
                at = slice(row * GELU_TILE, (row + 1) * GELU_TILE)
                clipped, factor, active = gelu_parts(source[at, :] + bias, clip_second)
                active_ref[at, cols] = clipped
                factor_ref[at, cols] = factor
                top = jnp.maximum(top, fold(jnp.abs(active), jnp.max))
            tops[2, :, 0:span] = top

        def multiply(target, index):
            cols = pl.ds(pl.multiple_of(index * span, span), span)
            target[...] = dot(normed_q[...], weight[:, cols], 1, 0)

        chunks = weight.shape[1] // span
        multiply(hidden_ref, 0)

        def pair(index, carry):
            multiply(second_ref, 2 * index + 1)
            gelu_chunk(hidden_ref, 2 * index)
            multiply(hidden_ref, jnp.minimum(2 * index + 2, chunks - 1))
            gelu_chunk(second_ref, 2 * index + 1)
            return carry

        lax.fori_loop(0, chunks // 2, pair, 0)
    work[...] += dot(active_own[...], down_own[...], 1, 0) + dot(
        active_other[...], down_other[...], 1, 0
    )

    def second_norm(index, carry):
        at = pl.ds(pl.multiple_of(index * TILE, TILE), TILE)
        value = work[at, :] + vectors[1:2, :]
        mean = jnp.mean(value, axis=-1, keepdims=True)
        centred = value - mean
        inverse = lax.rsqrt(jnp.mean(centred * centred, axis=-1, keepdims=True) + EPSILON)
        unit = centred * inverse
        output[at, :] = (unit * vectors[3:4, :] + vectors[5:6, :]).astype(BF16)
        upstream = cotangent[at, :].astype(F32)
        scaled = upstream * vectors[3:4, :]
        grad = inverse * (
            scaled
            - jnp.mean(scaled, axis=-1, keepdims=True)
            - unit * jnp.mean(scaled * unit, axis=-1, keepdims=True)
        )
        grad_sum[at, :] = grad
        grad_feed[at, :] = grad.astype(BF16)
        sum_ref[0] += fold(upstream * unit, jnp.sum)
        sum_ref[1] += fold(upstream, jnp.sum)
        sum_ref[2] += fold(grad, jnp.sum)
        return carry

    lax.fori_loop(0, total // TILE, second_norm, 0)
    for row in range(3):
        sums[row : row + 1, :] = jnp.sum(sum_ref[row], axis=0, keepdims=True)
    for row in range(3):
        top = jnp.max(jnp.max(tops[row], axis=0, keepdims=True), axis=1, keepdims=True)
        sums[3 + row : 4 + row, :] = jnp.broadcast_to(top, (1, sums.shape[1]))
    sums[6:8, :] = jnp.zeros((2, sums.shape[1]), F32)


def half_base(rel, half, blocks):
    return (half ^ (rel // (blocks // 2))) * (blocks // 2)


def down_grad_body(which, half, ids, active, grad_feed, chunk):
    rel = ids[which]
    count = chunk.shape[0]
    rows = active.shape[1] // (2 * count)
    base = half_base(rel, half, 2 * count)
    per = count // 2
    for tile in range(2):
        first = base + tile * per
        cols = pl.ds(pl.multiple_of(first * rows, per * rows), per * rows)
        grad = dot(active[:, cols], grad_feed[...], 0, 0)
        for block in range(per):
            piece = grad[block * rows : (block + 1) * rows, :].astype(BF16)
            to = ((first + block) ^ rel) % count
            chunk[to, 0:rows, :] = piece[:, :LANES]
            chunk[to, rows : 2 * rows, :] = piece[:, LANES:]


def up_grad_body(
    which, ids, grad_feed, down, up, factor, normed_q, before, high, low, bias_row, grad_normed, g_ref
):
    rel = ids[which]
    count = high.shape[0]
    span = 512

    def columns(index, carry):
        cols = pl.ds(pl.multiple_of(index * span, span), span)
        grad = dot(grad_feed[...], down[cols, :], 1, 1) * factor[:, cols].astype(F32)
        grad = grad.astype(BF16)
        g_ref[:, cols] = grad
        bias_row[0:1, cols] = jnp.sum(grad.astype(F32), axis=0, keepdims=True)
        return carry

    lax.fori_loop(0, g_ref.shape[1] // span, columns, 0)
    rows = normed_q.shape[1] // (2 * count)
    for half, chunk in ((1, high), (0, low)):
        base = half_base(rel, half, 2 * count)
        cols = pl.ds(pl.multiple_of(base * rows, count * rows), count * rows)
        grad = dot(normed_q[:, cols], g_ref[...], 0, 0)
        for block in range(count):
            to = ((base + block) ^ rel) % count
            for part in range(grad.shape[1] // LANES):
                piece = grad[block * rows : (block + 1) * rows, part * LANES : (part + 1) * LANES]
                chunk[to, part * rows : (part + 1) * rows, :] = piece.astype(BF16)
    result = dot(g_ref[...], up[...], 1, 1)
    if before is not None:
        result = result + before[...]
    grad_normed[...] = result


def up_grad_first_body(which, ids, grad_feed, down, up, factor, normed_q, *outs):
    up_grad_body(which, ids, grad_feed, down, up, factor, normed_q, None, *outs)


def first_norm_back_body(
    clips,
    grad_normed,
    grad_sum,
    unit_ref,
    inverse_ref,
    vectors,
    sums,
    bias_other,
    bias_own,
    grad_first,
    grad_branch,
    pack_other,
    pack_own,
    sum_ref,
):
    clip_first = clips[1]
    sum_ref[...] = jnp.zeros_like(sum_ref)

    def rows(index, carry):
        at = pl.ds(pl.multiple_of(index * TILE, TILE), TILE)
        unit = unit_ref[at, :]
        bent = jnp.tanh((unit * vectors[2:3, :] + vectors[4:5, :]) * (1.0 / clip_first))
        grad = grad_normed[at, :] * (1.0 - bent * bent) + grad_sum[at, :]
        scaled = grad * vectors[2:3, :]
        back = inverse_ref[at, 0:1] * (
            scaled
            - jnp.mean(scaled, axis=-1, keepdims=True)
            - unit * jnp.mean(scaled * unit, axis=-1, keepdims=True)
        )
        grad_first[at, :] = back
        grad_branch[at, :] = back.astype(BF16)
        sum_ref[0] += fold(grad * unit, jnp.sum)
        sum_ref[1] += fold(grad, jnp.sum)
        sum_ref[2] += fold(back, jnp.sum)
        return carry

    lax.fori_loop(0, unit_ref.shape[0] // TILE, rows, 0)
    width = unit_ref.shape[1]
    for pack, bias in ((pack_other, bias_other), (pack_own, bias_own)):
        pack[...] = jnp.zeros_like(pack)
        for row, source in ((0, 0), (2, 1), (4, 2)):
            pack[row : row + 1, :] = jnp.sum(sum_ref[source], axis=0, keepdims=True)
        pack[1:2, :] = sums[0:1, :]
        pack[3:4, :] = sums[1:2, :]
        pack[5:6, :] = sums[2:3, :]
        pack[6:7, :] = bias[0:1, 0:width]
        pack[7:8, :] = bias[0:1, width : 2 * width]
        pack[12:15, :] = sums[3:6, :]


def input_grad_body(clips, inputs, grad_first, w_own, w_other, d_own, d_other, out):
    terms = []
    for d_ref, weight in ((d_own, w_own), (d_other, w_other)):
        for part in range(3):
            terms.append(dot(d_ref[part], weight[part], 0, 1))
    bent = jnp.tanh(inputs[...].astype(F32) * (1.0 / clips[0]))
    out[...] = sum(terms[1:], terms[0]) * (1.0 - bent * bent) + grad_first[...]


def slope_of(weight, scale):
    bent = jnp.tanh(weight.astype(F32) * (1.0 / scale))
    return 1.0 - bent * bent


def block_value(rel, low, high, at):
    half = low.shape[0]
    at = at ^ rel
    first = low[jnp.minimum(at, half - 1)].astype(F32)
    return jnp.where(at < half, first, high[jnp.maximum(at - half, 0)].astype(F32))


def down_final_body(per, ids, own, other, low, high, weight, out):
    rows = weight.shape[0] // per
    slope = slope_of(weight[...], scale_row(own, other, 2, weight.shape[1]))
    for index in range(per):
        value = block_value(ids[0], low, high, pl.program_id(0) * per + index)
        at = slice(index * rows, (index + 1) * rows)
        out[at, :LANES] = value[:rows] * slope[at, :LANES]
        out[at, LANES:] = value[rows:] * slope[at, LANES:]


def up_final_body(per, ids, own, other, low, high, weight, out):
    rows = weight.shape[0] // per
    slope = slope_of(weight[...], scale_row(own, other, 1, weight.shape[1]))
    for index in range(per):
        value = block_value(ids[0], low, high, pl.program_id(0) * per + index)
        at = slice(index * rows, (index + 1) * rows)
        for part in range(weight.shape[1] // LANES):
            cols = slice(part * LANES, (part + 1) * LANES)
            out[at, cols] = value[part * rows : (part + 1) * rows] * slope[at, cols]


def rest_final_body(half, per, ids, own, other, chunk, p_own, p_other, project, merge, *refs):
    project_out, merge_out = refs[-2:]
    rows, step = project.shape[1] // per, merge.shape[0] // per
    count = chunk.shape[0]
    first = half_base(ids[0], half, 2 * count) + pl.program_id(0) * per
    values = []
    for index in range(per):
        values.append(chunk[((first + index) ^ ids[0]) % count].astype(F32))
    for part in range(3):
        slope = slope_of(project[part], scale_row(p_own, p_other, part, LANES))
        for index in range(per):
            at = slice(index * rows, (index + 1) * rows)
            project_out[part, at, :] = values[index][part * rows : (part + 1) * rows] * slope[at]
    slope = slope_of(merge[...], scale_row(own, other, 0, merge.shape[1]))
    for part in range(2):
        across = slice(part * LANES, (part + 1) * LANES)
        piece = [v[3 * rows + part * step : 3 * rows + (part + 1) * step] for v in values]
        merge_out[:, across] = jnp.concatenate(piece, axis=0) * slope[:, across]


class Exchange:
    def __init__(self, size, first):
        self.bits = size.bit_length() - 1
        assert 1 << self.bits == size and self.bits >= 4
        self.size = size
        self.orders = [list(order) + list(range(4, self.bits)) for order in first]
        self.blocks = 16

    def relative(self, position, core):
        total = 0
        for stage in range(4):
            bit = (position >> self.orders[core][stage]) & 1
            total = total + (bit << (3 - stage))
        return total

    def swap(self, value, stage):
        pairs = []
        for index in range(self.size):
            for core in range(2):
                to = index ^ (1 << self.orders[core][stage])
                pairs.append((2 * index + core, 2 * to + core))
        return lax.ppermute(value, ("dp", "tensor"), pairs)

    def core_swap(self, value):
        return lax.ppermute(value, "tensor", [(0, 1), (1, 0)])


class Task:
    def __init__(self, body, deps):
        self.body, self.deps, self.sends = body, list(deps), []


class Plan:
    def __init__(self):
        self.tasks = {}
        self.values = {}
        self.source = {}

    def given(self, name, value):
        self.values[name] = value
        return name

    def core(self, name, body, deps):
        self.tasks[name] = Task(body, deps)
        return name

    def send(self, name, source, body):
        self.tasks[source].sends.append((name, body))
        self.source[name] = source
        return name

    def run(self):
        values, last = dict(self.values), None

        def take(name):
            nonlocal last
            if name in values:
                return
            if name in self.source:
                take(self.source[name])
                return
            task = self.tasks[name]
            for dep in task.deps:
                take(dep)
            inputs = [values[dep] for dep in task.deps]
            if last is not None:
                inputs, last = lax.optimization_barrier((inputs, last))
            with jax.named_scope(name.replace(".", "_")):
                result = task.body(*inputs)
            values[name] = result
            last = jax.tree.leaves(result)[0]
            for sent, body in task.sends:
                with jax.named_scope(sent.replace(".", "_")):
                    values[sent] = body(result)

        for name in ORDER:
            if name in self.tasks:
                take(name)
            elif name[1:] in self.source:
                take(name[1:])
                values[name[1:]], last = lax.optimization_barrier((values[name[1:]], last))
        for name in self.tasks:
            take(name)
        return values

    def swap(self, name, source, way, stage, pick=lambda value: value):
        return self.send(name, source, lambda value: way.swap(pick(value), stage))

    def reduce(self, name, way, mine, theirs, pick):
        def swapped(index):
            return lambda v: [way.core_swap(value) for value in pick(v, index)]

        def whole(values):
            return values[0] if len(values) == 1 else jnp.concatenate(values, axis=1)

        high = self.send(name + ".high", theirs[0], swapped(0))
        low = self.send(name + ".low", theirs[1], swapped(1))
        value = self.core(
            f"{name}.add0",
            lambda mine, high: total([whole(pick(mine, 0)), whole(high)]),
            [mine[0], high],
        )
        got = self.swap(f"{name}.in0", value, way, 0)

        def second(mine, low, got):
            return split_in_two([whole(pick(mine, 1)), whole(low), got])

        def more(kept, got):
            return split_in_two([kept[0], got])

        value = self.core(f"{name}.add1", second, [mine[1], low, got])
        for stage in (1, 2, 3):
            got = self.swap(f"{name}.in{stage}", value, way, stage, second_of)
            if stage < 3:
                value = self.core(f"{name}.add{stage + 1}", more, [value, got])
        value = self.core(f"{name}.sum", lambda kept, got: total([kept[0], got]), [value, got])
        for stage in range(4, way.bits):
            sent = self.swap(f"{name}.in{stage}", value, way, stage)
            value = self.core(f"{name}.sum{stage}", lambda a, b: total([a, b]), [value, sent])
        for stage in reversed(range(4)):
            sent = self.swap(f"{name}.out{stage}", value, way, stage)
            if stage > 0:
                value = self.core(
                    f"{name}.join{stage}",
                    lambda a, b: jnp.concatenate([a, b], axis=0),
                    [value, sent],
                )
        return [value, sent]


def total(values):
    out = values[0].astype(F32)
    for value in values[1:]:
        out = out + value.astype(F32)
    return out.astype(BF16)


def split_in_two(values):
    half = values[0].shape[0] // 2
    return total([value[:half] for value in values]), total([value[half:] for value in values])


def second_of(value):
    return value[1]


def local(
    inputs,
    row_lengths,
    project_weight,
    merge_weight,
    up_weight,
    down_weight,
    query_value_bias,
    merge_bias,
    up_bias,
    down_bias,
    norm_gains,
    norm_shifts,
    clip_scales,
    cotangent,
):
    size = lax.axis_size("dp")
    exchange = Exchange(size, ((0, 1, 2, 3), (1, 0, 2, 3)))
    same_way = Exchange(size, ((0, 1, 2, 3), (0, 1, 2, 3)))
    blocks = exchange.blocks
    member = lax.axis_index("tensor")
    place = lax.axis_index("dp")
    rel0, rel1 = exchange.relative(place, 0), exchange.relative(place, 1)
    own_rel = jnp.where(member == 0, rel0, rel1)
    other_rel = jnp.where(member == 0, rel1, rel0)
    ids = jnp.stack([own_rel, other_rel, member * (LONG // SHORT)]).astype(jnp.int32)
    total, width = inputs.shape
    hidden = up_weight.shape[1]
    project = jnp.transpose(project_weight, (1, 0, 2))

    steps = 4
    small_grid = pltpu.CompilerParams(vmem_limit_bytes=12 << 20)
    project_block = pl.BlockSpec((3, width // steps, LANES), lambda i: (0, i, 0))
    rest_blocks = [
        pl.BlockSpec((LANES // steps, width), lambda i: (i, 0)),
        pl.BlockSpec((width // steps, hidden), lambda i: (i, 0)),
        pl.BlockSpec((hidden // steps, width), lambda i: (i, 0)),
    ]
    project_pack_spec = pl.BlockSpec((16, LANES), lambda i: (0, 0))
    pack_spec = pl.BlockSpec((16, hidden), lambda i: (0, 0))
    rest_weights = (merge_weight, up_weight, down_weight)

    def project_peaks():
        return pl.pallas_call(
            project_peaks_body,
            grid=(steps,),
            in_specs=[project_block, pl.BlockSpec((2, LANES), lambda i: (0, 0))],
            out_specs=project_pack_spec,
            out_shape=shaped((16, LANES), F32),
            compiler_params=small_grid,
        )(project, query_value_bias)

    def rest_peaks(weights):
        return pl.pallas_call(
            rest_peaks_body,
            grid=(steps,),
            in_specs=rest_blocks + [pl.BlockSpec((1, hidden), lambda i: (0, 0))],
            out_specs=pack_spec,
            out_shape=shaped((16, hidden), F32),
            compiler_params=small_grid,
        )(*weights, up_bias[None])

    def clip_project(own, other):
        return pl.pallas_call(
            clip_project_body,
            grid=(steps,),
            in_specs=[project_pack_spec, project_pack_spec, project_block],
            out_specs=project_block,
            out_shape=shaped(project.shape, BF16),
            compiler_params=small_grid,
        )(own, other, project)

    def clip_rest(own, other):
        return pl.pallas_call(
            clip_rest_body,
            grid=(steps,),
            in_specs=[pack_spec, pack_spec] + rest_blocks,
            out_specs=rest_blocks,
            out_shape=[shaped(a.shape, BF16) for a in rest_weights],
            compiler_params=small_grid,
        )(own, other, *rest_weights)

    project_own_pack = project_peaks()
    project_other_pack = exchange.core_swap(project_own_pack)
    project_own = clip_project(project_own_pack, project_other_pack)
    project_other = exchange.core_swap(project_own)
    tied, project_own = lax.optimization_barrier((rest_weights, project_own))
    own_pack = rest_peaks(tied)
    other_pack = exchange.core_swap(own_pack)
    other_pack, project_other = lax.optimization_barrier((other_pack, project_other))
    merge_own, up_own, down_own = clip_rest(own_pack, other_pack)
    merge_other = exchange.core_swap(merge_own)
    up_other = exchange.core_swap(up_own)
    down_other = exchange.core_swap(down_own)
    project_own, merge_own = lax.optimization_barrier((project_own, merge_own))

    head_shape = shaped((LANES, total), BF16)
    heads_out = [head_shape] * 4 + [shaped((8, total), F32)]
    mask_scratch = pltpu.VMEM((LONG, LONG), F32)
    xq, *own_heads = call(
        forward_first_body,
        [shaped((total, width), BF16)] + heads_out,
        (ids, row_lengths, clip_scales, inputs, project_own, project_own_pack),
        [mask_scratch],
        in_specs=[SMEM] * 3 + [VMEM] * 3,
        out_specs=[VMEM] * 6,
        limit=16 << 20,
    )
    other_heads = call(
        forward_second_body,
        heads_out,
        (ids, row_lengths, xq, project_other, project_other_pack),
        [mask_scratch],
        in_specs=[SMEM] * 2 + [VMEM] * 3,
        out_specs=[VMEM] * 5,
        limit=16 << 20,
    )

    vectors = jnp.concatenate([merge_bias[None], down_bias[None], norm_gains, norm_shifts], axis=0)
    rows_f32 = shaped((total, width), F32)
    rows_bf16 = shaped((total, width), BF16)
    wide = shaped((total, hidden), BF16)
    (
        unit,
        inverse,
        normed_q,
        active_own,
        active_other,
        factor_own,
        factor_other,
        output,
        grad_sum,
        grad_feed,
        sums,
    ) = call(
        middle_body,
        [
            rows_f32,
            shaped((total, 128), F32),
            rows_bf16,
            wide,
            wide,
            wide,
            wide,
            rows_bf16,
            rows_f32,
            rows_bf16,
            shaped((8, width), F32),
        ],
        (
            clip_scales,
            own_heads[3],
            other_heads[3],
            merge_own,
            merge_other,
            inputs,
            up_own,
            up_other,
            down_own,
            down_other,
            own_pack,
            other_pack,
            vectors,
            cotangent,
        ),
        [
            pltpu.VMEM((total, width), F32),
            pltpu.VMEM((total, 256), F32),
            pltpu.VMEM((total, 256), F32),
            pltpu.VMEM((3, 8, width), F32),
            pltpu.VMEM((3, 8, width), F32),
        ],
        in_specs=[SMEM] + [VMEM] * 13,
        out_specs=[VMEM] * 11,
        limit=32 << 20,
    )

    plan = Plan()
    chunk = shaped((blocks // 2, 2 * hidden // blocks, LANES), BF16)

    def down_half(which, half, active, grad):
        return call(
            partial(down_grad_body, which, half),
            chunk,
            (ids, active, grad),
            in_specs=[SMEM] + [VMEM] * 2,
            out_specs=VMEM,
            limit=9 << 20,
        )

    feed = plan.given("feed", grad_feed)
    down_tasks = {}
    for half, word in ((1, "high"), (0, "low")):
        for which, active in ((1, active_other), (0, active_own)):
            down_tasks[which, half] = plan.core(
                ("down.mine", "down.theirs")[which] + word,
                lambda grad, which=which, half=half, active=active: down_half(
                    which, half, active, grad
                ),
                [feed],
            )

    def take(index):
        return lambda values: values[index]

    def part(values, index):
        return values[index]

    def one(values, index):
        return [values[index]]

    down_out = plan.reduce(
        "down",
        exchange,
        (down_tasks[0, 1], down_tasks[0, 0]),
        (down_tasks[1, 1], down_tasks[1, 0]),
        lambda value, index: [value],
    )

    def up_half(body, which, grad, down, up, factor, *before):
        return call(
            partial(body, which),
            [chunk, chunk, shaped((1, hidden), F32), rows_f32],
            (ids, grad, down, up, factor, normed_q) + before,
            [pltpu.VMEM((total, hidden), BF16)],
            in_specs=[SMEM] + [VMEM] * (5 + len(before)),
            out_specs=[VMEM] * 4,
            limit=20 << 20,
        )

    up_theirs = plan.core(
        "up.theirs",
        lambda grad: up_half(
            up_grad_first_body, 1, grad, down_other, up_other, factor_other
        ),
        [feed],
    )
    up_mine = plan.core(
        "up.mine",
        lambda grad, before: up_half(
            up_grad_body, 0, grad, down_own, up_own, factor_own, before[3]
        ),
        [feed, up_theirs],
    )
    up_out = plan.reduce("up", exchange, (up_mine, up_mine), (up_theirs, up_theirs), one)

    small = shaped((16, width), F32)

    def norm_back(theirs, mine):
        ins = (clip_scales, mine[3], grad_sum, unit, inverse, vectors, sums, theirs[2], mine[2])
        return call(
            first_norm_back_body,
            [rows_f32, rows_bf16, small, small],
            ins,
            [pltpu.VMEM((3, 8, width), F32)],
            in_specs=[SMEM] + [VMEM] * 8,
            out_specs=[VMEM] * 4,
        )

    first_back = plan.core("norm", norm_back, [up_theirs, up_mine])

    def heads_back(which, back, heads, merge_q):
        count = (1, 4)[which]
        parts = [shaped((chunk.shape[0], chunk.shape[1] // count, LANES), BF16)] * count
        *outs, grads, row = call(
            partial(backward_heads_body, which),
            parts + parts + [shaped((3, LANES, total), BF16), shaped((8, 2 * LANES), F32)],
            (ids, row_lengths, xq, back[1]) + tuple(heads) + (merge_q,),
            [
                mask_scratch,
                pltpu.VMEM((LANES, total), BF16),
                pltpu.VMEM((width, total), BF16),
            ],
            in_specs=[SMEM] * 2 + [VMEM] * 8,
            out_specs=[VMEM] * (2 * count + 2),
            limit=18 << 20,
        )
        return outs[:count], outs[count:], grads, row

    heads_theirs = plan.core(
        "heads.theirs", lambda back: heads_back(1, back, other_heads, merge_other), [first_back]
    )
    heads_mine = plan.core(
        "heads.mine", lambda back: heads_back(0, back, own_heads, merge_own), [first_back]
    )
    rest_out = plan.reduce(
        "rest", exchange, (heads_mine, heads_mine), (heads_theirs, heads_theirs), part
    )

    def input_part(back, theirs, mine):
        return call(
            input_grad_body,
            rows_f32,
            (clip_scales, inputs, back[0], project_own, project_other, mine[2], theirs[2]),
            in_specs=[SMEM] + [VMEM] * 6,
            out_specs=VMEM,
            limit=16 << 20,
        )

    input_task = plan.core("input", input_part, [first_back, heads_theirs, heads_mine])

    def joined(sums_part, row):
        return jnp.concatenate([sums_part[:8], row[0:1], sums_part[12:15]], axis=0)

    small_row = lax.broadcasted_iota(jnp.int32, (12, width), 0)

    def merge_small(a, b):
        return jnp.where(small_row < 9, a + b, jnp.maximum(a, b))

    theirs_small = plan.core(
        "small.theirs", lambda back, heads: joined(back[2], heads[3]), [first_back, heads_theirs]
    )
    small_got = plan.send("small.got", theirs_small, exchange.core_swap)
    small_value = plan.core(
        "small.mine",
        lambda got, back, heads: merge_small(joined(back[3], heads[3]), got),
        [small_got, first_back, heads_mine],
    )
    for stage in range(exchange.bits):
        swap = partial(same_way.swap, stage=stage)
        small_in = plan.send(f"small.in{stage}", small_value, swap)
        small_value = plan.core(f"small.sum{stage}", merge_small, [small_value, small_in])

    final_steps = 4
    per = blocks // final_steps

    def final(body, parts, weights, specs):
        part_specs = [pl.BlockSpec(part.shape, lambda i, s: (0, 0, 0)) for part in parts]
        pack = pl.BlockSpec((16, hidden), lambda i, s: (0, 0))
        ins = (ids, own_pack, other_pack) + tuple(parts) + weights
        return pl.pallas_call(
            partial(body, per),
            grid_spec=pltpu.PrefetchScalarGridSpec(
                num_scalar_prefetch=1,
                grid=(final_steps,),
                in_specs=[pack, pack]
                + part_specs
                + specs,
                out_specs=specs,
            ),
            out_shape=[shaped(weight.shape, F32) for weight in weights],
            compiler_params=pltpu.CompilerParams(vmem_limit_bytes=10 << 20),
            cost_estimate=pl.CostEstimate(flops=1, bytes_accessed=1, transcendentals=0),
        )(*ins)

    down_spec = pl.BlockSpec((hidden // final_steps, width), lambda i, s: (i, 0))
    plan.core(
        "down.final",
        lambda *parts: final(down_final_body, parts, (down_weight,), [down_spec])[0],
        down_out,
    )
    up_spec = pl.BlockSpec((width // final_steps, hidden), lambda i, s: (i, 0))
    plan.core(
        "up.final",
        lambda *parts: final(up_final_body, parts, (up_weight,), [up_spec])[0],
        up_out,
    )

    def rest_final(half, chunk, *before):
        before = tuple(before[0]) if before else ()

        def place(i, s):
            return (half ^ (s[0] // (blocks // 2))) * (final_steps // 2) + i

        specs = [
            pl.BlockSpec((3, width // final_steps, LANES), lambda i, s: (0, place(i, s), 0)),
            pl.BlockSpec((LANES // final_steps, width), lambda i, s: (place(i, s), 0)),
        ]
        weights = (project, merge_weight)
        packs = (project_own_pack, project_other_pack)
        ins = (ids, own_pack, other_pack, chunk) + packs + weights
        pack = pl.BlockSpec((16, hidden), lambda i, s: (0, 0))
        narrow = pl.BlockSpec((16, LANES), lambda i, s: (0, 0))
        return pl.pallas_call(
            partial(rest_final_body, half, per),
            grid_spec=pltpu.PrefetchScalarGridSpec(
                num_scalar_prefetch=1,
                grid=(final_steps // 2,),
                in_specs=[pack, pack, pl.BlockSpec(chunk.shape, lambda i, s: (0, 0, 0))]
                + [narrow, narrow]
                + specs
                + [pl.BlockSpec(memory_space=pl.ANY)] * len(before),
                out_specs=specs,
            ),
            out_shape=[shaped(weight.shape, F32) for weight in weights],
            input_output_aliases={len(ins) + at: at for at in range(len(before))},
            compiler_params=pltpu.CompilerParams(vmem_limit_bytes=10 << 20),
            cost_estimate=pl.CostEstimate(flops=1, bytes_accessed=1, transcendentals=0),
        )(*ins, *before)

    plan.core("rest.half", partial(rest_final, 0), rest_out[:1])
    plan.core("rest.final", partial(rest_final, 1), [rest_out[1], "rest.half"])
    values = plan.run()
    small_all = values[small_value]
    project_grad, merge_grad = values["rest.final"]
    peaks = small_all[9:12, 0]
    return (
        output,
        values[input_task],
        jnp.transpose(project_grad, (1, 0, 2)),
        merge_grad,
        values["up.final"],
        values["down.final"],
        small_all[8].reshape(2, LANES),
        small_all[4],
        small_all[6:8].reshape(hidden),
        small_all[5],
        small_all[0:2],
        small_all[2:4],
        DECAY * clip_scales + (1.0 - DECAY) * peaks,
    )


def solution(mesh):
    return jax.shard_map(
        local,
        mesh=mesh,
        in_specs=(
            P(("dp", "tensor"), None),
            P("dp"),
            P(None, None, "tensor"),
            P("tensor", None),
            P(None, "tensor"),
            P("tensor", None),
            P(None, "tensor"),
            P(),
            P("tensor"),
            P(),
            P(),
            P(),
            P(),
            P(("dp", "tensor"), None),
        ),
        out_specs=(
            P(("dp", "tensor"), None),
            P(("dp", "tensor"), None),
            P(None, None, "tensor"),
            P("tensor", None),
            P(None, "tensor"),
            P("tensor", None),
            P(None, "tensor"),
            P(),
            P("tensor"),
            P(),
            P(),
            P(),
            P(),
        ),
        check_vma=False,
    )
```

```python
from functools import partial

import jax
import jax.numpy as jnp
from jax import lax
from jax.experimental import pallas as pl
from jax.experimental.pallas import tpu as pltpu
from jax.sharding import PartitionSpec as P

HEAD = 64
LONG = 512
SHORT = 128
EPSILON = 1e-12
DECAY = 0.9
F32 = jnp.float32
BF16 = jnp.bfloat16
VMEM = pl.BlockSpec(memory_space=pltpu.VMEM)
SMEM = pl.BlockSpec(memory_space=pltpu.SMEM)
ORDER = (
    "down.theirshigh",
    "down.minehigh",
    "down.theirslow",
    "down.add0",
    "down.minelow",
    "up.theirs",
    "up.mine",
    "down.add1",
    "up.add0",
    "norm",
    "heads.theirs",
    "heads.mine",
    "down.add2",
    "up.add1",
    "rest.add0",
    "input",
    "down.add3",
    "small.theirs",
    "down.sum",
    "up.add2",
    "rest.add1",
    "small.mine",
    "down.join3",
    "up.add3",
    "rest.add2",
    "down.join2",
    "up.sum",
    "rest.add3",
    "small.sum0",
    "down.join1",
    "up.join3",
    "small.sum1",
    "rest.sum",
    "small.sum2",
    "up.join2",
    "rest.join3",
    "down.final",
    "rest.join2",
    "up.join1",
    "small.sum3",
    "rest.join1",
    "rest.half",
    "up.final",
    "rest.final",
)
COST = 1
LANES = 384
TILE = 128
GELU_TILE = 32


def dot(a, b, ca, cb):
    return lax.dot_general(a, b, (((ca,), (cb,)), ((), ())), preferred_element_type=F32)


def shaped(shape, dtype):
    return jax.ShapeDtypeStruct(shape, dtype)


def call(
    body, out_shape, ins, scratch=(), in_specs=None, out_specs=None, limit=None
):
    nbytes = sum(a.size * a.dtype.itemsize for a in ins)
    nbytes += sum(o.size * o.dtype.itemsize for o in jax.tree.leaves(out_shape))
    params = dict(
        out_shape=out_shape,
        compiler_params=pltpu.CompilerParams(vmem_limit_bytes=limit or (nbytes + (6 << 20))),
        cost_estimate=pl.CostEstimate(flops=1, bytes_accessed=COST, transcendentals=0),
    )
    return pl.pallas_call(
        body, in_specs=in_specs, out_specs=out_specs, scratch_shapes=list(scratch), **params
    )(*ins)


def peak(value):
    top = jnp.max(jnp.abs(value.astype(F32)), axis=0, keepdims=True)
    return jnp.max(top, axis=1, keepdims=True)


def raise_peaks(pack, tiles):
    for row, tile in enumerate(tiles):
        at = slice(8 + row, 9 + row)
        pack[at, :] = jnp.maximum(pack[at, :], peak(tile))


def project_peaks_body(project, qv_bias, pack):
    @pl.when(pl.program_id(0) == 0)
    def _():
        pack[...] = jnp.zeros_like(pack)
        pack[0:2, :] = qv_bias[...]

    raise_peaks(pack, [project[0], project[1], project[2]])


def rest_peaks_body(merge, up, down, up_bias, pack):
    @pl.when(pl.program_id(0) == 0)
    def _():
        pack[...] = jnp.zeros_like(pack)
        pack[0:1, :] = up_bias[...]

    raise_peaks(pack, [merge[...], up[...], down[...]])


def scale_row(own, other, row, width):
    at = slice(8 + row, 9 + row)
    return 0.5 * jnp.maximum(own[at, 0:width], other[at, 0:width])


def clip_tile(value, scale):
    return (scale * jnp.tanh(value.astype(F32) * (1.0 / scale))).astype(BF16)


def clip_project_body(own, other, project, out):
    for part in range(3):
        out[part] = clip_tile(project[part], scale_row(own, other, part, LANES))


def clip_rest_body(own, other, merge, up, down, merge_q, up_q, down_q):
    for row, (src, dst) in enumerate(((merge, merge_q), (up, up_q), (down, down_q))):
        dst[...] = clip_tile(src[...], scale_row(own, other, row, src.shape[1]))


def key_bias(lengths, first):
    key = lax.broadcasted_iota(jnp.int32, (LONG, 1), 0)
    query = lax.broadcasted_iota(jnp.int32, (1, LONG), 1)
    single = lengths[first] > SHORT
    limit = jnp.full((LONG, 1), lengths[first], jnp.int32)
    for slot in range(1, LONG // SHORT):
        own = jnp.where(single, lengths[first], slot * SHORT + lengths[first + slot])
        limit = jnp.where(key >= slot * SHORT, own, limit)
    key_row = jnp.where(single, 0, key // SHORT)
    query_row = jnp.where(single, 0, query // SHORT)
    key_row = jnp.where(key < limit, key_row, -1)
    return jnp.where(key_row == query_row, 0.0, -1e30).astype(F32)


def qkv_into(xq, weight, bias_pack, q_ref, k_ref, v_ref):
    for part, ref in enumerate((q_ref, k_ref, v_ref)):
        value = dot(xq, weight[part], 1, 0)
        if part == 0:
            value = value + bias_pack[0:1, :]
        if part == 2:
            value = value + bias_pack[1:2, :]
        value = value.astype(BF16)
        if part == 0:
            value = value * jnp.asarray(0.125, BF16)
        ref[...] = value.T


def attend(lengths, first, q_ref, k_ref, v_ref, c_ref, lse_ref, bias_ref):
    bias_ref[...] = key_bias(lengths, first)

    def head(index, carry):
        at = pl.ds(pl.multiple_of(index * HEAD, HEAD), HEAD)
        scores = dot(k_ref[at, :], q_ref[at, :], 0, 0) + bias_ref[...]
        top = jnp.max(scores, axis=0, keepdims=True)
        prob = jnp.exp(scores - top)
        total = jnp.sum(prob, axis=0, keepdims=True)
        mixed = dot(v_ref[at, :], prob.astype(BF16), 1, 0)
        c_ref[at, :] = (mixed * (1.0 / total)).astype(BF16)
        lse_ref[pl.ds(index, 1), :] = top + jnp.log(total)
        return carry

    lax.fori_loop(0, q_ref.shape[0] // HEAD, head, 0, unroll=True)


def forward_first_body(
    ids, lengths, clips, inputs, weight, pack, xq, q_ref, k_ref, v_ref, c_ref, lse_ref, bias_ref
):
    scale = clips[0]
    xq[...] = clip_tile(inputs[...], scale)
    qkv_into(xq[...], weight, pack, q_ref, k_ref, v_ref)
    attend(lengths, ids[2], q_ref, k_ref, v_ref, c_ref, lse_ref, bias_ref)


def forward_second_body(
    ids, lengths, xq, weight, pack, q_ref, k_ref, v_ref, c_ref, lse_ref, bias_ref
):
    qkv_into(xq[...], weight, pack, q_ref, k_ref, v_ref)
    attend(lengths, ids[2], q_ref, k_ref, v_ref, c_ref, lse_ref, bias_ref)


def backward_heads_body(
    which,
    ids,
    lengths,
    xq,
    grad_branch,
    q_ref,
    k_ref,
    v_ref,
    c_ref,
    lse_ref,
    merge_q,
    *refs,
):
    *outs, d_ref, qv_row, bias_ref, g_ref, x_t = refs
    bias_ref[...] = key_bias(lengths, ids[2])
    x_t[...] = xq[...].T
    count, rel = outs[0].shape[0], ids[which]
    width = q_ref.shape[0]
    g_ref[...] = dot(merge_q[...], grad_branch[...], 1, 1).astype(BF16)

    def head(index, carry):
        at = pl.ds(pl.multiple_of(index * HEAD, HEAD), HEAD)
        q, k, v, g = q_ref[at, :], k_ref[at, :], v_ref[at, :], g_ref[at, :]
        scores = dot(k, q, 0, 0) + bias_ref[...]
        prob = jnp.exp(scores - lse_ref[pl.ds(index, 1), :])
        grad_prob = dot(v, g, 0, 0)
        inner = jnp.sum(g.astype(F32) * c_ref[at, :].astype(F32), axis=0, keepdims=True)
        grad_score = (prob * (grad_prob - inner)).astype(BF16)
        d_ref[2, at, :] = dot(g, prob.astype(BF16), 1, 1).astype(BF16)
        d_ref[0, at, :] = (dot(k, grad_score, 1, 0) * 0.125).astype(BF16)
        d_ref[1, at, :] = dot(q, grad_score, 1, 1).astype(BF16)
        return carry

    lax.fori_loop(0, width // HEAD, head, 0, unroll=True)
    rows, step = x_t.shape[0] // (2 * count), width // (2 * count)
    if len(outs) == 2:
        outs = [out.at[:, at * rows : (at + 1) * rows, :] for out in outs for at in range(4)]
    for half, parts in ((1, outs[:4]), (0, outs[4:])):
        base = half_base(rel, half, 2 * count)
        at = pl.ds(pl.multiple_of(base * rows, count * rows), count * rows)
        for part in range(3):
            grad = dot(x_t[at, :], d_ref[part], 1, 1).astype(BF16)
            for block in range(count):
                to = ((base + block) ^ rel) % count
                piece = grad[block * rows : (block + 1) * rows, :]
                parts[part][to] = piece
        at = pl.ds(pl.multiple_of(base * step, count * step), count * step)
        grad = dot(c_ref[at, :], grad_branch[...], 1, 0)
        for block in range(count):
            to = ((base + block) ^ rel) % count
            piece = grad[block * step : (block + 1) * step, :]
            piece = jnp.concatenate([piece[:, :width], piece[:, width:]], axis=0)
            parts[3][to] = piece.astype(BF16)
    ones = jnp.ones((8, xq.shape[0]), BF16)
    qv_row[:, 0:width] = dot(ones, d_ref[0], 1, 1)
    qv_row[:, width : 2 * width] = dot(ones, d_ref[2], 1, 1)


def gelu_parts(hidden, scale):
    area = 0.5 + 0.5 * lax.erf(hidden * 0.7071067811865476)
    bell = jnp.exp(-0.5 * hidden * hidden)
    active = hidden * area
    slope = area + hidden * bell * 0.3989422804014327
    bent = jnp.tanh(active * (1.0 / scale))
    return (scale * bent).astype(BF16), ((1.0 - bent * bent) * slope).astype(BF16), active


def fold(value, op):
    rows, lanes = value.shape
    return op(value.reshape(rows // 8, 8, lanes), axis=0)


def middle_body(
    clips,
    c_own,
    c_other,
    merge_own,
    merge_other,
    inputs,
    up_own,
    up_other,
    down_own,
    down_other,
    pack_own,
    pack_other,
    vectors,
    cotangent,
    unit_out,
    inverse_out,
    normed_q,
    active_own,
    active_other,
    factor_own,
    factor_other,
    output,
    grad_sum,
    grad_feed,
    sums,
    work,
    hidden_ref,
    second_ref,
    tops,
    sum_ref,
):
    total = inputs.shape[0]
    work[...] = dot(c_own[...], merge_own[...], 0, 0) + dot(c_other[...], merge_other[...], 0, 0)
    tops[...] = jnp.zeros_like(tops)
    sum_ref[...] = jnp.zeros_like(sum_ref)
    clip_first, clip_second = clips[1], clips[2]

    def first_norm(index, carry):
        at = pl.ds(pl.multiple_of(index * TILE, TILE), TILE)
        rows = inputs[at, :].astype(F32)
        value = rows + work[at, :] + vectors[0:1, :]
        mean = jnp.mean(value, axis=-1, keepdims=True)
        centred = value - mean
        inverse = lax.rsqrt(jnp.mean(centred * centred, axis=-1, keepdims=True) + EPSILON)
        unit = centred * inverse
        normed = unit * vectors[2:3, :] + vectors[4:5, :]
        unit_out[at, :] = unit
        inverse_out[at, :] = jnp.broadcast_to(inverse, (TILE, 128))
        normed_q[at, :] = clip_tile(normed, clip_first)
        tops[0] = jnp.maximum(tops[0], fold(jnp.abs(rows), jnp.max))
        tops[1] = jnp.maximum(tops[1], fold(jnp.abs(normed), jnp.max))
        work[at, :] = normed
        return carry

    lax.fori_loop(0, total // TILE, first_norm, 0)
    span = hidden_ref.shape[1]
    for weight, pack, active_ref, factor_ref in (
        (up_own, pack_own, active_own, factor_own),
        (up_other, pack_other, active_other, factor_other),
    ):

        def gelu_chunk(source, index):
            cols = pl.ds(pl.multiple_of(index * span, span), span)
            bias = pack[0:1, cols]
            top = tops[2, :, 0:span]
            for row in range(total // GELU_TILE):
                at = slice(row * GELU_TILE, (row + 1) * GELU_TILE)
                clipped, factor, active = gelu_parts(source[at, :] + bias, clip_second)
                active_ref[at, cols] = clipped
                factor_ref[at, cols] = factor
                top = jnp.maximum(top, fold(jnp.abs(active), jnp.max))
            tops[2, :, 0:span] = top

        def multiply(target, index):
            cols = pl.ds(pl.multiple_of(index * span, span), span)
            target[...] = dot(normed_q[...], weight[:, cols], 1, 0)

        chunks = weight.shape[1] // span
        multiply(hidden_ref, 0)

        def pair(index, carry):
            multiply(second_ref, 2 * index + 1)
            gelu_chunk(hidden_ref, 2 * index)
            multiply(hidden_ref, jnp.minimum(2 * index + 2, chunks - 1))
            gelu_chunk(second_ref, 2 * index + 1)
            return carry

        lax.fori_loop(0, chunks // 2, pair, 0)
    work[...] += dot(active_own[...], down_own[...], 1, 0) + dot(
        active_other[...], down_other[...], 1, 0
    )

    def second_norm(index, carry):
        at = pl.ds(pl.multiple_of(index * TILE, TILE), TILE)
        value = work[at, :] + vectors[1:2, :]
        mean = jnp.mean(value, axis=-1, keepdims=True)
        centred = value - mean
        inverse = lax.rsqrt(jnp.mean(centred * centred, axis=-1, keepdims=True) + EPSILON)
        unit = centred * inverse
        output[at, :] = (unit * vectors[3:4, :] + vectors[5:6, :]).astype(BF16)
        upstream = cotangent[at, :].astype(F32)
        scaled = upstream * vectors[3:4, :]
        grad = inverse * (
            scaled
            - jnp.mean(scaled, axis=-1, keepdims=True)
            - unit * jnp.mean(scaled * unit, axis=-1, keepdims=True)
        )
        grad_sum[at, :] = grad
        grad_feed[at, :] = grad.astype(BF16)
        sum_ref[0] += fold(upstream * unit, jnp.sum)
        sum_ref[1] += fold(upstream, jnp.sum)
        sum_ref[2] += fold(grad, jnp.sum)
        return carry

    lax.fori_loop(0, total // TILE, second_norm, 0)
    for row in range(3):
        sums[row : row + 1, :] = jnp.sum(sum_ref[row], axis=0, keepdims=True)
    for row in range(3):
        top = jnp.max(jnp.max(tops[row], axis=0, keepdims=True), axis=1, keepdims=True)
        sums[3 + row : 4 + row, :] = jnp.broadcast_to(top, (1, sums.shape[1]))
    sums[6:8, :] = jnp.zeros((2, sums.shape[1]), F32)


def half_base(rel, half, blocks):
    return (half ^ (rel // (blocks // 2))) * (blocks // 2)


def down_grad_body(which, half, ids, active, grad_feed, chunk):
    rel = ids[which]
    count = chunk.shape[0]
    rows = active.shape[1] // (2 * count)
    base = half_base(rel, half, 2 * count)
    per = count // 2
    for tile in range(2):
        first = base + tile * per
        cols = pl.ds(pl.multiple_of(first * rows, per * rows), per * rows)
        grad = dot(active[:, cols], grad_feed[...], 0, 0)
        for block in range(per):
            piece = grad[block * rows : (block + 1) * rows, :].astype(BF16)
            to = ((first + block) ^ rel) % count
            chunk[to, 0:rows, :] = piece[:, :LANES]
            chunk[to, rows : 2 * rows, :] = piece[:, LANES:]


def up_grad_body(
    which, ids, grad_feed, down, up, factor, normed_q, before, high, low, bias_row, grad_normed, g_ref
):
    rel = ids[which]
    count = high.shape[0]
    span = 512

    def columns(index, carry):
        cols = pl.ds(pl.multiple_of(index * span, span), span)
        grad = dot(grad_feed[...], down[cols, :], 1, 1) * factor[:, cols].astype(F32)
        grad = grad.astype(BF16)
        g_ref[:, cols] = grad
        bias_row[0:1, cols] = jnp.sum(grad.astype(F32), axis=0, keepdims=True)
        return carry

    lax.fori_loop(0, g_ref.shape[1] // span, columns, 0, unroll=True)
    rows = normed_q.shape[1] // (2 * count)
    for half, chunk in ((1, high), (0, low)):
        base = half_base(rel, half, 2 * count)
        cols = pl.ds(pl.multiple_of(base * rows, count * rows), count * rows)
        grad = dot(normed_q[:, cols], g_ref[...], 0, 0)
        for block in range(count):
            to = ((base + block) ^ rel) % count
            for part in range(grad.shape[1] // LANES):
                piece = grad[block * rows : (block + 1) * rows, part * LANES : (part + 1) * LANES]
                chunk[to, part * rows : (part + 1) * rows, :] = piece.astype(BF16)
    result = dot(g_ref[...], up[...], 1, 1)
    if before is not None:
        result = result + before[...]
    grad_normed[...] = result


def up_grad_first_body(which, ids, grad_feed, down, up, factor, normed_q, *outs):
    up_grad_body(which, ids, grad_feed, down, up, factor, normed_q, None, *outs)


def first_norm_back_body(
    clips,
    grad_normed,
    grad_sum,
    unit_ref,
    inverse_ref,
    vectors,
    sums,
    bias_other,
    bias_own,
    grad_first,
    grad_branch,
    pack_other,
    pack_own,
    sum_ref,
):
    clip_first = clips[1]
    sum_ref[...] = jnp.zeros_like(sum_ref)

    def rows(index, carry):
        at = pl.ds(pl.multiple_of(index * TILE, TILE), TILE)
        unit = unit_ref[at, :]
        bent = jnp.tanh((unit * vectors[2:3, :] + vectors[4:5, :]) * (1.0 / clip_first))
        grad = grad_normed[at, :] * (1.0 - bent * bent) + grad_sum[at, :]
        scaled = grad * vectors[2:3, :]
        back = inverse_ref[at, 0:1] * (
            scaled
            - jnp.mean(scaled, axis=-1, keepdims=True)
            - unit * jnp.mean(scaled * unit, axis=-1, keepdims=True)
        )
        grad_first[at, :] = back
        grad_branch[at, :] = back.astype(BF16)
        sum_ref[0] += fold(grad * unit, jnp.sum)
        sum_ref[1] += fold(grad, jnp.sum)
        sum_ref[2] += fold(back, jnp.sum)
        return carry

    lax.fori_loop(0, unit_ref.shape[0] // TILE, rows, 0)
    width = unit_ref.shape[1]
    for pack, bias in ((pack_other, bias_other), (pack_own, bias_own)):
        pack[...] = jnp.zeros_like(pack)
        for row, source in ((0, 0), (2, 1), (4, 2)):
            pack[row : row + 1, :] = jnp.sum(sum_ref[source], axis=0, keepdims=True)
        pack[1:2, :] = sums[0:1, :]
        pack[3:4, :] = sums[1:2, :]
        pack[5:6, :] = sums[2:3, :]
        pack[6:7, :] = bias[0:1, 0:width]
        pack[7:8, :] = bias[0:1, width : 2 * width]
        pack[12:15, :] = sums[3:6, :]


def input_grad_body(clips, inputs, grad_first, w_own, w_other, d_own, d_other, out):
    terms = []
    for d_ref, weight in ((d_own, w_own), (d_other, w_other)):
        for part in range(3):
            terms.append(dot(d_ref[part], weight[part], 0, 1))
    bent = jnp.tanh(inputs[...].astype(F32) * (1.0 / clips[0]))
    out[...] = sum(terms[1:], terms[0]) * (1.0 - bent * bent) + grad_first[...]


def slope_of(weight, scale):
    bent = jnp.tanh(weight.astype(F32) * (1.0 / scale))
    return 1.0 - bent * bent


def block_value(rel, low, high, at):
    half = low.shape[0]
    at = at ^ rel
    first = low[jnp.minimum(at, half - 1)].astype(F32)
    return jnp.where(at < half, first, high[jnp.maximum(at - half, 0)].astype(F32))


def down_final_body(per, ids, own, other, low, high, weight, out):
    rows = weight.shape[0] // per
    slope = slope_of(weight[...], scale_row(own, other, 2, weight.shape[1]))
    for index in range(per):
        value = block_value(ids[0], low, high, pl.program_id(0) * per + index)
        at = slice(index * rows, (index + 1) * rows)
        out[at, :LANES] = value[:rows] * slope[at, :LANES]
        out[at, LANES:] = value[rows:] * slope[at, LANES:]


def up_final_body(per, ids, own, other, low, high, weight, out):
    rows = weight.shape[0] // per
    slope = slope_of(weight[...], scale_row(own, other, 1, weight.shape[1]))
    for index in range(per):
        value = block_value(ids[0], low, high, pl.program_id(0) * per + index)
        at = slice(index * rows, (index + 1) * rows)
        for part in range(weight.shape[1] // LANES):
            cols = slice(part * LANES, (part + 1) * LANES)
            out[at, cols] = value[part * rows : (part + 1) * rows] * slope[at, cols]


def rest_final_body(half, per, ids, own, other, chunk, p_own, p_other, project, merge, *refs):
    project_out, merge_out = refs[-2:]
    rows, step = project.shape[1] // per, merge.shape[0] // per
    count = chunk.shape[0]
    first = half_base(ids[0], half, 2 * count) + pl.program_id(0) * per
    values = []
    for index in range(per):
        values.append(chunk[((first + index) ^ ids[0]) % count].astype(F32))
    for part in range(3):
        slope = slope_of(project[part], scale_row(p_own, p_other, part, LANES))
        for index in range(per):
            at = slice(index * rows, (index + 1) * rows)
            project_out[part, at, :] = values[index][part * rows : (part + 1) * rows] * slope[at]
    slope = slope_of(merge[...], scale_row(own, other, 0, merge.shape[1]))
    for part in range(2):
        across = slice(part * LANES, (part + 1) * LANES)
        piece = [v[3 * rows + part * step : 3 * rows + (part + 1) * step] for v in values]
        merge_out[:, across] = jnp.concatenate(piece, axis=0) * slope[:, across]


class Exchange:
    def __init__(self, size, first):
        self.bits = size.bit_length() - 1
        assert 1 << self.bits == size and self.bits >= 4
        self.size = size
        self.orders = [list(order) + list(range(4, self.bits)) for order in first]
        self.blocks = 16

    def relative(self, position, core):
        total = 0
        for stage in range(4):
            bit = (position >> self.orders[core][stage]) & 1
            total = total + (bit << (3 - stage))
        return total

    def swap(self, value, stage):
        pairs = []
        for index in range(self.size):
            for core in range(2):
                to = index ^ (1 << self.orders[core][stage])
                pairs.append((2 * index + core, 2 * to + core))
        return lax.ppermute(value, ("dp", "tensor"), pairs)

    def core_swap(self, value):
        return lax.ppermute(value, "tensor", [(0, 1), (1, 0)])


class Task:
    def __init__(self, body, deps):
        self.body, self.deps, self.sends = body, list(deps), []


class Plan:
    def __init__(self):
        self.tasks = {}
        self.values = {}
        self.source = {}

    def given(self, name, value):
        self.values[name] = value
        return name

    def core(self, name, body, deps):
        self.tasks[name] = Task(body, deps)
        return name

    def send(self, name, source, body):
        self.tasks[source].sends.append((name, body))
        self.source[name] = source
        return name

    def run(self):
        values, last = dict(self.values), None

        def take(name):
            nonlocal last
            if name in values:
                return
            if name in self.source:
                take(self.source[name])
                return
            task = self.tasks[name]
            for dep in task.deps:
                take(dep)
            inputs = [values[dep] for dep in task.deps]
            if last is not None:
                inputs, last = lax.optimization_barrier((inputs, last))
            with jax.named_scope(name.replace(".", "_")):
                result = task.body(*inputs)
            values[name] = result
            last = jax.tree.leaves(result)[0]
            for sent, body in task.sends:
                with jax.named_scope(sent.replace(".", "_")):
                    values[sent] = body(result)

        for name in ORDER:
            if name in self.tasks:
                take(name)
            elif name[1:] in self.source:
                take(name[1:])
                values[name[1:]], last = lax.optimization_barrier((values[name[1:]], last))
        for name in self.tasks:
            take(name)
        return values

    def swap(self, name, source, way, stage, pick=lambda value: value):
        return self.send(name, source, lambda value: way.swap(pick(value), stage))

    def reduce(self, name, way, mine, theirs, pick):
        def swapped(index):
            return lambda v: [way.core_swap(value) for value in pick(v, index)]

        def whole(values):
            return values[0] if len(values) == 1 else jnp.concatenate(values, axis=1)

        high = self.send(name + ".high", theirs[0], swapped(0))
        low = self.send(name + ".low", theirs[1], swapped(1))
        value = self.core(
            f"{name}.add0",
            lambda mine, high: total([whole(pick(mine, 0)), whole(high)]),
            [mine[0], high],
        )
        got = self.swap(f"{name}.in0", value, way, 0)

        def second(mine, low, got):
            return split_in_two([whole(pick(mine, 1)), whole(low), got])

        def more(kept, got):
            return split_in_two([kept[0], got])

        value = self.core(f"{name}.add1", second, [mine[1], low, got])
        for stage in (1, 2, 3):
            got = self.swap(f"{name}.in{stage}", value, way, stage, second_of)
            if stage < 3:
                value = self.core(f"{name}.add{stage + 1}", more, [value, got])
        value = self.core(f"{name}.sum", lambda kept, got: total([kept[0], got]), [value, got])
        for stage in range(4, way.bits):
            sent = self.swap(f"{name}.in{stage}", value, way, stage)
            value = self.core(f"{name}.sum{stage}", lambda a, b: total([a, b]), [value, sent])
        for stage in reversed(range(4)):
            sent = self.swap(f"{name}.out{stage}", value, way, stage)
            if stage > 0:
                value = self.core(
                    f"{name}.join{stage}",
                    lambda a, b: jnp.concatenate([a, b], axis=0),
                    [value, sent],
                )
        return [value, sent]


def total(values):
    out = values[0].astype(F32)
    for value in values[1:]:
        out = out + value.astype(F32)
    return out.astype(BF16)


def split_in_two(values):
    half = values[0].shape[0] // 2
    return total([value[:half] for value in values]), total([value[half:] for value in values])


def second_of(value):
    return value[1]


def local(
    inputs,
    row_lengths,
    project_weight,
    merge_weight,
    up_weight,
    down_weight,
    query_value_bias,
    merge_bias,
    up_bias,
    down_bias,
    norm_gains,
    norm_shifts,
    clip_scales,
    cotangent,
):
    size = lax.axis_size("dp")
    exchange = Exchange(size, ((0, 1, 2, 3), (1, 0, 2, 3)))
    same_way = Exchange(size, ((0, 1, 2, 3), (0, 1, 2, 3)))
    blocks = exchange.blocks
    member = lax.axis_index("tensor")
    place = lax.axis_index("dp")
    rel0, rel1 = exchange.relative(place, 0), exchange.relative(place, 1)
    own_rel = jnp.where(member == 0, rel0, rel1)
    other_rel = jnp.where(member == 0, rel1, rel0)
    ids = jnp.stack([own_rel, other_rel, member * (LONG // SHORT)]).astype(jnp.int32)
    total, width = inputs.shape
    hidden = up_weight.shape[1]
    project = jnp.transpose(project_weight, (1, 0, 2))

    steps = 4
    small_grid = pltpu.CompilerParams(vmem_limit_bytes=12 << 20)
    project_block = pl.BlockSpec((3, width // steps, LANES), lambda i: (0, i, 0))
    rest_blocks = [
        pl.BlockSpec((LANES // steps, width), lambda i: (i, 0)),
        pl.BlockSpec((width // steps, hidden), lambda i: (i, 0)),
        pl.BlockSpec((hidden // steps, width), lambda i: (i, 0)),
    ]
    project_pack_spec = pl.BlockSpec((16, LANES), lambda i: (0, 0))
    pack_spec = pl.BlockSpec((16, hidden), lambda i: (0, 0))
    rest_weights = (merge_weight, up_weight, down_weight)

    def project_peaks():
        return pl.pallas_call(
            project_peaks_body,
            grid=(steps,),
            in_specs=[project_block, pl.BlockSpec((2, LANES), lambda i: (0, 0))],
            out_specs=project_pack_spec,
            out_shape=shaped((16, LANES), F32),
            compiler_params=small_grid,
        )(project, query_value_bias)

    def rest_peaks(weights):
        return pl.pallas_call(
            rest_peaks_body,
            grid=(steps,),
            in_specs=rest_blocks + [pl.BlockSpec((1, hidden), lambda i: (0, 0))],
            out_specs=pack_spec,
            out_shape=shaped((16, hidden), F32),
            compiler_params=small_grid,
        )(*weights, up_bias[None])

    def clip_project(own, other):
        return pl.pallas_call(
            clip_project_body,
            grid=(steps,),
            in_specs=[project_pack_spec, project_pack_spec, project_block],
            out_specs=project_block,
            out_shape=shaped(project.shape, BF16),
            compiler_params=small_grid,
        )(own, other, project)

    def clip_rest(own, other):
        return pl.pallas_call(
            clip_rest_body,
            grid=(steps,),
            in_specs=[pack_spec, pack_spec] + rest_blocks,
            out_specs=rest_blocks,
            out_shape=[shaped(a.shape, BF16) for a in rest_weights],
            compiler_params=small_grid,
        )(own, other, *rest_weights)

    project_own_pack = project_peaks()
    project_other_pack = exchange.core_swap(project_own_pack)
    project_own = clip_project(project_own_pack, project_other_pack)
    project_other = exchange.core_swap(project_own)
    tied, project_own = lax.optimization_barrier((rest_weights, project_own))
    own_pack = rest_peaks(tied)
    other_pack = exchange.core_swap(own_pack)
    other_pack, project_other = lax.optimization_barrier((other_pack, project_other))
    merge_own, up_own, down_own = clip_rest(own_pack, other_pack)
    merge_other = exchange.core_swap(merge_own)
    up_other = exchange.core_swap(up_own)
    down_other = exchange.core_swap(down_own)
    project_own, merge_own = lax.optimization_barrier((project_own, merge_own))

    head_shape = shaped((LANES, total), BF16)
    heads_out = [head_shape] * 4 + [shaped((8, total), F32)]
    mask_scratch = pltpu.VMEM((LONG, LONG), F32)
    xq, *own_heads = call(
        forward_first_body,
        [shaped((total, width), BF16)] + heads_out,
        (ids, row_lengths, clip_scales, inputs, project_own, project_own_pack),
        [mask_scratch],
        in_specs=[SMEM] * 3 + [VMEM] * 3,
        out_specs=[VMEM] * 6,
        limit=16 << 20,
    )
    other_heads = call(
        forward_second_body,
        heads_out,
        (ids, row_lengths, xq, project_other, project_other_pack),
        [mask_scratch],
        in_specs=[SMEM] * 2 + [VMEM] * 3,
        out_specs=[VMEM] * 5,
        limit=16 << 20,
    )

    vectors = jnp.concatenate([merge_bias[None], down_bias[None], norm_gains, norm_shifts], axis=0)
    rows_f32 = shaped((total, width), F32)
    rows_bf16 = shaped((total, width), BF16)
    wide = shaped((total, hidden), BF16)
    (
        unit,
        inverse,
        normed_q,
        active_own,
        active_other,
        factor_own,
        factor_other,
        output,
        grad_sum,
        grad_feed,
        sums,
    ) = call(
        middle_body,
        [
            rows_f32,
            shaped((total, 128), F32),
            rows_bf16,
            wide,
            wide,
            wide,
            wide,
            rows_bf16,
            rows_f32,
            rows_bf16,
            shaped((8, width), F32),
        ],
        (
            clip_scales,
            own_heads[3],
            other_heads[3],
            merge_own,
            merge_other,
            inputs,
            up_own,
            up_other,
            down_own,
            down_other,
            own_pack,
            other_pack,
            vectors,
            cotangent,
        ),
        [
            pltpu.VMEM((total, width), F32),
            pltpu.VMEM((total, 256), F32),
            pltpu.VMEM((total, 256), F32),
            pltpu.VMEM((3, 8, width), F32),
            pltpu.VMEM((3, 8, width), F32),
        ],
        in_specs=[SMEM] + [VMEM] * 13,
        out_specs=[VMEM] * 11,
        limit=32 << 20,
    )

    plan = Plan()
    chunk = shaped((blocks // 2, 2 * hidden // blocks, LANES), BF16)

    def down_half(which, half, active, grad):
        return call(
            partial(down_grad_body, which, half),
            chunk,
            (ids, active, grad),
            in_specs=[SMEM] + [VMEM] * 2,
            out_specs=VMEM,
            limit=9 << 20,
        )

    feed = plan.given("feed", grad_feed)
    down_tasks = {}
    for half, word in ((1, "high"), (0, "low")):
        for which, active in ((1, active_other), (0, active_own)):
            down_tasks[which, half] = plan.core(
                ("down.mine", "down.theirs")[which] + word,
                lambda grad, which=which, half=half, active=active: down_half(
                    which, half, active, grad
                ),
                [feed],
            )

    def take(index):
        return lambda values: values[index]

    def part(values, index):
        return values[index]

    def one(values, index):
        return [values[index]]

    down_out = plan.reduce(
        "down",
        exchange,
        (down_tasks[0, 1], down_tasks[0, 0]),
        (down_tasks[1, 1], down_tasks[1, 0]),
        lambda value, index: [value],
    )

    def up_half(body, which, grad, down, up, factor, *before):
        return call(
            partial(body, which),
            [chunk, chunk, shaped((1, hidden), F32), rows_f32],
            (ids, grad, down, up, factor, normed_q) + before,
            [pltpu.VMEM((total, hidden), BF16)],
            in_specs=[SMEM] + [VMEM] * (5 + len(before)),
            out_specs=[VMEM] * 4,
            limit=20 << 20,
        )

    up_theirs = plan.core(
        "up.theirs",
        lambda grad: up_half(
            up_grad_first_body, 1, grad, down_other, up_other, factor_other
        ),
        [feed],
    )
    up_mine = plan.core(
        "up.mine",
        lambda grad, before: up_half(
            up_grad_body, 0, grad, down_own, up_own, factor_own, before[3]
        ),
        [feed, up_theirs],
    )
    up_out = plan.reduce("up", exchange, (up_mine, up_mine), (up_theirs, up_theirs), one)

    small = shaped((16, width), F32)

    def norm_back(theirs, mine):
        ins = (clip_scales, mine[3], grad_sum, unit, inverse, vectors, sums, theirs[2], mine[2])
        return call(
            first_norm_back_body,
            [rows_f32, rows_bf16, small, small],
            ins,
            [pltpu.VMEM((3, 8, width), F32)],
            in_specs=[SMEM] + [VMEM] * 8,
            out_specs=[VMEM] * 4,
        )

    first_back = plan.core("norm", norm_back, [up_theirs, up_mine])

    def heads_back(which, back, heads, merge_q):
        count = (1, 4)[which]
        parts = [shaped((chunk.shape[0], chunk.shape[1] // count, LANES), BF16)] * count
        *outs, grads, row = call(
            partial(backward_heads_body, which),
            parts + parts + [shaped((3, LANES, total), BF16), shaped((8, 2 * LANES), F32)],
            (ids, row_lengths, xq, back[1]) + tuple(heads) + (merge_q,),
            [
                mask_scratch,
                pltpu.VMEM((LANES, total), BF16),
                pltpu.VMEM((width, total), BF16),
            ],
            in_specs=[SMEM] * 2 + [VMEM] * 8,
            out_specs=[VMEM] * (2 * count + 2),
            limit=18 << 20,
        )
        return outs[:count], outs[count:], grads, row

    heads_theirs = plan.core(
        "heads.theirs", lambda back: heads_back(1, back, other_heads, merge_other), [first_back]
    )
    heads_mine = plan.core(
        "heads.mine", lambda back: heads_back(0, back, own_heads, merge_own), [first_back]
    )
    rest_out = plan.reduce(
        "rest", exchange, (heads_mine, heads_mine), (heads_theirs, heads_theirs), part
    )

    def input_part(back, theirs, mine):
        return call(
            input_grad_body,
            rows_f32,
            (clip_scales, inputs, back[0], project_own, project_other, mine[2], theirs[2]),
            in_specs=[SMEM] + [VMEM] * 6,
            out_specs=VMEM,
            limit=16 << 20,
        )

    input_task = plan.core("input", input_part, [first_back, heads_theirs, heads_mine])

    def joined(sums_part, row):
        return jnp.concatenate([sums_part[:8], row[0:1], sums_part[12:15]], axis=0)

    small_row = lax.broadcasted_iota(jnp.int32, (12, width), 0)

    def merge_small(a, b):
        return jnp.where(small_row < 9, a + b, jnp.maximum(a, b))

    theirs_small = plan.core(
        "small.theirs", lambda back, heads: joined(back[2], heads[3]), [first_back, heads_theirs]
    )
    small_got = plan.send("small.got", theirs_small, exchange.core_swap)
    small_value = plan.core(
        "small.mine",
        lambda got, back, heads: merge_small(joined(back[3], heads[3]), got),
        [small_got, first_back, heads_mine],
    )
    for stage in range(exchange.bits):
        swap = partial(same_way.swap, stage=stage)
        small_in = plan.send(f"small.in{stage}", small_value, swap)
        small_value = plan.core(f"small.sum{stage}", merge_small, [small_value, small_in])

    final_steps = 4
    per = blocks // final_steps

    def final(body, parts, weights, specs):
        part_specs = [pl.BlockSpec(part.shape, lambda i, s: (0, 0, 0)) for part in parts]
        pack = pl.BlockSpec((16, hidden), lambda i, s: (0, 0))
        ins = (ids, own_pack, other_pack) + tuple(parts) + weights
        return pl.pallas_call(
            partial(body, per),
            grid_spec=pltpu.PrefetchScalarGridSpec(
                num_scalar_prefetch=1,
                grid=(final_steps,),
                in_specs=[pack, pack]
                + part_specs
                + specs,
                out_specs=specs,
            ),
            out_shape=[shaped(weight.shape, F32) for weight in weights],
            compiler_params=pltpu.CompilerParams(vmem_limit_bytes=10 << 20),
            cost_estimate=pl.CostEstimate(flops=1, bytes_accessed=1, transcendentals=0),
        )(*ins)

    down_spec = pl.BlockSpec((hidden // final_steps, width), lambda i, s: (i, 0))
    plan.core(
        "down.final",
        lambda *parts: final(down_final_body, parts, (down_weight,), [down_spec])[0],
        down_out,
    )
    up_spec = pl.BlockSpec((width // final_steps, hidden), lambda i, s: (i, 0))
    plan.core(
        "up.final",
        lambda *parts: final(up_final_body, parts, (up_weight,), [up_spec])[0],
        up_out,
    )

    def rest_final(half, chunk, *before):
        before = tuple(before[0]) if before else ()

        def place(i, s):
            return (half ^ (s[0] // (blocks // 2))) * (final_steps // 2) + i

        specs = [
            pl.BlockSpec((3, width // final_steps, LANES), lambda i, s: (0, place(i, s), 0)),
            pl.BlockSpec((LANES // final_steps, width), lambda i, s: (place(i, s), 0)),
        ]
        weights = (project, merge_weight)
        packs = (project_own_pack, project_other_pack)
        ins = (ids, own_pack, other_pack, chunk) + packs + weights
        pack = pl.BlockSpec((16, hidden), lambda i, s: (0, 0))
        narrow = pl.BlockSpec((16, LANES), lambda i, s: (0, 0))
        return pl.pallas_call(
            partial(rest_final_body, half, per),
            grid_spec=pltpu.PrefetchScalarGridSpec(
                num_scalar_prefetch=1,
                grid=(final_steps // 2,),
                in_specs=[pack, pack, pl.BlockSpec(chunk.shape, lambda i, s: (0, 0, 0))]
                + [narrow, narrow]
                + specs
                + [pl.BlockSpec(memory_space=pl.ANY)] * len(before),
                out_specs=specs,
            ),
            out_shape=[shaped(weight.shape, F32) for weight in weights],
            input_output_aliases={len(ins) + at: at for at in range(len(before))},
            compiler_params=pltpu.CompilerParams(vmem_limit_bytes=10 << 20),
            cost_estimate=pl.CostEstimate(flops=1, bytes_accessed=1, transcendentals=0),
        )(*ins, *before)

    plan.core("rest.half", partial(rest_final, 0), rest_out[:1])
    plan.core("rest.final", partial(rest_final, 1), [rest_out[1], "rest.half"])
    values = plan.run()
    small_all = values[small_value]
    project_grad, merge_grad = values["rest.final"]
    peaks = small_all[9:12, 0]
    return (
        output,
        values[input_task],
        jnp.transpose(project_grad, (1, 0, 2)),
        merge_grad,
        values["up.final"],
        values["down.final"],
        small_all[8].reshape(2, LANES),
        small_all[4],
        small_all[6:8].reshape(hidden),
        small_all[5],
        small_all[0:2],
        small_all[2:4],
        DECAY * clip_scales + (1.0 - DECAY) * peaks,
    )


def solution(mesh):
    return jax.shard_map(
        local,
        mesh=mesh,
        in_specs=(
            P(("dp", "tensor"), None),
            P("dp"),
            P(None, None, "tensor"),
            P("tensor", None),
            P(None, "tensor"),
            P("tensor", None),
            P(None, "tensor"),
            P(),
            P("tensor"),
            P(),
            P(),
            P(),
            P(),
            P(("dp", "tensor"), None),
        ),
        out_specs=(
            P(("dp", "tensor"), None),
            P(("dp", "tensor"), None),
            P(None, None, "tensor"),
            P("tensor", None),
            P(None, "tensor"),
            P("tensor", None),
            P(None, "tensor"),
            P(),
            P("tensor"),
            P(),
            P(),
            P(),
            P(),
        ),
        check_vma=False,
    )
```

```python
from functools import partial

import jax
import jax.numpy as jnp
from jax import lax
from jax.experimental import pallas as pl
from jax.experimental.pallas import tpu as pltpu
from jax.sharding import PartitionSpec as P

HEAD = 64
LONG = 512
SHORT = 128
EPSILON = 1e-12
DECAY = 0.9
F32 = jnp.float32
BF16 = jnp.bfloat16
VMEM = pl.BlockSpec(memory_space=pltpu.VMEM)
SMEM = pl.BlockSpec(memory_space=pltpu.SMEM)
ORDER = (
    "down.theirshigh",
    "down.minehigh",
    "down.theirslow",
    "down.add0",
    "down.minelow",
    "up.theirs",
    "up.mine",
    "down.add1",
    "up.add0",
    "norm",
    "heads.theirs",
    "heads.mine",
    "down.add2",
    "up.add1",
    "rest.add0",
    "input",
    "down.add3",
    "small.theirs",
    "down.sum",
    "up.add2",
    "rest.add1",
    "small.mine",
    "down.join3",
    "up.add3",
    "rest.add2",
    "down.join2",
    "up.sum",
    "rest.add3",
    "small.sum0",
    "down.join1",
    "up.join3",
    "small.sum1",
    "rest.sum",
    "small.sum2",
    "up.join2",
    "rest.join3",
    "down.final",
    "rest.join2",
    "up.join1",
    "small.sum3",
    "rest.join1",
    "up.final",
    "rest.final",
)
COST = 1
LANES = 384
TILE = 128
GELU_TILE = 32


def dot(a, b, ca, cb):
    return lax.dot_general(a, b, (((ca,), (cb,)), ((), ())), preferred_element_type=F32)


def shaped(shape, dtype):
    return jax.ShapeDtypeStruct(shape, dtype)


def call(
    body, out_shape, ins, scratch=(), in_specs=None, out_specs=None, limit=None
):
    nbytes = sum(a.size * a.dtype.itemsize for a in ins)
    nbytes += sum(o.size * o.dtype.itemsize for o in jax.tree.leaves(out_shape))
    params = dict(
        out_shape=out_shape,
        compiler_params=pltpu.CompilerParams(vmem_limit_bytes=limit or (nbytes + (6 << 20))),
        cost_estimate=pl.CostEstimate(flops=1, bytes_accessed=COST, transcendentals=0),
    )
    return pl.pallas_call(
        body, in_specs=in_specs, out_specs=out_specs, scratch_shapes=list(scratch), **params
    )(*ins)


def peak(value):
    top = jnp.max(jnp.abs(value.astype(F32)), axis=0, keepdims=True)
    return jnp.max(top, axis=1, keepdims=True)


def raise_peaks(pack, tiles):
    for row, tile in enumerate(tiles):
        at = slice(8 + row, 9 + row)
        pack[at, :] = jnp.maximum(pack[at, :], peak(tile))


def project_peaks_body(project, qv_bias, pack):
    @pl.when(pl.program_id(0) == 0)
    def _():
        pack[...] = jnp.zeros_like(pack)
        pack[0:2, :] = qv_bias[...]

    raise_peaks(pack, [project[0], project[1], project[2]])


def rest_peaks_body(merge, up, down, up_bias, pack):
    @pl.when(pl.program_id(0) == 0)
    def _():
        pack[...] = jnp.zeros_like(pack)
        pack[0:1, :] = up_bias[...]

    raise_peaks(pack, [merge[...], up[...], down[...]])


def scale_row(own, other, row, width):
    at = slice(8 + row, 9 + row)
    return 0.5 * jnp.maximum(own[at, 0:width], other[at, 0:width])


def clip_tile(value, scale):
    return (scale * jnp.tanh(value.astype(F32) * (1.0 / scale))).astype(BF16)


def clip_project_body(own, other, project, out):
    for part in range(3):
        out[part] = clip_tile(project[part], scale_row(own, other, part, LANES))


def clip_rest_body(own, other, merge, up, down, merge_q, up_q, down_q):
    for row, (src, dst) in enumerate(((merge, merge_q), (up, up_q), (down, down_q))):
        dst[...] = clip_tile(src[...], scale_row(own, other, row, src.shape[1]))


def key_bias(lengths, first):
    key = lax.broadcasted_iota(jnp.int32, (LONG, 1), 0)
    query = lax.broadcasted_iota(jnp.int32, (1, LONG), 1)
    single = lengths[first] > SHORT
    limit = jnp.full((LONG, 1), lengths[first], jnp.int32)
    for slot in range(1, LONG // SHORT):
        own = jnp.where(single, lengths[first], slot * SHORT + lengths[first + slot])
        limit = jnp.where(key >= slot * SHORT, own, limit)
    key_row = jnp.where(single, 0, key // SHORT)
    query_row = jnp.where(single, 0, query // SHORT)
    key_row = jnp.where(key < limit, key_row, -1)
    return jnp.where(key_row == query_row, 0.0, -1e30).astype(F32)


def qkv_into(xq, weight, bias_pack, q_ref, k_ref, v_ref):
    for part, ref in enumerate((q_ref, k_ref, v_ref)):
        value = dot(xq, weight[part], 1, 0)
        if part == 0:
            value = value + bias_pack[0:1, :]
        if part == 2:
            value = value + bias_pack[1:2, :]
        value = value.astype(BF16)
        if part == 0:
            value = value * jnp.asarray(0.125, BF16)
        ref[...] = value.T


def attend(lengths, first, q_ref, k_ref, v_ref, c_ref, lse_ref, bias_ref):
    bias_ref[...] = key_bias(lengths, first)

    def head(index, carry):
        at = pl.ds(pl.multiple_of(index * HEAD, HEAD), HEAD)
        scores = dot(k_ref[at, :], q_ref[at, :], 0, 0) + bias_ref[...]
        top = jnp.max(scores, axis=0, keepdims=True)
        prob = jnp.exp(scores - top)
        total = jnp.sum(prob, axis=0, keepdims=True)
        mixed = dot(v_ref[at, :], prob.astype(BF16), 1, 0)
        c_ref[at, :] = (mixed * (1.0 / total)).astype(BF16)
        lse_ref[pl.ds(index, 1), :] = top + jnp.log(total)
        return carry

    lax.fori_loop(0, q_ref.shape[0] // HEAD, head, 0, unroll=2)


def forward_first_body(
    ids, lengths, clips, inputs, weight, pack, xq, q_ref, k_ref, v_ref, c_ref, lse_ref, bias_ref
):
    scale = clips[0]
    xq[...] = clip_tile(inputs[...], scale)
    qkv_into(xq[...], weight, pack, q_ref, k_ref, v_ref)
    attend(lengths, ids[2], q_ref, k_ref, v_ref, c_ref, lse_ref, bias_ref)


def forward_second_body(
    ids, lengths, xq, weight, pack, q_ref, k_ref, v_ref, c_ref, lse_ref, bias_ref
):
    qkv_into(xq[...], weight, pack, q_ref, k_ref, v_ref)
    attend(lengths, ids[2], q_ref, k_ref, v_ref, c_ref, lse_ref, bias_ref)


def backward_heads_body(
    which,
    ids,
    lengths,
    xq,
    grad_branch,
    q_ref,
    k_ref,
    v_ref,
    c_ref,
    lse_ref,
    merge_q,
    *refs,
):
    *outs, d_ref, qv_row, bias_ref, g_ref, x_t = refs
    bias_ref[...] = key_bias(lengths, ids[2])
    x_t[...] = xq[...].T
    count, rel = outs[0].shape[0], ids[which]
    width = q_ref.shape[0]
    g_ref[...] = dot(merge_q[...], grad_branch[...], 1, 1).astype(BF16)

    def head(index, carry):
        at = pl.ds(pl.multiple_of(index * HEAD, HEAD), HEAD)
        q, k, v, g = q_ref[at, :], k_ref[at, :], v_ref[at, :], g_ref[at, :]
        scores = dot(k, q, 0, 0) + bias_ref[...]
        prob = jnp.exp(scores - lse_ref[pl.ds(index, 1), :])
        grad_prob = dot(v, g, 0, 0)
        inner = jnp.sum(g.astype(F32) * c_ref[at, :].astype(F32), axis=0, keepdims=True)
        grad_score = (prob * (grad_prob - inner)).astype(BF16)
        d_ref[2, at, :] = dot(g, prob.astype(BF16), 1, 1).astype(BF16)
        d_ref[0, at, :] = (dot(k, grad_score, 1, 0) * 0.125).astype(BF16)
        d_ref[1, at, :] = dot(q, grad_score, 1, 1).astype(BF16)
        return carry

    lax.fori_loop(0, width // HEAD, head, 0, unroll=2)
    rows, step = x_t.shape[0] // (2 * count), width // (2 * count)
    if len(outs) == 2:
        outs = [out.at[:, at * rows : (at + 1) * rows, :] for out in outs for at in range(4)]
    for half, parts in ((1, outs[:4]), (0, outs[4:])):
        base = half_base(rel, half, 2 * count)
        at = pl.ds(pl.multiple_of(base * rows, count * rows), count * rows)
        for part in range(3):
            grad = dot(x_t[at, :], d_ref[part], 1, 1).astype(BF16)
            for block in range(count):
                to = ((base + block) ^ rel) % count
                piece = grad[block * rows : (block + 1) * rows, :]
                parts[part][to] = piece
        at = pl.ds(pl.multiple_of(base * step, count * step), count * step)
        grad = dot(c_ref[at, :], grad_branch[...], 1, 0)
        for block in range(count):
            to = ((base + block) ^ rel) % count
            piece = grad[block * step : (block + 1) * step, :]
            piece = jnp.concatenate([piece[:, :width], piece[:, width:]], axis=0)
            parts[3][to] = piece.astype(BF16)
    ones = jnp.ones((8, xq.shape[0]), BF16)
    qv_row[:, 0:width] = dot(ones, d_ref[0], 1, 1)
    qv_row[:, width : 2 * width] = dot(ones, d_ref[2], 1, 1)


def gelu_parts(hidden, scale):
    area = 0.5 + 0.5 * lax.erf(hidden * 0.7071067811865476)
    bell = jnp.exp(-0.5 * hidden * hidden)
    active = hidden * area
    slope = area + hidden * bell * 0.3989422804014327
    bent = jnp.tanh(active * (1.0 / scale))
    return (scale * bent).astype(BF16), ((1.0 - bent * bent) * slope).astype(BF16), active


def fold(value, op):
    rows, lanes = value.shape
    return op(value.reshape(rows // 8, 8, lanes), axis=0)


def middle_body(
    clips,
    c_own,
    c_other,
    merge_own,
    merge_other,
    inputs,
    up_own,
    up_other,
    down_own,
    down_other,
    pack_own,
    pack_other,
    vectors,
    cotangent,
    unit_out,
    inverse_out,
    normed_q,
    active_own,
    active_other,
    factor_own,
    factor_other,
    output,
    grad_sum,
    grad_feed,
    sums,
    work,
    hidden_ref,
    second_ref,
    tops,
    sum_ref,
):
    total = inputs.shape[0]
    work[...] = dot(c_own[...], merge_own[...], 0, 0) + dot(c_other[...], merge_other[...], 0, 0)
    tops[...] = jnp.zeros_like(tops)
    sum_ref[...] = jnp.zeros_like(sum_ref)
    clip_first, clip_second = clips[1], clips[2]

    def first_norm(index, carry):
        at = pl.ds(pl.multiple_of(index * TILE, TILE), TILE)
        rows = inputs[at, :].astype(F32)
        value = rows + work[at, :] + vectors[0:1, :]
        mean = jnp.mean(value, axis=-1, keepdims=True)
        centred = value - mean
        inverse = lax.rsqrt(jnp.mean(centred * centred, axis=-1, keepdims=True) + EPSILON)
        unit = centred * inverse
        normed = unit * vectors[2:3, :] + vectors[4:5, :]
        unit_out[at, :] = unit
        inverse_out[at, :] = jnp.broadcast_to(inverse, (TILE, 128))
        normed_q[at, :] = clip_tile(normed, clip_first)
        tops[0] = jnp.maximum(tops[0], fold(jnp.abs(rows), jnp.max))
        tops[1] = jnp.maximum(tops[1], fold(jnp.abs(normed), jnp.max))
        work[at, :] = normed
        return carry

    lax.fori_loop(0, total // TILE, first_norm, 0)
    span = hidden_ref.shape[1]
    for weight, pack, active_ref, factor_ref in (
        (up_own, pack_own, active_own, factor_own),
        (up_other, pack_other, active_other, factor_other),
    ):

        def gelu_chunk(source, index):
            cols = pl.ds(pl.multiple_of(index * span, span), span)
            bias = pack[0:1, cols]
            top = tops[2, :, 0:span]
            for row in range(total // GELU_TILE):
                at = slice(row * GELU_TILE, (row + 1) * GELU_TILE)
                clipped, factor, active = gelu_parts(source[at, :] + bias, clip_second)
                active_ref[at, cols] = clipped
                factor_ref[at, cols] = factor
                top = jnp.maximum(top, fold(jnp.abs(active), jnp.max))
            tops[2, :, 0:span] = top

        def multiply(target, index):
            cols = pl.ds(pl.multiple_of(index * span, span), span)
            target[...] = dot(normed_q[...], weight[:, cols], 1, 0)

        chunks = weight.shape[1] // span
        multiply(hidden_ref, 0)

        def pair(index, carry):
            multiply(second_ref, 2 * index + 1)
            gelu_chunk(hidden_ref, 2 * index)
            multiply(hidden_ref, jnp.minimum(2 * index + 2, chunks - 1))
            gelu_chunk(second_ref, 2 * index + 1)
            return carry

        lax.fori_loop(0, chunks // 2, pair, 0)
    work[...] += dot(active_own[...], down_own[...], 1, 0) + dot(
        active_other[...], down_other[...], 1, 0
    )

    def second_norm(index, carry):
        at = pl.ds(pl.multiple_of(index * TILE, TILE), TILE)
        value = work[at, :] + vectors[1:2, :]
        mean = jnp.mean(value, axis=-1, keepdims=True)
        centred = value - mean
        inverse = lax.rsqrt(jnp.mean(centred * centred, axis=-1, keepdims=True) + EPSILON)
        unit = centred * inverse
        output[at, :] = (unit * vectors[3:4, :] + vectors[5:6, :]).astype(BF16)
        upstream = cotangent[at, :].astype(F32)
        scaled = upstream * vectors[3:4, :]
        grad = inverse * (
            scaled
            - jnp.mean(scaled, axis=-1, keepdims=True)
            - unit * jnp.mean(scaled * unit, axis=-1, keepdims=True)
        )
        grad_sum[at, :] = grad
        grad_feed[at, :] = grad.astype(BF16)
        sum_ref[0] += fold(upstream * unit, jnp.sum)
        sum_ref[1] += fold(upstream, jnp.sum)
        sum_ref[2] += fold(grad, jnp.sum)
        return carry

    lax.fori_loop(0, total // TILE, second_norm, 0)
    for row in range(3):
        sums[row : row + 1, :] = jnp.sum(sum_ref[row], axis=0, keepdims=True)
    for row in range(3):
        top = jnp.max(jnp.max(tops[row], axis=0, keepdims=True), axis=1, keepdims=True)
        sums[3 + row : 4 + row, :] = jnp.broadcast_to(top, (1, sums.shape[1]))
    sums[6:8, :] = jnp.zeros((2, sums.shape[1]), F32)


def half_base(rel, half, blocks):
    return (half ^ (rel // (blocks // 2))) * (blocks // 2)


def down_grad_body(which, half, ids, active, grad_feed, chunk):
    rel = ids[which]
    count = chunk.shape[0]
    rows = active.shape[1] // (2 * count)
    base = half_base(rel, half, 2 * count)
    per = count // 2
    for tile in range(2):
        first = base + tile * per
        cols = pl.ds(pl.multiple_of(first * rows, per * rows), per * rows)
        grad = dot(active[:, cols], grad_feed[...], 0, 0)
        for block in range(per):
            piece = grad[block * rows : (block + 1) * rows, :].astype(BF16)
            to = ((first + block) ^ rel) % count
            chunk[to, 0:rows, :] = piece[:, :LANES]
            chunk[to, rows : 2 * rows, :] = piece[:, LANES:]


def up_grad_body(
    which, ids, grad_feed, down, up, factor, normed_q, before, high, low, bias_row, grad_normed, g_ref
):
    rel = ids[which]
    count = high.shape[0]
    span = 512

    def columns(index, carry):
        cols = pl.ds(pl.multiple_of(index * span, span), span)
        grad = dot(grad_feed[...], down[cols, :], 1, 1) * factor[:, cols].astype(F32)
        grad = grad.astype(BF16)
        g_ref[:, cols] = grad
        bias_row[0:1, cols] = jnp.sum(grad.astype(F32), axis=0, keepdims=True)
        return carry

    lax.fori_loop(0, g_ref.shape[1] // span, columns, 0, unroll=True)
    rows = normed_q.shape[1] // (2 * count)
    for half, chunk in ((1, high), (0, low)):
        base = half_base(rel, half, 2 * count)
        cols = pl.ds(pl.multiple_of(base * rows, count * rows), count * rows)
        grad = dot(normed_q[:, cols], g_ref[...], 0, 0)
        for block in range(count):
            to = ((base + block) ^ rel) % count
            for part in range(grad.shape[1] // LANES):
                piece = grad[block * rows : (block + 1) * rows, part * LANES : (part + 1) * LANES]
                chunk[to, part * rows : (part + 1) * rows, :] = piece.astype(BF16)
    result = dot(g_ref[...], up[...], 1, 1)
    if before is not None:
        result = result + before[...]
    grad_normed[...] = result


def up_grad_first_body(which, ids, grad_feed, down, up, factor, normed_q, *outs):
    up_grad_body(which, ids, grad_feed, down, up, factor, normed_q, None, *outs)


def first_norm_back_body(
    clips,
    grad_normed,
    grad_sum,
    unit_ref,
    inverse_ref,
    vectors,
    sums,
    bias_other,
    bias_own,
    grad_first,
    grad_branch,
    pack_other,
    pack_own,
    sum_ref,
):
    clip_first = clips[1]
    sum_ref[...] = jnp.zeros_like(sum_ref)

    def rows(index, carry):
        at = pl.ds(pl.multiple_of(index * TILE, TILE), TILE)
        unit = unit_ref[at, :]
        bent = jnp.tanh((unit * vectors[2:3, :] + vectors[4:5, :]) * (1.0 / clip_first))
        grad = grad_normed[at, :] * (1.0 - bent * bent) + grad_sum[at, :]
        scaled = grad * vectors[2:3, :]
        back = inverse_ref[at, 0:1] * (
            scaled
            - jnp.mean(scaled, axis=-1, keepdims=True)
            - unit * jnp.mean(scaled * unit, axis=-1, keepdims=True)
        )
        grad_first[at, :] = back
        grad_branch[at, :] = back.astype(BF16)
        sum_ref[0] += fold(grad * unit, jnp.sum)
        sum_ref[1] += fold(grad, jnp.sum)
        sum_ref[2] += fold(back, jnp.sum)
        return carry

    lax.fori_loop(0, unit_ref.shape[0] // TILE, rows, 0)
    width = unit_ref.shape[1]
    for pack, bias in ((pack_other, bias_other), (pack_own, bias_own)):
        pack[...] = jnp.zeros_like(pack)
        for row, source in ((0, 0), (2, 1), (4, 2)):
            pack[row : row + 1, :] = jnp.sum(sum_ref[source], axis=0, keepdims=True)
        pack[1:2, :] = sums[0:1, :]
        pack[3:4, :] = sums[1:2, :]
        pack[5:6, :] = sums[2:3, :]
        pack[6:7, :] = bias[0:1, 0:width]
        pack[7:8, :] = bias[0:1, width : 2 * width]
        pack[12:15, :] = sums[3:6, :]


def input_grad_body(clips, inputs, grad_first, w_own, w_other, d_own, d_other, out):
    terms = []
    for d_ref, weight in ((d_own, w_own), (d_other, w_other)):
        for part in range(3):
            terms.append(dot(d_ref[part], weight[part], 0, 1))
    bent = jnp.tanh(inputs[...].astype(F32) * (1.0 / clips[0]))
    out[...] = sum(terms[1:], terms[0]) * (1.0 - bent * bent) + grad_first[...]


def slope_of(weight, scale):
    bent = jnp.tanh(weight.astype(F32) * (1.0 / scale))
    return 1.0 - bent * bent


def block_value(rel, low, high, at):
    half = low.shape[0]
    at = at ^ rel
    first = low[jnp.minimum(at, half - 1)].astype(F32)
    return jnp.where(at < half, first, high[jnp.maximum(at - half, 0)].astype(F32))


def down_final_body(per, ids, own, other, low, high, weight, out):
    rows = weight.shape[0] // per
    slope = slope_of(weight[...], scale_row(own, other, 2, weight.shape[1]))
    for index in range(per):
        value = block_value(ids[0], low, high, pl.program_id(0) * per + index)
        at = slice(index * rows, (index + 1) * rows)
        out[at, :LANES] = value[:rows] * slope[at, :LANES]
        out[at, LANES:] = value[rows:] * slope[at, LANES:]


def up_final_body(per, ids, own, other, low, high, weight, out):
    rows = weight.shape[0] // per
    slope = slope_of(weight[...], scale_row(own, other, 1, weight.shape[1]))
    for index in range(per):
        value = block_value(ids[0], low, high, pl.program_id(0) * per + index)
        at = slice(index * rows, (index + 1) * rows)
        for part in range(weight.shape[1] // LANES):
            cols = slice(part * LANES, (part + 1) * LANES)
            out[at, cols] = value[part * rows : (part + 1) * rows] * slope[at, cols]


def rest_final_body(
    per, ids, own, other, low, high, p_own, p_other, project, merge, project_out, merge_out
):
    rows = project.shape[1] // per
    slopes = []
    for part in range(3):
        slopes.append(slope_of(project[part], scale_row(p_own, p_other, part, LANES)))
    scale = scale_row(own, other, 0, merge.shape[1])
    values = []
    for index in range(per):
        value = block_value(ids[0], low, high, pl.program_id(0) * per + index)
        values.append(value[3 * rows :])
        at = slice(index * rows, (index + 1) * rows)
        for part in range(3):
            project_out[part, at, :] = value[part * rows : (part + 1) * rows] * slopes[part][at]
    step = merge.shape[0] // per
    slope = slope_of(merge[...], scale)
    for part in range(2):
        across = slice(part * LANES, (part + 1) * LANES)
        piece = jnp.concatenate([v[part * step : (part + 1) * step] for v in values], axis=0)
        merge_out[:, across] = piece * slope[:, across]


class Exchange:
    def __init__(self, size, first):
        self.bits = size.bit_length() - 1
        assert 1 << self.bits == size and self.bits >= 4
        self.size = size
        self.orders = [list(order) + list(range(4, self.bits)) for order in first]
        self.blocks = 16

    def relative(self, position, core):
        total = 0
        for stage in range(4):
            bit = (position >> self.orders[core][stage]) & 1
            total = total + (bit << (3 - stage))
        return total

    def swap(self, value, stage):
        pairs = []
        for index in range(self.size):
            for core in range(2):
                to = index ^ (1 << self.orders[core][stage])
                pairs.append((2 * index + core, 2 * to + core))
        return lax.ppermute(value, ("dp", "tensor"), pairs)

    def core_swap(self, value):
        return lax.ppermute(value, "tensor", [(0, 1), (1, 0)])


class Task:
    def __init__(self, body, deps):
        self.body, self.deps, self.sends = body, list(deps), []


class Plan:
    def __init__(self):
        self.tasks = {}
        self.values = {}
        self.source = {}

    def given(self, name, value):
        self.values[name] = value
        return name

    def core(self, name, body, deps):
        self.tasks[name] = Task(body, deps)
        return name

    def send(self, name, source, body):
        self.tasks[source].sends.append((name, body))
        self.source[name] = source
        return name

    def run(self):
        values, last = dict(self.values), None

        def take(name):
            nonlocal last
            if name in values:
                return
            if name in self.source:
                take(self.source[name])
                return
            task = self.tasks[name]
            for dep in task.deps:
                take(dep)
            inputs = [values[dep] for dep in task.deps]
            if last is not None:
                inputs, last = lax.optimization_barrier((inputs, last))
            with jax.named_scope(name.replace(".", "_")):
                result = task.body(*inputs)
            values[name] = result
            last = jax.tree.leaves(result)[0]
            for sent, body in task.sends:
                with jax.named_scope(sent.replace(".", "_")):
                    values[sent] = body(result)

        for name in ORDER:
            if name in self.tasks:
                take(name)
            elif name[1:] in self.source:
                take(name[1:])
                values[name[1:]], last = lax.optimization_barrier((values[name[1:]], last))
        for name in self.tasks:
            take(name)
        return values

    def swap(self, name, source, way, stage, pick=lambda value: value):
        return self.send(name, source, lambda value: way.swap(pick(value), stage))

    def reduce(self, name, way, mine, theirs, pick):
        def swapped(index):
            return lambda v: [way.core_swap(value) for value in pick(v, index)]

        def whole(values):
            return values[0] if len(values) == 1 else jnp.concatenate(values, axis=1)

        high = self.send(name + ".high", theirs[0], swapped(0))
        low = self.send(name + ".low", theirs[1], swapped(1))
        value = self.core(
            f"{name}.add0",
            lambda mine, high: total([whole(pick(mine, 0)), whole(high)]),
            [mine[0], high],
        )
        got = self.swap(f"{name}.in0", value, way, 0)

        def second(mine, low, got):
            return split_in_two([whole(pick(mine, 1)), whole(low), got])

        def more(kept, got):
            return split_in_two([kept[0], got])

        value = self.core(f"{name}.add1", second, [mine[1], low, got])
        for stage in (1, 2, 3):
            got = self.swap(f"{name}.in{stage}", value, way, stage, second_of)
            if stage < 3:
                value = self.core(f"{name}.add{stage + 1}", more, [value, got])
        value = self.core(f"{name}.sum", lambda kept, got: total([kept[0], got]), [value, got])
        for stage in range(4, way.bits):
            sent = self.swap(f"{name}.in{stage}", value, way, stage)
            value = self.core(f"{name}.sum{stage}", lambda a, b: total([a, b]), [value, sent])
        for stage in reversed(range(4)):
            sent = self.swap(f"{name}.out{stage}", value, way, stage)
            if stage > 0:
                value = self.core(
                    f"{name}.join{stage}",
                    lambda a, b: jnp.concatenate([a, b], axis=0),
                    [value, sent],
                )
        return [value, sent]


def total(values):
    out = values[0].astype(F32)
    for value in values[1:]:
        out = out + value.astype(F32)
    return out.astype(BF16)


def split_in_two(values):
    half = values[0].shape[0] // 2
    return total([value[:half] for value in values]), total([value[half:] for value in values])


def second_of(value):
    return value[1]


def local(
    inputs,
    row_lengths,
    project_weight,
    merge_weight,
    up_weight,
    down_weight,
    query_value_bias,
    merge_bias,
    up_bias,
    down_bias,
    norm_gains,
    norm_shifts,
    clip_scales,
    cotangent,
):
    size = lax.axis_size("dp")
    exchange = Exchange(size, ((0, 1, 2, 3), (1, 0, 2, 3)))
    same_way = Exchange(size, ((0, 1, 2, 3), (0, 1, 2, 3)))
    blocks = exchange.blocks
    member = lax.axis_index("tensor")
    place = lax.axis_index("dp")
    rel0, rel1 = exchange.relative(place, 0), exchange.relative(place, 1)
    own_rel = jnp.where(member == 0, rel0, rel1)
    other_rel = jnp.where(member == 0, rel1, rel0)
    ids = jnp.stack([own_rel, other_rel, member * (LONG // SHORT)]).astype(jnp.int32)
    total, width = inputs.shape
    hidden = up_weight.shape[1]
    project = jnp.transpose(project_weight, (1, 0, 2))

    steps = 4
    small_grid = pltpu.CompilerParams(vmem_limit_bytes=12 << 20)
    project_block = pl.BlockSpec((3, width // steps, LANES), lambda i: (0, i, 0))
    rest_blocks = [
        pl.BlockSpec((LANES // steps, width), lambda i: (i, 0)),
        pl.BlockSpec((width // steps, hidden), lambda i: (i, 0)),
        pl.BlockSpec((hidden // steps, width), lambda i: (i, 0)),
    ]
    project_pack_spec = pl.BlockSpec((16, LANES), lambda i: (0, 0))
    pack_spec = pl.BlockSpec((16, hidden), lambda i: (0, 0))
    rest_weights = (merge_weight, up_weight, down_weight)

    def project_peaks():
        return pl.pallas_call(
            project_peaks_body,
            grid=(steps,),
            in_specs=[project_block, pl.BlockSpec((2, LANES), lambda i: (0, 0))],
            out_specs=project_pack_spec,
            out_shape=shaped((16, LANES), F32),
            compiler_params=small_grid,
        )(project, query_value_bias)

    def rest_peaks(weights):
        return pl.pallas_call(
            rest_peaks_body,
            grid=(steps,),
            in_specs=rest_blocks + [pl.BlockSpec((1, hidden), lambda i: (0, 0))],
            out_specs=pack_spec,
            out_shape=shaped((16, hidden), F32),
            compiler_params=small_grid,
        )(*weights, up_bias[None])

    def clip_project(own, other):
        return pl.pallas_call(
            clip_project_body,
            grid=(steps,),
            in_specs=[project_pack_spec, project_pack_spec, project_block],
            out_specs=project_block,
            out_shape=shaped(project.shape, BF16),
            compiler_params=small_grid,
        )(own, other, project)

    def clip_rest(own, other):
        return pl.pallas_call(
            clip_rest_body,
            grid=(steps,),
            in_specs=[pack_spec, pack_spec] + rest_blocks,
            out_specs=rest_blocks,
            out_shape=[shaped(a.shape, BF16) for a in rest_weights],
            compiler_params=small_grid,
        )(own, other, *rest_weights)

    project_own_pack = project_peaks()
    project_other_pack = exchange.core_swap(project_own_pack)
    project_own = clip_project(project_own_pack, project_other_pack)
    project_other = exchange.core_swap(project_own)
    tied, project_own = lax.optimization_barrier((rest_weights, project_own))
    own_pack = rest_peaks(tied)
    other_pack = exchange.core_swap(own_pack)
    other_pack, project_other = lax.optimization_barrier((other_pack, project_other))
    merge_own, up_own, down_own = clip_rest(own_pack, other_pack)
    merge_other = exchange.core_swap(merge_own)
    up_other = exchange.core_swap(up_own)
    down_other = exchange.core_swap(down_own)
    project_own, merge_own = lax.optimization_barrier((project_own, merge_own))

    head_shape = shaped((LANES, total), BF16)
    heads_out = [head_shape] * 4 + [shaped((8, total), F32)]
    mask_scratch = pltpu.VMEM((LONG, LONG), F32)
    xq, *own_heads = call(
        forward_first_body,
        [shaped((total, width), BF16)] + heads_out,
        (ids, row_lengths, clip_scales, inputs, project_own, project_own_pack),
        [mask_scratch],
        in_specs=[SMEM] * 3 + [VMEM] * 3,
        out_specs=[VMEM] * 6,
        limit=16 << 20,
    )
    other_heads = call(
        forward_second_body,
        heads_out,
        (ids, row_lengths, xq, project_other, project_other_pack),
        [mask_scratch],
        in_specs=[SMEM] * 2 + [VMEM] * 3,
        out_specs=[VMEM] * 5,
        limit=16 << 20,
    )

    vectors = jnp.concatenate([merge_bias[None], down_bias[None], norm_gains, norm_shifts], axis=0)
    rows_f32 = shaped((total, width), F32)
    rows_bf16 = shaped((total, width), BF16)
    wide = shaped((total, hidden), BF16)
    (
        unit,
        inverse,
        normed_q,
        active_own,
        active_other,
        factor_own,
        factor_other,
        output,
        grad_sum,
        grad_feed,
        sums,
    ) = call(
        middle_body,
        [
            rows_f32,
            shaped((total, 128), F32),
            rows_bf16,
            wide,
            wide,
            wide,
            wide,
            rows_bf16,
            rows_f32,
            rows_bf16,
            shaped((8, width), F32),
        ],
        (
            clip_scales,
            own_heads[3],
            other_heads[3],
            merge_own,
            merge_other,
            inputs,
            up_own,
            up_other,
            down_own,
            down_other,
            own_pack,
            other_pack,
            vectors,
            cotangent,
        ),
        [
            pltpu.VMEM((total, width), F32),
            pltpu.VMEM((total, 256), F32),
            pltpu.VMEM((total, 256), F32),
            pltpu.VMEM((3, 8, width), F32),
            pltpu.VMEM((3, 8, width), F32),
        ],
        in_specs=[SMEM] + [VMEM] * 13,
        out_specs=[VMEM] * 11,
        limit=32 << 20,
    )

    plan = Plan()
    chunk = shaped((blocks // 2, 2 * hidden // blocks, LANES), BF16)

    def down_half(which, half, active, grad):
        return call(
            partial(down_grad_body, which, half),
            chunk,
            (ids, active, grad),
            in_specs=[SMEM] + [VMEM] * 2,
            out_specs=VMEM,
            limit=9 << 20,
        )

    feed = plan.given("feed", grad_feed)
    down_tasks = {}
    for half, word in ((1, "high"), (0, "low")):
        for which, active in ((1, active_other), (0, active_own)):
            down_tasks[which, half] = plan.core(
                ("down.mine", "down.theirs")[which] + word,
                lambda grad, which=which, half=half, active=active: down_half(
                    which, half, active, grad
                ),
                [feed],
            )

    def take(index):
        return lambda values: values[index]

    def part(values, index):
        return values[index]

    def one(values, index):
        return [values[index]]

    down_out = plan.reduce(
        "down",
        exchange,
        (down_tasks[0, 1], down_tasks[0, 0]),
        (down_tasks[1, 1], down_tasks[1, 0]),
        lambda value, index: [value],
    )

    def up_half(body, which, grad, down, up, factor, *before):
        return call(
            partial(body, which),
            [chunk, chunk, shaped((1, hidden), F32), rows_f32],
            (ids, grad, down, up, factor, normed_q) + before,
            [pltpu.VMEM((total, hidden), BF16)],
            in_specs=[SMEM] + [VMEM] * (5 + len(before)),
            out_specs=[VMEM] * 4,
            limit=20 << 20,
        )

    up_theirs = plan.core(
        "up.theirs",
        lambda grad: up_half(
            up_grad_first_body, 1, grad, down_other, up_other, factor_other
        ),
        [feed],
    )
    up_mine = plan.core(
        "up.mine",
        lambda grad, before: up_half(
            up_grad_body, 0, grad, down_own, up_own, factor_own, before[3]
        ),
        [feed, up_theirs],
    )
    up_out = plan.reduce("up", exchange, (up_mine, up_mine), (up_theirs, up_theirs), one)

    small = shaped((16, width), F32)

    def norm_back(theirs, mine):
        ins = (clip_scales, mine[3], grad_sum, unit, inverse, vectors, sums, theirs[2], mine[2])
        return call(
            first_norm_back_body,
            [rows_f32, rows_bf16, small, small],
            ins,
            [pltpu.VMEM((3, 8, width), F32)],
            in_specs=[SMEM] + [VMEM] * 8,
            out_specs=[VMEM] * 4,
        )

    first_back = plan.core("norm", norm_back, [up_theirs, up_mine])

    def heads_back(which, back, heads, merge_q):
        count = (1, 4)[which]
        parts = [shaped((chunk.shape[0], chunk.shape[1] // count, LANES), BF16)] * count
        *outs, grads, row = call(
            partial(backward_heads_body, which),
            parts + parts + [shaped((3, LANES, total), BF16), shaped((8, 2 * LANES), F32)],
            (ids, row_lengths, xq, back[1]) + tuple(heads) + (merge_q,),
            [
                mask_scratch,
                pltpu.VMEM((LANES, total), BF16),
                pltpu.VMEM((width, total), BF16),
            ],
            in_specs=[SMEM] * 2 + [VMEM] * 8,
            out_specs=[VMEM] * (2 * count + 2),
            limit=18 << 20,
        )
        return outs[:count], outs[count:], grads, row

    heads_theirs = plan.core(
        "heads.theirs", lambda back: heads_back(1, back, other_heads, merge_other), [first_back]
    )
    heads_mine = plan.core(
        "heads.mine", lambda back: heads_back(0, back, own_heads, merge_own), [first_back]
    )
    rest_out = plan.reduce(
        "rest", exchange, (heads_mine, heads_mine), (heads_theirs, heads_theirs), part
    )

    def input_part(back, theirs, mine):
        return call(
            input_grad_body,
            rows_f32,
            (clip_scales, inputs, back[0], project_own, project_other, mine[2], theirs[2]),
            in_specs=[SMEM] + [VMEM] * 6,
            out_specs=VMEM,
            limit=16 << 20,
        )

    input_task = plan.core("input", input_part, [first_back, heads_theirs, heads_mine])

    def joined(sums_part, row):
        return jnp.concatenate([sums_part[:8], row[0:1], sums_part[12:15]], axis=0)

    small_row = lax.broadcasted_iota(jnp.int32, (12, width), 0)

    def merge_small(a, b):
        return jnp.where(small_row < 9, a + b, jnp.maximum(a, b))

    theirs_small = plan.core(
        "small.theirs", lambda back, heads: joined(back[2], heads[3]), [first_back, heads_theirs]
    )
    small_got = plan.send("small.got", theirs_small, exchange.core_swap)
    small_value = plan.core(
        "small.mine",
        lambda got, back, heads: merge_small(joined(back[3], heads[3]), got),
        [small_got, first_back, heads_mine],
    )
    for stage in range(exchange.bits):
        swap = partial(same_way.swap, stage=stage)
        small_in = plan.send(f"small.in{stage}", small_value, swap)
        small_value = plan.core(f"small.sum{stage}", merge_small, [small_value, small_in])

    final_steps = 4
    per = blocks // final_steps

    def final(body, parts, weights, specs, packs=()):
        part_specs = [pl.BlockSpec(part.shape, lambda i, s: (0, 0, 0)) for part in parts]
        pack = pl.BlockSpec((16, hidden), lambda i, s: (0, 0))
        ins = (ids, own_pack, other_pack) + tuple(parts) + tuple(packs) + weights
        return pl.pallas_call(
            partial(body, per),
            grid_spec=pltpu.PrefetchScalarGridSpec(
                num_scalar_prefetch=1,
                grid=(final_steps,),
                in_specs=[pack, pack]
                + part_specs
                + [pl.BlockSpec((16, LANES), lambda i, s: (0, 0))] * len(packs)
                + specs,
                out_specs=specs,
            ),
            out_shape=[shaped(weight.shape, F32) for weight in weights],
            compiler_params=pltpu.CompilerParams(vmem_limit_bytes=10 << 20),
            cost_estimate=pl.CostEstimate(flops=1, bytes_accessed=1, transcendentals=0),
        )(*ins)

    down_spec = pl.BlockSpec((hidden // final_steps, width), lambda i, s: (i, 0))
    plan.core(
        "down.final",
        lambda *parts: final(down_final_body, parts, (down_weight,), [down_spec])[0],
        down_out,
    )
    up_spec = pl.BlockSpec((width // final_steps, hidden), lambda i, s: (i, 0))
    plan.core(
        "up.final",
        lambda *parts: final(up_final_body, parts, (up_weight,), [up_spec])[0],
        up_out,
    )
    project_spec = pl.BlockSpec((3, width // final_steps, LANES), lambda i, s: (0, i, 0))
    merge_spec = pl.BlockSpec((LANES // final_steps, width), lambda i, s: (i, 0))
    plan.core(
        "rest.final",
        lambda *parts: final(
            rest_final_body,
            parts,
            (project, merge_weight),
            [project_spec, merge_spec],
            (project_own_pack, project_other_pack),
        ),
        rest_out,
    )
    values = plan.run()
    small_all = values[small_value]
    project_grad, merge_grad = values["rest.final"]
    peaks = small_all[9:12, 0]
    return (
        output,
        values[input_task],
        jnp.transpose(project_grad, (1, 0, 2)),
        merge_grad,
        values["up.final"],
        values["down.final"],
        small_all[8].reshape(2, LANES),
        small_all[4],
        small_all[6:8].reshape(hidden),
        small_all[5],
        small_all[0:2],
        small_all[2:4],
        DECAY * clip_scales + (1.0 - DECAY) * peaks,
    )


def solution(mesh):
    return jax.shard_map(
        local,
        mesh=mesh,
        in_specs=(
            P(("dp", "tensor"), None),
            P("dp"),
            P(None, None, "tensor"),
            P("tensor", None),
            P(None, "tensor"),
            P("tensor", None),
            P(None, "tensor"),
            P(),
            P("tensor"),
            P(),
            P(),
            P(),
            P(),
            P(("dp", "tensor"), None),
        ),
        out_specs=(
            P(("dp", "tensor"), None),
            P(("dp", "tensor"), None),
            P(None, None, "tensor"),
            P("tensor", None),
            P(None, "tensor"),
            P("tensor", None),
            P(None, "tensor"),
            P(),
            P("tensor"),
            P(),
            P(),
            P(),
            P(),
        ),
        check_vma=False,
    )
```

```python
from functools import partial

import jax
import jax.numpy as jnp
from jax import lax
from jax.experimental import pallas as pl
from jax.experimental.pallas import tpu as pltpu
from jax.sharding import PartitionSpec as P

HEAD = 64
LONG = 512
SHORT = 128
EPSILON = 1e-12
DECAY = 0.9
F32 = jnp.float32
BF16 = jnp.bfloat16
VMEM = pl.BlockSpec(memory_space=pltpu.VMEM)
SMEM = pl.BlockSpec(memory_space=pltpu.SMEM)
ORDER = (
    "down.theirshigh",
    "down.minehigh",
    "down.theirslow",
    "down.add0",
    "down.minelow",
    "up.theirs",
    "up.mine",
    "down.add1",
    "up.add0",
    "norm",
    "heads.theirs",
    "heads.mine",
    "down.add2",
    "up.add1",
    "rest.add0",
    "input",
    "down.add3",
    "small.theirs",
    "down.sum",
    "up.add2",
    "rest.add1",
    "small.mine",
    "down.join3",
    "up.add3",
    "rest.add2",
    "down.join2",
    "up.sum",
    "rest.add3",
    "small.sum0",
    "down.join1",
    "up.join3",
    "small.sum1",
    "rest.sum",
    "small.sum2",
    "up.join2",
    "rest.join3",
    "down.final",
    "rest.join2",
    "up.join1",
    "small.sum3",
    "rest.join1",
    "up.final",
    "rest.final",
)
COST = 1
LANES = 384
TILE = 128
GELU_TILE = 32


def dot(a, b, ca, cb):
    return lax.dot_general(a, b, (((ca,), (cb,)), ((), ())), preferred_element_type=F32)


def shaped(shape, dtype):
    return jax.ShapeDtypeStruct(shape, dtype)


def call(
    body, out_shape, ins, scratch=(), in_specs=None, out_specs=None, limit=None
):
    nbytes = sum(a.size * a.dtype.itemsize for a in ins)
    nbytes += sum(o.size * o.dtype.itemsize for o in jax.tree.leaves(out_shape))
    params = dict(
        out_shape=out_shape,
        compiler_params=pltpu.CompilerParams(vmem_limit_bytes=limit or (nbytes + (6 << 20))),
        cost_estimate=pl.CostEstimate(flops=1, bytes_accessed=COST, transcendentals=0),
    )
    return pl.pallas_call(
        body, in_specs=in_specs, out_specs=out_specs, scratch_shapes=list(scratch), **params
    )(*ins)


def peak(value):
    top = jnp.max(jnp.abs(value.astype(F32)), axis=0, keepdims=True)
    return jnp.max(top, axis=1, keepdims=True)


def raise_peaks(pack, tiles):
    for row, tile in enumerate(tiles):
        at = slice(8 + row, 9 + row)
        pack[at, :] = jnp.maximum(pack[at, :], peak(tile))


def project_peaks_body(project, qv_bias, pack):
    @pl.when(pl.program_id(0) == 0)
    def _():
        pack[...] = jnp.zeros_like(pack)
        pack[0:2, :] = qv_bias[...]

    raise_peaks(pack, [project[0], project[1], project[2]])


def rest_peaks_body(merge, up, down, up_bias, pack):
    @pl.when(pl.program_id(0) == 0)
    def _():
        pack[...] = jnp.zeros_like(pack)
        pack[0:1, :] = up_bias[...]

    raise_peaks(pack, [merge[...], up[...], down[...]])


def scale_row(own, other, row, width):
    at = slice(8 + row, 9 + row)
    return 0.5 * jnp.maximum(own[at, 0:width], other[at, 0:width])


def clip_tile(value, scale):
    return (scale * jnp.tanh(value.astype(F32) * (1.0 / scale))).astype(BF16)


def clip_project_body(own, other, project, out):
    for part in range(3):
        out[part] = clip_tile(project[part], scale_row(own, other, part, LANES))


def clip_rest_body(own, other, merge, up, down, merge_q, up_q, down_q):
    for row, (src, dst) in enumerate(((merge, merge_q), (up, up_q), (down, down_q))):
        dst[...] = clip_tile(src[...], scale_row(own, other, row, src.shape[1]))


def key_bias(lengths, first):
    key = lax.broadcasted_iota(jnp.int32, (LONG, 1), 0)
    query = lax.broadcasted_iota(jnp.int32, (1, LONG), 1)
    single = lengths[first] > SHORT
    limit = jnp.full((LONG, 1), lengths[first], jnp.int32)
    for slot in range(1, LONG // SHORT):
        own = jnp.where(single, lengths[first], slot * SHORT + lengths[first + slot])
        limit = jnp.where(key >= slot * SHORT, own, limit)
    key_row = jnp.where(single, 0, key // SHORT)
    query_row = jnp.where(single, 0, query // SHORT)
    key_row = jnp.where(key < limit, key_row, -1)
    return jnp.where(key_row == query_row, 0.0, -1e30).astype(F32)


def qkv_into(xq, weight, bias_pack, q_ref, k_ref, v_ref):
    for part, ref in enumerate((q_ref, k_ref, v_ref)):
        value = dot(xq, weight[part], 1, 0)
        if part == 0:
            value = value + bias_pack[0:1, :]
        if part == 2:
            value = value + bias_pack[1:2, :]
        value = value.astype(BF16)
        if part == 0:
            value = value * jnp.asarray(0.125, BF16)
        ref[...] = value.T


def attend(lengths, first, q_ref, k_ref, v_ref, c_ref, lse_ref, bias_ref):
    bias_ref[...] = key_bias(lengths, first)

    def head(index, carry):
        at = pl.ds(pl.multiple_of(index * HEAD, HEAD), HEAD)
        scores = dot(k_ref[at, :], q_ref[at, :], 0, 0) + bias_ref[...]
        top = jnp.max(scores, axis=0, keepdims=True)
        prob = jnp.exp(scores - top)
        total = jnp.sum(prob, axis=0, keepdims=True)
        mixed = dot(v_ref[at, :], prob.astype(BF16), 1, 0)
        c_ref[at, :] = (mixed * (1.0 / total)).astype(BF16)
        lse_ref[pl.ds(index, 1), :] = top + jnp.log(total)
        return carry

    lax.fori_loop(0, q_ref.shape[0] // HEAD, head, 0)


def forward_first_body(
    ids, lengths, clips, inputs, weight, pack, xq, q_ref, k_ref, v_ref, c_ref, lse_ref, bias_ref
):
    scale = clips[0]
    xq[...] = clip_tile(inputs[...], scale)
    qkv_into(xq[...], weight, pack, q_ref, k_ref, v_ref)
    attend(lengths, ids[2], q_ref, k_ref, v_ref, c_ref, lse_ref, bias_ref)


def forward_second_body(
    ids, lengths, xq, weight, pack, q_ref, k_ref, v_ref, c_ref, lse_ref, bias_ref
):
    qkv_into(xq[...], weight, pack, q_ref, k_ref, v_ref)
    attend(lengths, ids[2], q_ref, k_ref, v_ref, c_ref, lse_ref, bias_ref)


def backward_heads_body(
    which,
    ids,
    lengths,
    xq,
    grad_branch,
    q_ref,
    k_ref,
    v_ref,
    c_ref,
    lse_ref,
    merge_q,
    *refs,
):
    *outs, d_ref, qv_row, bias_ref, g_ref, x_t = refs
    bias_ref[...] = key_bias(lengths, ids[2])
    x_t[...] = xq[...].T
    count, rel = outs[0].shape[0], ids[which]
    width = q_ref.shape[0]
    g_ref[...] = dot(merge_q[...], grad_branch[...], 1, 1).astype(BF16)

    def head(index, carry):
        at = pl.ds(pl.multiple_of(index * HEAD, HEAD), HEAD)
        q, k, v, g = q_ref[at, :], k_ref[at, :], v_ref[at, :], g_ref[at, :]
        scores = dot(k, q, 0, 0) + bias_ref[...]
        prob = jnp.exp(scores - lse_ref[pl.ds(index, 1), :])
        grad_prob = dot(v, g, 0, 0)
        inner = jnp.sum(g.astype(F32) * c_ref[at, :].astype(F32), axis=0, keepdims=True)
        grad_score = (prob * (grad_prob - inner)).astype(BF16)
        d_ref[2, at, :] = dot(g, prob.astype(BF16), 1, 1).astype(BF16)
        d_ref[0, at, :] = (dot(k, grad_score, 1, 0) * 0.125).astype(BF16)
        d_ref[1, at, :] = dot(q, grad_score, 1, 1).astype(BF16)
        return carry

    lax.fori_loop(0, width // HEAD, head, 0)
    rows, step = x_t.shape[0] // (2 * count), width // (2 * count)
    if len(outs) == 2:
        outs = [out.at[:, at * rows : (at + 1) * rows, :] for out in outs for at in range(4)]
    for half, parts in ((1, outs[:4]), (0, outs[4:])):
        base = half_base(rel, half, 2 * count)
        at = pl.ds(pl.multiple_of(base * rows, count * rows), count * rows)
        for part in range(3):
            grad = dot(x_t[at, :], d_ref[part], 1, 1).astype(BF16)
            for block in range(count):
                to = ((base + block) ^ rel) % count
                piece = grad[block * rows : (block + 1) * rows, :]
                parts[part][to] = piece
        at = pl.ds(pl.multiple_of(base * step, count * step), count * step)
        grad = dot(c_ref[at, :], grad_branch[...], 1, 0)
        for block in range(count):
            to = ((base + block) ^ rel) % count
            piece = grad[block * step : (block + 1) * step, :]
            piece = jnp.concatenate([piece[:, :width], piece[:, width:]], axis=0)
            parts[3][to] = piece.astype(BF16)
    ones = jnp.ones((8, xq.shape[0]), BF16)
    qv_row[:, 0:width] = dot(ones, d_ref[0], 1, 1)
    qv_row[:, width : 2 * width] = dot(ones, d_ref[2], 1, 1)


def gelu_parts(hidden, scale):
    area = 0.5 + 0.5 * lax.erf(hidden * 0.7071067811865476)
    bell = jnp.exp(-0.5 * hidden * hidden)
    active = hidden * area
    slope = area + hidden * bell * 0.3989422804014327
    bent = jnp.tanh(active * (1.0 / scale))
    return (scale * bent).astype(BF16), ((1.0 - bent * bent) * slope).astype(BF16), active


def fold(value, op):
    rows, lanes = value.shape
    return op(value.reshape(rows // 8, 8, lanes), axis=0)


def middle_body(
    clips,
    c_own,
    c_other,
    merge_own,
    merge_other,
    inputs,
    up_own,
    up_other,
    down_own,
    down_other,
    pack_own,
    pack_other,
    vectors,
    cotangent,
    unit_out,
    inverse_out,
    normed_q,
    active_own,
    active_other,
    factor_own,
    factor_other,
    output,
    grad_sum,
    grad_feed,
    sums,
    work,
    hidden_ref,
    second_ref,
    tops,
    sum_ref,
):
    total = inputs.shape[0]
    work[...] = dot(c_own[...], merge_own[...], 0, 0) + dot(c_other[...], merge_other[...], 0, 0)
    tops[...] = jnp.zeros_like(tops)
    sum_ref[...] = jnp.zeros_like(sum_ref)
    clip_first, clip_second = clips[1], clips[2]

    def first_norm(index, carry):
        at = pl.ds(pl.multiple_of(index * TILE, TILE), TILE)
        rows = inputs[at, :].astype(F32)
        value = rows + work[at, :] + vectors[0:1, :]
        mean = jnp.mean(value, axis=-1, keepdims=True)
        centred = value - mean
        inverse = lax.rsqrt(jnp.mean(centred * centred, axis=-1, keepdims=True) + EPSILON)
        unit = centred * inverse
        normed = unit * vectors[2:3, :] + vectors[4:5, :]
        unit_out[at, :] = unit
        inverse_out[at, :] = jnp.broadcast_to(inverse, (TILE, 128))
        normed_q[at, :] = clip_tile(normed, clip_first)
        tops[0] = jnp.maximum(tops[0], fold(jnp.abs(rows), jnp.max))
        tops[1] = jnp.maximum(tops[1], fold(jnp.abs(normed), jnp.max))
        work[at, :] = normed
        return carry

    lax.fori_loop(0, total // TILE, first_norm, 0)
    span = hidden_ref.shape[1]
    for weight, pack, active_ref, factor_ref in (
        (up_own, pack_own, active_own, factor_own),
        (up_other, pack_other, active_other, factor_other),
    ):

        def gelu_chunk(source, index):
            cols = pl.ds(pl.multiple_of(index * span, span), span)
            bias = pack[0:1, cols]
            top = tops[2, :, 0:span]
            for row in range(total // GELU_TILE):
                at = slice(row * GELU_TILE, (row + 1) * GELU_TILE)
                clipped, factor, active = gelu_parts(source[at, :] + bias, clip_second)
                active_ref[at, cols] = clipped
                factor_ref[at, cols] = factor
                top = jnp.maximum(top, fold(jnp.abs(active), jnp.max))
            tops[2, :, 0:span] = top

        def multiply(target, index):
            cols = pl.ds(pl.multiple_of(index * span, span), span)
            target[...] = dot(normed_q[...], weight[:, cols], 1, 0)

        chunks = weight.shape[1] // span
        multiply(hidden_ref, 0)

        def pair(index, carry):
            multiply(second_ref, 2 * index + 1)
            gelu_chunk(hidden_ref, 2 * index)
            multiply(hidden_ref, jnp.minimum(2 * index + 2, chunks - 1))
            gelu_chunk(second_ref, 2 * index + 1)
            return carry

        lax.fori_loop(0, chunks // 2, pair, 0)
    work[...] += dot(active_own[...], down_own[...], 1, 0) + dot(
        active_other[...], down_other[...], 1, 0
    )

    def second_norm(index, carry):
        at = pl.ds(pl.multiple_of(index * TILE, TILE), TILE)
        value = work[at, :] + vectors[1:2, :]
        mean = jnp.mean(value, axis=-1, keepdims=True)
        centred = value - mean
        inverse = lax.rsqrt(jnp.mean(centred * centred, axis=-1, keepdims=True) + EPSILON)
        unit = centred * inverse
        output[at, :] = (unit * vectors[3:4, :] + vectors[5:6, :]).astype(BF16)
        upstream = cotangent[at, :].astype(F32)
        scaled = upstream * vectors[3:4, :]
        grad = inverse * (
            scaled
            - jnp.mean(scaled, axis=-1, keepdims=True)
            - unit * jnp.mean(scaled * unit, axis=-1, keepdims=True)
        )
        grad_sum[at, :] = grad
        grad_feed[at, :] = grad.astype(BF16)
        sum_ref[0] += fold(upstream * unit, jnp.sum)
        sum_ref[1] += fold(upstream, jnp.sum)
        sum_ref[2] += fold(grad, jnp.sum)
        return carry

    lax.fori_loop(0, total // TILE, second_norm, 0)
    for row in range(3):
        sums[row : row + 1, :] = jnp.sum(sum_ref[row], axis=0, keepdims=True)
    for row in range(3):
        top = jnp.max(jnp.max(tops[row], axis=0, keepdims=True), axis=1, keepdims=True)
        sums[3 + row : 4 + row, :] = jnp.broadcast_to(top, (1, sums.shape[1]))
    sums[6:8, :] = jnp.zeros((2, sums.shape[1]), F32)


def half_base(rel, half, blocks):
    return (half ^ (rel // (blocks // 2))) * (blocks // 2)


def down_grad_body(which, half, ids, active, grad_feed, chunk):
    rel = ids[which]
    count = chunk.shape[0]
    rows = active.shape[1] // (2 * count)
    base = half_base(rel, half, 2 * count)
    per = count // 2
    for tile in range(2):
        first = base + tile * per
        cols = pl.ds(pl.multiple_of(first * rows, per * rows), per * rows)
        grad = dot(active[:, cols], grad_feed[...], 0, 0)
        for block in range(per):
            piece = grad[block * rows : (block + 1) * rows, :].astype(BF16)
            to = ((first + block) ^ rel) % count
            chunk[to, 0:rows, :] = piece[:, :LANES]
            chunk[to, rows : 2 * rows, :] = piece[:, LANES:]


def up_grad_body(
    which, ids, grad_feed, down, up, factor, normed_q, before, high, low, bias_row, grad_normed, g_ref
):
    rel = ids[which]
    count = high.shape[0]
    span = 512

    def columns(index, carry):
        cols = pl.ds(pl.multiple_of(index * span, span), span)
        grad = dot(grad_feed[...], down[cols, :], 1, 1) * factor[:, cols].astype(F32)
        grad = grad.astype(BF16)
        g_ref[:, cols] = grad
        bias_row[0:1, cols] = jnp.sum(grad.astype(F32), axis=0, keepdims=True)
        return carry

    lax.fori_loop(0, g_ref.shape[1] // span, columns, 0)
    rows = normed_q.shape[1] // (2 * count)
    for half, chunk in ((1, high), (0, low)):
        base = half_base(rel, half, 2 * count)
        cols = pl.ds(pl.multiple_of(base * rows, count * rows), count * rows)
        grad = dot(normed_q[:, cols], g_ref[...], 0, 0)
        for block in range(count):
            to = ((base + block) ^ rel) % count
            for part in range(grad.shape[1] // LANES):
                piece = grad[block * rows : (block + 1) * rows, part * LANES : (part + 1) * LANES]
                chunk[to, part * rows : (part + 1) * rows, :] = piece.astype(BF16)
    result = dot(g_ref[...], up[...], 1, 1)
    if before is not None:
        result = result + before[...]
    grad_normed[...] = result


def up_grad_first_body(which, ids, grad_feed, down, up, factor, normed_q, *outs):
    up_grad_body(which, ids, grad_feed, down, up, factor, normed_q, None, *outs)


def first_norm_back_body(
    clips,
    grad_normed,
    grad_sum,
    unit_ref,
    inverse_ref,
    vectors,
    sums,
    bias_other,
    bias_own,
    grad_first,
    grad_branch,
    pack_other,
    pack_own,
    sum_ref,
):
    clip_first = clips[1]
    sum_ref[...] = jnp.zeros_like(sum_ref)

    def rows(index, carry):
        at = pl.ds(pl.multiple_of(index * TILE, TILE), TILE)
        unit = unit_ref[at, :]
        bent = jnp.tanh((unit * vectors[2:3, :] + vectors[4:5, :]) * (1.0 / clip_first))
        grad = grad_normed[at, :] * (1.0 - bent * bent) + grad_sum[at, :]
        scaled = grad * vectors[2:3, :]
        back = inverse_ref[at, 0:1] * (
            scaled
            - jnp.mean(scaled, axis=-1, keepdims=True)
            - unit * jnp.mean(scaled * unit, axis=-1, keepdims=True)
        )
        grad_first[at, :] = back
        grad_branch[at, :] = back.astype(BF16)
        sum_ref[0] += fold(grad * unit, jnp.sum)
        sum_ref[1] += fold(grad, jnp.sum)
        sum_ref[2] += fold(back, jnp.sum)
        return carry

    lax.fori_loop(0, unit_ref.shape[0] // TILE, rows, 0)
    width = unit_ref.shape[1]
    for pack, bias in ((pack_other, bias_other), (pack_own, bias_own)):
        pack[...] = jnp.zeros_like(pack)
        for row, source in ((0, 0), (2, 1), (4, 2)):
            pack[row : row + 1, :] = jnp.sum(sum_ref[source], axis=0, keepdims=True)
        pack[1:2, :] = sums[0:1, :]
        pack[3:4, :] = sums[1:2, :]
        pack[5:6, :] = sums[2:3, :]
        pack[6:7, :] = bias[0:1, 0:width]
        pack[7:8, :] = bias[0:1, width : 2 * width]
        pack[12:15, :] = sums[3:6, :]


def input_grad_body(clips, inputs, grad_first, w_own, w_other, d_own, d_other, out):
    terms = []
    for d_ref, weight in ((d_own, w_own), (d_other, w_other)):
        for part in range(3):
            terms.append(dot(d_ref[part], weight[part], 0, 1))
    bent = jnp.tanh(inputs[...].astype(F32) * (1.0 / clips[0]))
    out[...] = sum(terms[1:], terms[0]) * (1.0 - bent * bent) + grad_first[...]


def slope_of(weight, scale):
    bent = jnp.tanh(weight.astype(F32) * (1.0 / scale))
    return 1.0 - bent * bent


def block_value(rel, low, high, at):
    half = low.shape[0]
    at = at ^ rel
    first = low[jnp.minimum(at, half - 1)].astype(F32)
    return jnp.where(at < half, first, high[jnp.maximum(at - half, 0)].astype(F32))


def down_final_body(per, ids, own, other, low, high, weight, out):
    rows = weight.shape[0] // per
    slope = slope_of(weight[...], scale_row(own, other, 2, weight.shape[1]))
    for index in range(per):
        value = block_value(ids[0], low, high, pl.program_id(0) * per + index)
        at = slice(index * rows, (index + 1) * rows)
        out[at, :LANES] = value[:rows] * slope[at, :LANES]
        out[at, LANES:] = value[rows:] * slope[at, LANES:]


def up_final_body(per, ids, own, other, low, high, weight, out):
    rows = weight.shape[0] // per
    slope = slope_of(weight[...], scale_row(own, other, 1, weight.shape[1]))
    for index in range(per):
        value = block_value(ids[0], low, high, pl.program_id(0) * per + index)
        at = slice(index * rows, (index + 1) * rows)
        for part in range(weight.shape[1] // LANES):
            cols = slice(part * LANES, (part + 1) * LANES)
            out[at, cols] = value[part * rows : (part + 1) * rows] * slope[at, cols]


def rest_final_body(
    per, ids, own, other, low, high, p_own, p_other, project, merge, project_out, merge_out
):
    rows = project.shape[1] // per
    slopes = []
    for part in range(3):
        slopes.append(slope_of(project[part], scale_row(p_own, p_other, part, LANES)))
    scale = scale_row(own, other, 0, merge.shape[1])
    values = []
    for index in range(per):
        value = block_value(ids[0], low, high, pl.program_id(0) * per + index)
        values.append(value[3 * rows :])
        at = slice(index * rows, (index + 1) * rows)
        for part in range(3):
            project_out[part, at, :] = value[part * rows : (part + 1) * rows] * slopes[part][at]
    step = merge.shape[0] // per
    slope = slope_of(merge[...], scale)
    for part in range(2):
        across = slice(part * LANES, (part + 1) * LANES)
        piece = jnp.concatenate([v[part * step : (part + 1) * step] for v in values], axis=0)
        merge_out[:, across] = piece * slope[:, across]


class Exchange:
    def __init__(self, size, first):
        self.bits = size.bit_length() - 1
        assert 1 << self.bits == size and self.bits >= 4
        self.size = size
        self.orders = [list(order) + list(range(4, self.bits)) for order in first]
        self.blocks = 16

    def relative(self, position, core):
        total = 0
        for stage in range(4):
            bit = (position >> self.orders[core][stage]) & 1
            total = total + (bit << (3 - stage))
        return total

    def swap(self, value, stage):
        pairs = []
        for index in range(self.size):
            for core in range(2):
                to = index ^ (1 << self.orders[core][stage])
                pairs.append((2 * index + core, 2 * to + core))
        return lax.ppermute(value, ("dp", "tensor"), pairs)

    def core_swap(self, value):
        return lax.ppermute(value, "tensor", [(0, 1), (1, 0)])


class Task:
    def __init__(self, body, deps):
        self.body, self.deps, self.sends = body, list(deps), []


class Plan:
    def __init__(self):
        self.tasks = {}
        self.values = {}
        self.source = {}

    def given(self, name, value):
        self.values[name] = value
        return name

    def core(self, name, body, deps):
        self.tasks[name] = Task(body, deps)
        return name

    def send(self, name, source, body):
        self.tasks[source].sends.append((name, body))
        self.source[name] = source
        return name

    def run(self):
        values, last = dict(self.values), None

        def take(name):
            nonlocal last
            if name in values:
                return
            if name in self.source:
                take(self.source[name])
                return
            task = self.tasks[name]
            for dep in task.deps:
                take(dep)
            inputs = [values[dep] for dep in task.deps]
            if last is not None:
                inputs, last = lax.optimization_barrier((inputs, last))
            with jax.named_scope(name.replace(".", "_")):
                result = task.body(*inputs)
            values[name] = result
            last = jax.tree.leaves(result)[0]
            for sent, body in task.sends:
                with jax.named_scope(sent.replace(".", "_")):
                    values[sent] = body(result)

        for name in ORDER:
            if name in self.tasks:
                take(name)
            elif name[1:] in self.source:
                take(name[1:])
                values[name[1:]], last = lax.optimization_barrier((values[name[1:]], last))
        for name in self.tasks:
            take(name)
        return values

    def swap(self, name, source, way, stage, pick=lambda value: value):
        return self.send(name, source, lambda value: way.swap(pick(value), stage))

    def reduce(self, name, way, mine, theirs, pick):
        def swapped(index):
            return lambda v: [way.core_swap(value) for value in pick(v, index)]

        def whole(values):
            return values[0] if len(values) == 1 else jnp.concatenate(values, axis=1)

        high = self.send(name + ".high", theirs[0], swapped(0))
        low = self.send(name + ".low", theirs[1], swapped(1))
        value = self.core(
            f"{name}.add0",
            lambda mine, high: total([whole(pick(mine, 0)), whole(high)]),
            [mine[0], high],
        )
        got = self.swap(f"{name}.in0", value, way, 0)

        def second(mine, low, got):
            return split_in_two([whole(pick(mine, 1)), whole(low), got])

        def more(kept, got):
            return split_in_two([kept[0], got])

        value = self.core(f"{name}.add1", second, [mine[1], low, got])
        for stage in (1, 2, 3):
            got = self.swap(f"{name}.in{stage}", value, way, stage, second_of)
            if stage < 3:
                value = self.core(f"{name}.add{stage + 1}", more, [value, got])
        value = self.core(f"{name}.sum", lambda kept, got: total([kept[0], got]), [value, got])
        for stage in range(4, way.bits):
            sent = self.swap(f"{name}.in{stage}", value, way, stage)
            value = self.core(f"{name}.sum{stage}", lambda a, b: total([a, b]), [value, sent])
        for stage in reversed(range(4)):
            sent = self.swap(f"{name}.out{stage}", value, way, stage)
            if stage > 0:
                value = self.core(
                    f"{name}.join{stage}",
                    lambda a, b: jnp.concatenate([a, b], axis=0),
                    [value, sent],
                )
        return [value, sent]


def total(values):
    out = values[0].astype(F32)
    for value in values[1:]:
        out = out + value.astype(F32)
    return out.astype(BF16)


def split_in_two(values):
    half = values[0].shape[0] // 2
    return total([value[:half] for value in values]), total([value[half:] for value in values])


def second_of(value):
    return value[1]


def local(
    inputs,
    row_lengths,
    project_weight,
    merge_weight,
    up_weight,
    down_weight,
    query_value_bias,
    merge_bias,
    up_bias,
    down_bias,
    norm_gains,
    norm_shifts,
    clip_scales,
    cotangent,
):
    size = lax.axis_size("dp")
    exchange = Exchange(size, ((0, 1, 2, 3), (1, 0, 2, 3)))
    same_way = Exchange(size, ((0, 1, 2, 3), (0, 1, 2, 3)))
    blocks = exchange.blocks
    member = lax.axis_index("tensor")
    place = lax.axis_index("dp")
    rel0, rel1 = exchange.relative(place, 0), exchange.relative(place, 1)
    own_rel = jnp.where(member == 0, rel0, rel1)
    other_rel = jnp.where(member == 0, rel1, rel0)
    ids = jnp.stack([own_rel, other_rel, member * (LONG // SHORT)]).astype(jnp.int32)
    total, width = inputs.shape
    hidden = up_weight.shape[1]
    project = jnp.transpose(project_weight, (1, 0, 2))

    steps = 4
    small_grid = pltpu.CompilerParams(vmem_limit_bytes=12 << 20)
    project_block = pl.BlockSpec((3, width // steps, LANES), lambda i: (0, i, 0))
    rest_blocks = [
        pl.BlockSpec((LANES // steps, width), lambda i: (i, 0)),
        pl.BlockSpec((width // steps, hidden), lambda i: (i, 0)),
        pl.BlockSpec((hidden // steps, width), lambda i: (i, 0)),
    ]
    project_pack_spec = pl.BlockSpec((16, LANES), lambda i: (0, 0))
    pack_spec = pl.BlockSpec((16, hidden), lambda i: (0, 0))
    rest_weights = (merge_weight, up_weight, down_weight)

    def project_peaks():
        return pl.pallas_call(
            project_peaks_body,
            grid=(steps,),
            in_specs=[project_block, pl.BlockSpec((2, LANES), lambda i: (0, 0))],
            out_specs=project_pack_spec,
            out_shape=shaped((16, LANES), F32),
            compiler_params=small_grid,
        )(project, query_value_bias)

    def rest_peaks(weights):
        return pl.pallas_call(
            rest_peaks_body,
            grid=(steps,),
            in_specs=rest_blocks + [pl.BlockSpec((1, hidden), lambda i: (0, 0))],
            out_specs=pack_spec,
            out_shape=shaped((16, hidden), F32),
            compiler_params=small_grid,
        )(*weights, up_bias[None])

    def clip_project(own, other):
        return pl.pallas_call(
            clip_project_body,
            grid=(steps,),
            in_specs=[project_pack_spec, project_pack_spec, project_block],
            out_specs=project_block,
            out_shape=shaped(project.shape, BF16),
            compiler_params=small_grid,
        )(own, other, project)

    def clip_rest(own, other):
        return pl.pallas_call(
            clip_rest_body,
            grid=(steps,),
            in_specs=[pack_spec, pack_spec] + rest_blocks,
            out_specs=rest_blocks,
            out_shape=[shaped(a.shape, BF16) for a in rest_weights],
            compiler_params=small_grid,
        )(own, other, *rest_weights)

    project_own_pack = project_peaks()
    project_other_pack = exchange.core_swap(project_own_pack)
    project_own = clip_project(project_own_pack, project_other_pack)
    project_other = exchange.core_swap(project_own)
    tied, project_own = lax.optimization_barrier((rest_weights, project_own))
    own_pack = rest_peaks(tied)
    other_pack = exchange.core_swap(own_pack)
    other_pack, project_other = lax.optimization_barrier((other_pack, project_other))
    merge_own, up_own, down_own = clip_rest(own_pack, other_pack)
    merge_other = exchange.core_swap(merge_own)
    up_other = exchange.core_swap(up_own)
    down_other = exchange.core_swap(down_own)
    project_own, merge_own = lax.optimization_barrier((project_own, merge_own))

    head_shape = shaped((LANES, total), BF16)
    heads_out = [head_shape] * 4 + [shaped((8, total), F32)]
    mask_scratch = pltpu.VMEM((LONG, LONG), F32)
    xq, *own_heads = call(
        forward_first_body,
        [shaped((total, width), BF16)] + heads_out,
        (ids, row_lengths, clip_scales, inputs, project_own, project_own_pack),
        [mask_scratch],
        in_specs=[SMEM] * 3 + [VMEM] * 3,
        out_specs=[VMEM] * 6,
        limit=16 << 20,
    )
    other_heads = call(
        forward_second_body,
        heads_out,
        (ids, row_lengths, xq, project_other, project_other_pack),
        [mask_scratch],
        in_specs=[SMEM] * 2 + [VMEM] * 3,
        out_specs=[VMEM] * 5,
        limit=16 << 20,
    )

    vectors = jnp.concatenate([merge_bias[None], down_bias[None], norm_gains, norm_shifts], axis=0)
    rows_f32 = shaped((total, width), F32)
    rows_bf16 = shaped((total, width), BF16)
    wide = shaped((total, hidden), BF16)
    (
        unit,
        inverse,
        normed_q,
        active_own,
        active_other,
        factor_own,
        factor_other,
        output,
        grad_sum,
        grad_feed,
        sums,
    ) = call(
        middle_body,
        [
            rows_f32,
            shaped((total, 128), F32),
            rows_bf16,
            wide,
            wide,
            wide,
            wide,
            rows_bf16,
            rows_f32,
            rows_bf16,
            shaped((8, width), F32),
        ],
        (
            clip_scales,
            own_heads[3],
            other_heads[3],
            merge_own,
            merge_other,
            inputs,
            up_own,
            up_other,
            down_own,
            down_other,
            own_pack,
            other_pack,
            vectors,
            cotangent,
        ),
        [
            pltpu.VMEM((total, width), F32),
            pltpu.VMEM((total, 256), F32),
            pltpu.VMEM((total, 256), F32),
            pltpu.VMEM((3, 8, width), F32),
            pltpu.VMEM((3, 8, width), F32),
        ],
        in_specs=[SMEM] + [VMEM] * 13,
        out_specs=[VMEM] * 11,
        limit=32 << 20,
    )

    plan = Plan()
    chunk = shaped((blocks // 2, 2 * hidden // blocks, LANES), BF16)

    def down_half(which, half, active, grad):
        return call(
            partial(down_grad_body, which, half),
            chunk,
            (ids, active, grad),
            in_specs=[SMEM] + [VMEM] * 2,
            out_specs=VMEM,
            limit=9 << 20,
        )

    feed = plan.given("feed", grad_feed)
    down_tasks = {}
    for half, word in ((1, "high"), (0, "low")):
        for which, active in ((1, active_other), (0, active_own)):
            down_tasks[which, half] = plan.core(
                ("down.mine", "down.theirs")[which] + word,
                lambda grad, which=which, half=half, active=active: down_half(
                    which, half, active, grad
                ),
                [feed],
            )

    def take(index):
        return lambda values: values[index]

    def part(values, index):
        return values[index]

    def one(values, index):
        return [values[index]]

    down_out = plan.reduce(
        "down",
        exchange,
        (down_tasks[0, 1], down_tasks[0, 0]),
        (down_tasks[1, 1], down_tasks[1, 0]),
        lambda value, index: [value],
    )

    def up_half(body, which, grad, down, up, factor, *before):
        return call(
            partial(body, which),
            [chunk, chunk, shaped((1, hidden), F32), rows_f32],
            (ids, grad, down, up, factor, normed_q) + before,
            [pltpu.VMEM((total, hidden), BF16)],
            in_specs=[SMEM] + [VMEM] * (5 + len(before)),
            out_specs=[VMEM] * 4,
            limit=20 << 20,
        )

    up_theirs = plan.core(
        "up.theirs",
        lambda grad: up_half(
            up_grad_first_body, 1, grad, down_other, up_other, factor_other
        ),
        [feed],
    )
    up_mine = plan.core(
        "up.mine",
        lambda grad, before: up_half(
            up_grad_body, 0, grad, down_own, up_own, factor_own, before[3]
        ),
        [feed, up_theirs],
    )
    up_out = plan.reduce("up", exchange, (up_mine, up_mine), (up_theirs, up_theirs), one)

    small = shaped((16, width), F32)

    def norm_back(theirs, mine):
        ins = (clip_scales, mine[3], grad_sum, unit, inverse, vectors, sums, theirs[2], mine[2])
        return call(
            first_norm_back_body,
            [rows_f32, rows_bf16, small, small],
            ins,
            [pltpu.VMEM((3, 8, width), F32)],
            in_specs=[SMEM] + [VMEM] * 8,
            out_specs=[VMEM] * 4,
        )

    first_back = plan.core("norm", norm_back, [up_theirs, up_mine])

    def heads_back(which, back, heads, merge_q):
        count = (1, 4)[which]
        parts = [shaped((chunk.shape[0], chunk.shape[1] // count, LANES), BF16)] * count
        *outs, grads, row = call(
            partial(backward_heads_body, which),
            parts + parts + [shaped((3, LANES, total), BF16), shaped((8, 2 * LANES), F32)],
            (ids, row_lengths, xq, back[1]) + tuple(heads) + (merge_q,),
            [
                mask_scratch,
                pltpu.VMEM((LANES, total), BF16),
                pltpu.VMEM((width, total), BF16),
            ],
            in_specs=[SMEM] * 2 + [VMEM] * 8,
            out_specs=[VMEM] * (2 * count + 2),
            limit=18 << 20,
        )
        return outs[:count], outs[count:], grads, row

    heads_theirs = plan.core(
        "heads.theirs", lambda back: heads_back(1, back, other_heads, merge_other), [first_back]
    )
    heads_mine = plan.core(
        "heads.mine", lambda back: heads_back(0, back, own_heads, merge_own), [first_back]
    )
    rest_out = plan.reduce(
        "rest", exchange, (heads_mine, heads_mine), (heads_theirs, heads_theirs), part
    )

    def input_part(back, theirs, mine):
        return call(
            input_grad_body,
            rows_f32,
            (clip_scales, inputs, back[0], project_own, project_other, mine[2], theirs[2]),
            in_specs=[SMEM] + [VMEM] * 6,
            out_specs=VMEM,
            limit=16 << 20,
        )

    input_task = plan.core("input", input_part, [first_back, heads_theirs, heads_mine])

    def joined(sums_part, row):
        return jnp.concatenate([sums_part[:8], row[0:1], sums_part[12:15]], axis=0)

    small_row = lax.broadcasted_iota(jnp.int32, (12, width), 0)

    def merge_small(a, b):
        return jnp.where(small_row < 9, a + b, jnp.maximum(a, b))

    theirs_small = plan.core(
        "small.theirs", lambda back, heads: joined(back[2], heads[3]), [first_back, heads_theirs]
    )
    small_got = plan.send("small.got", theirs_small, exchange.core_swap)
    small_value = plan.core(
        "small.mine",
        lambda got, back, heads: merge_small(joined(back[3], heads[3]), got),
        [small_got, first_back, heads_mine],
    )
    for stage in range(exchange.bits):
        swap = partial(same_way.swap, stage=stage)
        small_in = plan.send(f"small.in{stage}", small_value, swap)
        small_value = plan.core(f"small.sum{stage}", merge_small, [small_value, small_in])

    final_steps = 4
    per = blocks // final_steps

    def final(body, parts, weights, specs, packs=()):
        part_specs = [pl.BlockSpec(part.shape, lambda i, s: (0, 0, 0)) for part in parts]
        pack = pl.BlockSpec((16, hidden), lambda i, s: (0, 0))
        ins = (ids, own_pack, other_pack) + tuple(parts) + tuple(packs) + weights
        return pl.pallas_call(
            partial(body, per),
            grid_spec=pltpu.PrefetchScalarGridSpec(
                num_scalar_prefetch=1,
                grid=(final_steps,),
                in_specs=[pack, pack]
                + part_specs
                + [pl.BlockSpec((16, LANES), lambda i, s: (0, 0))] * len(packs)
                + specs,
                out_specs=specs,
            ),
            out_shape=[shaped(weight.shape, F32) for weight in weights],
            compiler_params=pltpu.CompilerParams(vmem_limit_bytes=10 << 20),
            cost_estimate=pl.CostEstimate(flops=1, bytes_accessed=1, transcendentals=0),
        )(*ins)

    down_spec = pl.BlockSpec((hidden // final_steps, width), lambda i, s: (i, 0))
    plan.core(
        "down.final",
        lambda *parts: final(down_final_body, parts, (down_weight,), [down_spec])[0],
        down_out,
    )
    up_spec = pl.BlockSpec((width // final_steps, hidden), lambda i, s: (i, 0))
    plan.core(
        "up.final",
        lambda *parts: final(up_final_body, parts, (up_weight,), [up_spec])[0],
        up_out,
    )
    project_spec = pl.BlockSpec((3, width // final_steps, LANES), lambda i, s: (0, i, 0))
    merge_spec = pl.BlockSpec((LANES // final_steps, width), lambda i, s: (i, 0))
    plan.core(
        "rest.final",
        lambda *parts: final(
            rest_final_body,
            parts,
            (project, merge_weight),
            [project_spec, merge_spec],
            (project_own_pack, project_other_pack),
        ),
        rest_out,
    )
    values = plan.run()
    small_all = values[small_value]
    project_grad, merge_grad = values["rest.final"]
    peaks = small_all[9:12, 0]
    return (
        output,
        values[input_task],
        jnp.transpose(project_grad, (1, 0, 2)),
        merge_grad,
        values["up.final"],
        values["down.final"],
        small_all[8].reshape(2, LANES),
        small_all[4],
        small_all[6:8].reshape(hidden),
        small_all[5],
        small_all[0:2],
        small_all[2:4],
        DECAY * clip_scales + (1.0 - DECAY) * peaks,
    )


def solution(mesh):
    return jax.shard_map(
        local,
        mesh=mesh,
        in_specs=(
            P(("dp", "tensor"), None),
            P("dp"),
            P(None, None, "tensor"),
            P("tensor", None),
            P(None, "tensor"),
            P("tensor", None),
            P(None, "tensor"),
            P(),
            P("tensor"),
            P(),
            P(),
            P(),
            P(),
            P(("dp", "tensor"), None),
        ),
        out_specs=(
            P(("dp", "tensor"), None),
            P(("dp", "tensor"), None),
            P(None, None, "tensor"),
            P("tensor", None),
            P(None, "tensor"),
            P("tensor", None),
            P(None, "tensor"),
            P(),
            P("tensor"),
            P(),
            P(),
            P(),
            P(),
        ),
        check_vma=False,
    )
```

```python
from functools import partial

import jax
import jax.numpy as jnp
from jax import lax
from jax.experimental import pallas as pl
from jax.experimental.pallas import tpu as pltpu
from jax.sharding import PartitionSpec as P

HEAD = 64
LONG = 512
SHORT = 128
EPSILON = 1e-12
DECAY = 0.9
F32 = jnp.float32
BF16 = jnp.bfloat16
VMEM = pl.BlockSpec(memory_space=pltpu.VMEM)
SMEM = pl.BlockSpec(memory_space=pltpu.SMEM)
ORDER = (
    "down.theirshigh",
    "down.minehigh",
    "down.theirslow",
    "down.add0",
    "down.minelow",
    "up.theirs",
    "up.mine",
    "down.add1",
    "up.add0",
    "norm",
    "heads.theirs",
    "heads.mine",
    "down.add2",
    "up.add1",
    "rest.add0",
    "input",
    "down.add3",
    "small.theirs",
    "down.sum",
    "up.add2",
    "rest.add1",
    "small.mine",
    "down.join3",
    "up.add3",
    "rest.add2",
    "down.join2",
    "up.sum",
    "rest.add3",
    "small.sum0",
    "down.join1",
    "up.join3",
    "small.sum1",
    "rest.sum",
    "small.sum2",
    "up.join2",
    "rest.join3",
    "down.final",
    "rest.join2",
    "up.join1",
    "small.sum3",
    "rest.join1",
    "rest.half",
    "up.final",
    "rest.final",
)
COST = 1
LANES = 384
TILE = 128
GELU_TILE = 32


def dot(a, b, ca, cb):
    return lax.dot_general(a, b, (((ca,), (cb,)), ((), ())), preferred_element_type=F32)


def shaped(shape, dtype):
    return jax.ShapeDtypeStruct(shape, dtype)


def call(
    body, out_shape, ins, scratch=(), in_specs=None, out_specs=None, limit=None
):
    nbytes = sum(a.size * a.dtype.itemsize for a in ins)
    nbytes += sum(o.size * o.dtype.itemsize for o in jax.tree.leaves(out_shape))
    params = dict(
        out_shape=out_shape,
        compiler_params=pltpu.CompilerParams(vmem_limit_bytes=limit or (nbytes + (6 << 20))),
        cost_estimate=pl.CostEstimate(flops=1, bytes_accessed=COST, transcendentals=0),
    )
    return pl.pallas_call(
        body, in_specs=in_specs, out_specs=out_specs, scratch_shapes=list(scratch), **params
    )(*ins)


def peak(value):
    top = jnp.max(jnp.abs(value.astype(F32)), axis=0, keepdims=True)
    return jnp.max(top, axis=1, keepdims=True)


def raise_peaks(pack, tiles):
    for row, tile in enumerate(tiles):
        at = slice(8 + row, 9 + row)
        pack[at, :] = jnp.maximum(pack[at, :], peak(tile))


def project_peaks_body(project, qv_bias, pack):
    @pl.when(pl.program_id(0) == 0)
    def _():
        pack[...] = jnp.zeros_like(pack)
        pack[0:2, :] = qv_bias[...]

    raise_peaks(pack, [project[0], project[1], project[2]])


def rest_peaks_body(merge, up, down, up_bias, pack):
    @pl.when(pl.program_id(0) == 0)
    def _():
        pack[...] = jnp.zeros_like(pack)
        pack[0:1, :] = up_bias[...]

    raise_peaks(pack, [merge[...], up[...], down[...]])


def scale_row(own, other, row, width):
    at = slice(8 + row, 9 + row)
    return 0.5 * jnp.maximum(own[at, 0:width], other[at, 0:width])


def clip_tile(value, scale):
    return (scale * jnp.tanh(value.astype(F32) * (1.0 / scale))).astype(BF16)


def clip_project_body(own, other, project, out):
    for part in range(3):
        out[part] = clip_tile(project[part], scale_row(own, other, part, LANES))


def clip_rest_body(own, other, merge, up, down, merge_q, up_q, down_q):
    for row, (src, dst) in enumerate(((merge, merge_q), (up, up_q), (down, down_q))):
        dst[...] = clip_tile(src[...], scale_row(own, other, row, src.shape[1]))


def key_bias(lengths, first):
    key = lax.broadcasted_iota(jnp.int32, (LONG, 1), 0)
    query = lax.broadcasted_iota(jnp.int32, (1, LONG), 1)
    single = lengths[first] > SHORT
    limit = jnp.full((LONG, 1), lengths[first], jnp.int32)
    for slot in range(1, LONG // SHORT):
        own = jnp.where(single, lengths[first], slot * SHORT + lengths[first + slot])
        limit = jnp.where(key >= slot * SHORT, own, limit)
    key_row = jnp.where(single, 0, key // SHORT)
    query_row = jnp.where(single, 0, query // SHORT)
    key_row = jnp.where(key < limit, key_row, -1)
    return jnp.where(key_row == query_row, 0.0, -1e30).astype(F32)


def qkv_into(xq, weight, bias_pack, q_ref, k_ref, v_ref):
    for part, ref in enumerate((q_ref, k_ref, v_ref)):
        value = dot(xq, weight[part], 1, 0)
        if part == 0:
            value = value + bias_pack[0:1, :]
        if part == 2:
            value = value + bias_pack[1:2, :]
        value = value.astype(BF16)
        if part == 0:
            value = value * jnp.asarray(0.125, BF16)
        ref[...] = value.T


def attend(lengths, first, q_ref, k_ref, v_ref, c_ref, lse_ref, bias_ref):
    bias_ref[...] = key_bias(lengths, first)

    def head(index, carry):
        at = pl.ds(pl.multiple_of(index * HEAD, HEAD), HEAD)
        scores = dot(k_ref[at, :], q_ref[at, :], 0, 0) + bias_ref[...]
        top = jnp.max(scores, axis=0, keepdims=True)
        prob = jnp.exp(scores - top)
        total = jnp.sum(prob, axis=0, keepdims=True)
        mixed = dot(v_ref[at, :], prob.astype(BF16), 1, 0)
        c_ref[at, :] = (mixed * (1.0 / total)).astype(BF16)
        lse_ref[pl.ds(index, 1), :] = top + jnp.log(total)
        return carry

    lax.fori_loop(0, q_ref.shape[0] // HEAD, head, 0, unroll=1)


def forward_first_body(
    ids, lengths, clips, inputs, weight, pack, xq, q_ref, k_ref, v_ref, c_ref, lse_ref, bias_ref
):
    scale = clips[0]
    xq[...] = clip_tile(inputs[...], scale)
    qkv_into(xq[...], weight, pack, q_ref, k_ref, v_ref)
    attend(lengths, ids[2], q_ref, k_ref, v_ref, c_ref, lse_ref, bias_ref)


def forward_second_body(
    ids, lengths, xq, weight, pack, q_ref, k_ref, v_ref, c_ref, lse_ref, bias_ref
):
    qkv_into(xq[...], weight, pack, q_ref, k_ref, v_ref)
    attend(lengths, ids[2], q_ref, k_ref, v_ref, c_ref, lse_ref, bias_ref)


def backward_heads_body(
    which,
    ids,
    lengths,
    xq,
    grad_branch,
    q_ref,
    k_ref,
    v_ref,
    c_ref,
    lse_ref,
    merge_q,
    *refs,
):
    *outs, d_ref, qv_row, bias_ref, g_ref, x_t = refs
    bias_ref[...] = key_bias(lengths, ids[2])
    x_t[...] = xq[...].T
    count, rel = outs[0].shape[0], ids[which]
    width = q_ref.shape[0]
    g_ref[...] = dot(merge_q[...], grad_branch[...], 1, 1).astype(BF16)

    def head(index, carry):
        at = pl.ds(pl.multiple_of(index * HEAD, HEAD), HEAD)
        q, k, v, g = q_ref[at, :], k_ref[at, :], v_ref[at, :], g_ref[at, :]
        scores = dot(k, q, 0, 0) + bias_ref[...]
        prob = jnp.exp(scores - lse_ref[pl.ds(index, 1), :])
        grad_prob = dot(v, g, 0, 0)
        inner = jnp.sum(g.astype(F32) * c_ref[at, :].astype(F32), axis=0, keepdims=True)
        grad_score = (prob * (grad_prob - inner)).astype(BF16)
        d_ref[2, at, :] = dot(g, prob.astype(BF16), 1, 1).astype(BF16)
        d_ref[0, at, :] = (dot(k, grad_score, 1, 0) * 0.125).astype(BF16)
        d_ref[1, at, :] = dot(q, grad_score, 1, 1).astype(BF16)
        return carry

    lax.fori_loop(0, width // HEAD, head, 0, unroll=1)
    rows, step = x_t.shape[0] // (2 * count), width // (2 * count)
    if len(outs) == 2:
        outs = [out.at[:, at * rows : (at + 1) * rows, :] for out in outs for at in range(4)]
    for half, parts in ((1, outs[:4]), (0, outs[4:])):
        base = half_base(rel, half, 2 * count)
        at = pl.ds(pl.multiple_of(base * rows, count * rows), count * rows)
        for part in range(3):
            grad = dot(x_t[at, :], d_ref[part], 1, 1).astype(BF16)
            for block in range(count):
                to = ((base + block) ^ rel) % count
                piece = grad[block * rows : (block + 1) * rows, :]
                parts[part][to] = piece
        at = pl.ds(pl.multiple_of(base * step, count * step), count * step)
        grad = dot(c_ref[at, :], grad_branch[...], 1, 0)
        for block in range(count):
            to = ((base + block) ^ rel) % count
            piece = grad[block * step : (block + 1) * step, :]
            piece = jnp.concatenate([piece[:, :width], piece[:, width:]], axis=0)
            parts[3][to] = piece.astype(BF16)
    ones = jnp.ones((8, xq.shape[0]), BF16)
    qv_row[:, 0:width] = dot(ones, d_ref[0], 1, 1)
    qv_row[:, width : 2 * width] = dot(ones, d_ref[2], 1, 1)


def gelu_parts(hidden, scale):
    area = 0.5 + 0.5 * lax.erf(hidden * 0.7071067811865476)
    bell = jnp.exp(-0.5 * hidden * hidden)
    active = hidden * area
    slope = area + hidden * bell * 0.3989422804014327
    bent = jnp.tanh(active * (1.0 / scale))
    return (scale * bent).astype(BF16), ((1.0 - bent * bent) * slope).astype(BF16), active


def fold(value, op):
    rows, lanes = value.shape
    return op(value.reshape(rows // 8, 8, lanes), axis=0)


def middle_body(
    clips,
    c_own,
    c_other,
    merge_own,
    merge_other,
    inputs,
    up_own,
    up_other,
    down_own,
    down_other,
    pack_own,
    pack_other,
    vectors,
    cotangent,
    unit_out,
    inverse_out,
    normed_q,
    active_own,
    active_other,
    factor_own,
    factor_other,
    output,
    grad_sum,
    grad_feed,
    sums,
    work,
    hidden_ref,
    second_ref,
    tops,
    sum_ref,
):
    total = inputs.shape[0]
    work[...] = dot(c_own[...], merge_own[...], 0, 0) + dot(c_other[...], merge_other[...], 0, 0)
    tops[...] = jnp.zeros_like(tops)
    sum_ref[...] = jnp.zeros_like(sum_ref)
    clip_first, clip_second = clips[1], clips[2]

    def first_norm(index, carry):
        at = pl.ds(pl.multiple_of(index * TILE, TILE), TILE)
        rows = inputs[at, :].astype(F32)
        value = rows + work[at, :] + vectors[0:1, :]
        mean = jnp.mean(value, axis=-1, keepdims=True)
        centred = value - mean
        inverse = lax.rsqrt(jnp.mean(centred * centred, axis=-1, keepdims=True) + EPSILON)
        unit = centred * inverse
        normed = unit * vectors[2:3, :] + vectors[4:5, :]
        unit_out[at, :] = unit
        inverse_out[at, :] = jnp.broadcast_to(inverse, (TILE, 128))
        normed_q[at, :] = clip_tile(normed, clip_first)
        tops[0] = jnp.maximum(tops[0], fold(jnp.abs(rows), jnp.max))
        tops[1] = jnp.maximum(tops[1], fold(jnp.abs(normed), jnp.max))
        work[at, :] = normed
        return carry

    lax.fori_loop(0, total // TILE, first_norm, 0)
    span = hidden_ref.shape[1]
    for weight, pack, active_ref, factor_ref in (
        (up_own, pack_own, active_own, factor_own),
        (up_other, pack_other, active_other, factor_other),
    ):

        def gelu_chunk(source, index):
            cols = pl.ds(pl.multiple_of(index * span, span), span)
            bias = pack[0:1, cols]
            top = tops[2, :, 0:span]
            for row in range(total // GELU_TILE):
                at = slice(row * GELU_TILE, (row + 1) * GELU_TILE)
                clipped, factor, active = gelu_parts(source[at, :] + bias, clip_second)
                active_ref[at, cols] = clipped
                factor_ref[at, cols] = factor
                top = jnp.maximum(top, fold(jnp.abs(active), jnp.max))
            tops[2, :, 0:span] = top

        def multiply(target, index):
            cols = pl.ds(pl.multiple_of(index * span, span), span)
            target[...] = dot(normed_q[...], weight[:, cols], 1, 0)

        chunks = weight.shape[1] // span
        multiply(hidden_ref, 0)

        def pair(index, carry):
            multiply(second_ref, 2 * index + 1)
            gelu_chunk(hidden_ref, 2 * index)
            multiply(hidden_ref, jnp.minimum(2 * index + 2, chunks - 1))
            gelu_chunk(second_ref, 2 * index + 1)
            return carry

        lax.fori_loop(0, chunks // 2, pair, 0)
    work[...] += dot(active_own[...], down_own[...], 1, 0) + dot(
        active_other[...], down_other[...], 1, 0
    )

    def second_norm(index, carry):
        at = pl.ds(pl.multiple_of(index * TILE, TILE), TILE)
        value = work[at, :] + vectors[1:2, :]
        mean = jnp.mean(value, axis=-1, keepdims=True)
        centred = value - mean
        inverse = lax.rsqrt(jnp.mean(centred * centred, axis=-1, keepdims=True) + EPSILON)
        unit = centred * inverse
        output[at, :] = (unit * vectors[3:4, :] + vectors[5:6, :]).astype(BF16)
        upstream = cotangent[at, :].astype(F32)
        scaled = upstream * vectors[3:4, :]
        grad = inverse * (
            scaled
            - jnp.mean(scaled, axis=-1, keepdims=True)
            - unit * jnp.mean(scaled * unit, axis=-1, keepdims=True)
        )
        grad_sum[at, :] = grad
        grad_feed[at, :] = grad.astype(BF16)
        sum_ref[0] += fold(upstream * unit, jnp.sum)
        sum_ref[1] += fold(upstream, jnp.sum)
        sum_ref[2] += fold(grad, jnp.sum)
        return carry

    lax.fori_loop(0, total // TILE, second_norm, 0)
    for row in range(3):
        sums[row : row + 1, :] = jnp.sum(sum_ref[row], axis=0, keepdims=True)
    for row in range(3):
        top = jnp.max(jnp.max(tops[row], axis=0, keepdims=True), axis=1, keepdims=True)
        sums[3 + row : 4 + row, :] = jnp.broadcast_to(top, (1, sums.shape[1]))
    sums[6:8, :] = jnp.zeros((2, sums.shape[1]), F32)


def half_base(rel, half, blocks):
    return (half ^ (rel // (blocks // 2))) * (blocks // 2)


def down_grad_body(which, half, ids, active, grad_feed, chunk):
    rel = ids[which]
    count = chunk.shape[0]
    rows = active.shape[1] // (2 * count)
    base = half_base(rel, half, 2 * count)
    per = count // 2
    for tile in range(2):
        first = base + tile * per
        cols = pl.ds(pl.multiple_of(first * rows, per * rows), per * rows)
        grad = dot(active[:, cols], grad_feed[...], 0, 0)
        for block in range(per):
            piece = grad[block * rows : (block + 1) * rows, :].astype(BF16)
            to = ((first + block) ^ rel) % count
            chunk[to, 0:rows, :] = piece[:, :LANES]
            chunk[to, rows : 2 * rows, :] = piece[:, LANES:]


def up_grad_body(
    which, ids, grad_feed, down, up, factor, normed_q, before, high, low, bias_row, grad_normed, g_ref
):
    rel = ids[which]
    count = high.shape[0]
    span = 512

    def columns(index, carry):
        cols = pl.ds(pl.multiple_of(index * span, span), span)
        grad = dot(grad_feed[...], down[cols, :], 1, 1) * factor[:, cols].astype(F32)
        grad = grad.astype(BF16)
        g_ref[:, cols] = grad
        bias_row[0:1, cols] = jnp.sum(grad.astype(F32), axis=0, keepdims=True)
        return carry

    lax.fori_loop(0, g_ref.shape[1] // span, columns, 0)
    rows = normed_q.shape[1] // (2 * count)
    for half, chunk in ((1, high), (0, low)):
        base = half_base(rel, half, 2 * count)
        cols = pl.ds(pl.multiple_of(base * rows, count * rows), count * rows)
        grad = dot(normed_q[:, cols], g_ref[...], 0, 0)
        for block in range(count):
            to = ((base + block) ^ rel) % count
            for part in range(grad.shape[1] // LANES):
                piece = grad[block * rows : (block + 1) * rows, part * LANES : (part + 1) * LANES]
                chunk[to, part * rows : (part + 1) * rows, :] = piece.astype(BF16)
    result = dot(g_ref[...], up[...], 1, 1)
    if before is not None:
        result = result + before[...]
    grad_normed[...] = result


def up_grad_first_body(which, ids, grad_feed, down, up, factor, normed_q, *outs):
    up_grad_body(which, ids, grad_feed, down, up, factor, normed_q, None, *outs)


def first_norm_back_body(
    clips,
    grad_normed,
    grad_sum,
    unit_ref,
    inverse_ref,
    vectors,
    sums,
    bias_other,
    bias_own,
    grad_first,
    grad_branch,
    pack_other,
    pack_own,
    sum_ref,
):
    clip_first = clips[1]
    sum_ref[...] = jnp.zeros_like(sum_ref)

    def rows(index, carry):
        at = pl.ds(pl.multiple_of(index * TILE, TILE), TILE)
        unit = unit_ref[at, :]
        bent = jnp.tanh((unit * vectors[2:3, :] + vectors[4:5, :]) * (1.0 / clip_first))
        grad = grad_normed[at, :] * (1.0 - bent * bent) + grad_sum[at, :]
        scaled = grad * vectors[2:3, :]
        back = inverse_ref[at, 0:1] * (
            scaled
            - jnp.mean(scaled, axis=-1, keepdims=True)
            - unit * jnp.mean(scaled * unit, axis=-1, keepdims=True)
        )
        grad_first[at, :] = back
        grad_branch[at, :] = back.astype(BF16)
        sum_ref[0] += fold(grad * unit, jnp.sum)
        sum_ref[1] += fold(grad, jnp.sum)
        sum_ref[2] += fold(back, jnp.sum)
        return carry

    lax.fori_loop(0, unit_ref.shape[0] // TILE, rows, 0)
    width = unit_ref.shape[1]
    for pack, bias in ((pack_other, bias_other), (pack_own, bias_own)):
        pack[...] = jnp.zeros_like(pack)
        for row, source in ((0, 0), (2, 1), (4, 2)):
            pack[row : row + 1, :] = jnp.sum(sum_ref[source], axis=0, keepdims=True)
        pack[1:2, :] = sums[0:1, :]
        pack[3:4, :] = sums[1:2, :]
        pack[5:6, :] = sums[2:3, :]
        pack[6:7, :] = bias[0:1, 0:width]
        pack[7:8, :] = bias[0:1, width : 2 * width]
        pack[12:15, :] = sums[3:6, :]


def input_grad_body(clips, inputs, grad_first, w_own, w_other, d_own, d_other, out):
    terms = []
    for d_ref, weight in ((d_own, w_own), (d_other, w_other)):
        for part in range(3):
            terms.append(dot(d_ref[part], weight[part], 0, 1))
    bent = jnp.tanh(inputs[...].astype(F32) * (1.0 / clips[0]))
    out[...] = sum(terms[1:], terms[0]) * (1.0 - bent * bent) + grad_first[...]


def slope_of(weight, scale):
    bent = jnp.tanh(weight.astype(F32) * (1.0 / scale))
    return 1.0 - bent * bent


def block_value(rel, low, high, at):
    half = low.shape[0]
    at = at ^ rel
    first = low[jnp.minimum(at, half - 1)].astype(F32)
    return jnp.where(at < half, first, high[jnp.maximum(at - half, 0)].astype(F32))


def down_final_body(per, ids, own, other, low, high, weight, out):
    rows = weight.shape[0] // per
    slope = slope_of(weight[...], scale_row(own, other, 2, weight.shape[1]))
    for index in range(per):
        value = block_value(ids[0], low, high, pl.program_id(0) * per + index)
        at = slice(index * rows, (index + 1) * rows)
        out[at, :LANES] = value[:rows] * slope[at, :LANES]
        out[at, LANES:] = value[rows:] * slope[at, LANES:]


def up_final_body(per, ids, own, other, low, high, weight, out):
    rows = weight.shape[0] // per
    slope = slope_of(weight[...], scale_row(own, other, 1, weight.shape[1]))
    for index in range(per):
        value = block_value(ids[0], low, high, pl.program_id(0) * per + index)
        at = slice(index * rows, (index + 1) * rows)
        for part in range(weight.shape[1] // LANES):
            cols = slice(part * LANES, (part + 1) * LANES)
            out[at, cols] = value[part * rows : (part + 1) * rows] * slope[at, cols]


def rest_final_body(half, per, ids, own, other, chunk, p_own, p_other, project, merge, *refs):
    project_out, merge_out = refs[-2:]
    rows, step = project.shape[1] // per, merge.shape[0] // per
    count = chunk.shape[0]
    first = half_base(ids[0], half, 2 * count) + pl.program_id(0) * per
    values = []
    for index in range(per):
        values.append(chunk[((first + index) ^ ids[0]) % count].astype(F32))
    for part in range(3):
        slope = slope_of(project[part], scale_row(p_own, p_other, part, LANES))
        for index in range(per):
            at = slice(index * rows, (index + 1) * rows)
            project_out[part, at, :] = values[index][part * rows : (part + 1) * rows] * slope[at]
    slope = slope_of(merge[...], scale_row(own, other, 0, merge.shape[1]))
    for part in range(2):
        across = slice(part * LANES, (part + 1) * LANES)
        piece = [v[3 * rows + part * step : 3 * rows + (part + 1) * step] for v in values]
        merge_out[:, across] = jnp.concatenate(piece, axis=0) * slope[:, across]


class Exchange:
    def __init__(self, size, first):
        self.bits = size.bit_length() - 1
        assert 1 << self.bits == size and self.bits >= 4
        self.size = size
        self.orders = [list(order) + list(range(4, self.bits)) for order in first]
        self.blocks = 16

    def relative(self, position, core):
        total = 0
        for stage in range(4):
            bit = (position >> self.orders[core][stage]) & 1
            total = total + (bit << (3 - stage))
        return total

    def swap(self, value, stage):
        pairs = []
        for index in range(self.size):
            for core in range(2):
                to = index ^ (1 << self.orders[core][stage])
                pairs.append((2 * index + core, 2 * to + core))
        return lax.ppermute(value, ("dp", "tensor"), pairs)

    def core_swap(self, value):
        return lax.ppermute(value, "tensor", [(0, 1), (1, 0)])


class Task:
    def __init__(self, body, deps):
        self.body, self.deps, self.sends = body, list(deps), []


class Plan:
    def __init__(self):
        self.tasks = {}
        self.values = {}
        self.source = {}

    def given(self, name, value):
        self.values[name] = value
        return name

    def core(self, name, body, deps):
        self.tasks[name] = Task(body, deps)
        return name

    def send(self, name, source, body):
        self.tasks[source].sends.append((name, body))
        self.source[name] = source
        return name

    def run(self):
        values, last = dict(self.values), None

        def take(name):
            nonlocal last
            if name in values:
                return
            if name in self.source:
                take(self.source[name])
                return
            task = self.tasks[name]
            for dep in task.deps:
                take(dep)
            inputs = [values[dep] for dep in task.deps]
            if last is not None:
                inputs, last = lax.optimization_barrier((inputs, last))
            with jax.named_scope(name.replace(".", "_")):
                result = task.body(*inputs)
            values[name] = result
            last = jax.tree.leaves(result)[0]
            for sent, body in task.sends:
                with jax.named_scope(sent.replace(".", "_")):
                    values[sent] = body(result)

        for name in ORDER:
            if name in self.tasks:
                take(name)
            elif name[1:] in self.source:
                take(name[1:])
                values[name[1:]], last = lax.optimization_barrier((values[name[1:]], last))
        for name in self.tasks:
            take(name)
        return values

    def swap(self, name, source, way, stage, pick=lambda value: value):
        return self.send(name, source, lambda value: way.swap(pick(value), stage))

    def reduce(self, name, way, mine, theirs, pick):
        def swapped(index):
            return lambda v: [way.core_swap(value) for value in pick(v, index)]

        def whole(values):
            return values[0] if len(values) == 1 else jnp.concatenate(values, axis=1)

        high = self.send(name + ".high", theirs[0], swapped(0))
        low = self.send(name + ".low", theirs[1], swapped(1))
        value = self.core(
            f"{name}.add0",
            lambda mine, high: total([whole(pick(mine, 0)), whole(high)]),
            [mine[0], high],
        )
        got = self.swap(f"{name}.in0", value, way, 0)

        def second(mine, low, got):
            return split_in_two([whole(pick(mine, 1)), whole(low), got])

        def more(kept, got):
            return split_in_two([kept[0], got])

        value = self.core(f"{name}.add1", second, [mine[1], low, got])
        for stage in (1, 2, 3):
            got = self.swap(f"{name}.in{stage}", value, way, stage, second_of)
            if stage < 3:
                value = self.core(f"{name}.add{stage + 1}", more, [value, got])
        value = self.core(f"{name}.sum", lambda kept, got: total([kept[0], got]), [value, got])
        for stage in range(4, way.bits):
            sent = self.swap(f"{name}.in{stage}", value, way, stage)
            value = self.core(f"{name}.sum{stage}", lambda a, b: total([a, b]), [value, sent])
        for stage in reversed(range(4)):
            sent = self.swap(f"{name}.out{stage}", value, way, stage)
            if stage > 0:
                value = self.core(
                    f"{name}.join{stage}",
                    lambda a, b: jnp.concatenate([a, b], axis=0),
                    [value, sent],
                )
        return [value, sent]


def total(values):
    out = values[0].astype(F32)
    for value in values[1:]:
        out = out + value.astype(F32)
    return out.astype(BF16)


def split_in_two(values):
    half = values[0].shape[0] // 2
    return total([value[:half] for value in values]), total([value[half:] for value in values])


def second_of(value):
    return value[1]


def local(
    inputs,
    row_lengths,
    project_weight,
    merge_weight,
    up_weight,
    down_weight,
    query_value_bias,
    merge_bias,
    up_bias,
    down_bias,
    norm_gains,
    norm_shifts,
    clip_scales,
    cotangent,
):
    size = lax.axis_size("dp")
    exchange = Exchange(size, ((0, 1, 2, 3), (1, 0, 2, 3)))
    same_way = Exchange(size, ((0, 1, 2, 3), (0, 1, 2, 3)))
    blocks = exchange.blocks
    member = lax.axis_index("tensor")
    place = lax.axis_index("dp")
    rel0, rel1 = exchange.relative(place, 0), exchange.relative(place, 1)
    own_rel = jnp.where(member == 0, rel0, rel1)
    other_rel = jnp.where(member == 0, rel1, rel0)
    ids = jnp.stack([own_rel, other_rel, member * (LONG // SHORT)]).astype(jnp.int32)
    total, width = inputs.shape
    hidden = up_weight.shape[1]
    project = jnp.transpose(project_weight, (1, 0, 2))

    steps = 4
    small_grid = pltpu.CompilerParams(vmem_limit_bytes=12 << 20)
    project_block = pl.BlockSpec((3, width // steps, LANES), lambda i: (0, i, 0))
    rest_blocks = [
        pl.BlockSpec((LANES // steps, width), lambda i: (i, 0)),
        pl.BlockSpec((width // steps, hidden), lambda i: (i, 0)),
        pl.BlockSpec((hidden // steps, width), lambda i: (i, 0)),
    ]
    project_pack_spec = pl.BlockSpec((16, LANES), lambda i: (0, 0))
    pack_spec = pl.BlockSpec((16, hidden), lambda i: (0, 0))
    rest_weights = (merge_weight, up_weight, down_weight)

    def project_peaks():
        return pl.pallas_call(
            project_peaks_body,
            grid=(steps,),
            in_specs=[project_block, pl.BlockSpec((2, LANES), lambda i: (0, 0))],
            out_specs=project_pack_spec,
            out_shape=shaped((16, LANES), F32),
            compiler_params=small_grid,
        )(project, query_value_bias)

    def rest_peaks(weights):
        return pl.pallas_call(
            rest_peaks_body,
            grid=(steps,),
            in_specs=rest_blocks + [pl.BlockSpec((1, hidden), lambda i: (0, 0))],
            out_specs=pack_spec,
            out_shape=shaped((16, hidden), F32),
            compiler_params=small_grid,
        )(*weights, up_bias[None])

    def clip_project(own, other):
        return pl.pallas_call(
            clip_project_body,
            grid=(steps,),
            in_specs=[project_pack_spec, project_pack_spec, project_block],
            out_specs=project_block,
            out_shape=shaped(project.shape, BF16),
            compiler_params=small_grid,
        )(own, other, project)

    def clip_rest(own, other):
        return pl.pallas_call(
            clip_rest_body,
            grid=(steps,),
            in_specs=[pack_spec, pack_spec] + rest_blocks,
            out_specs=rest_blocks,
            out_shape=[shaped(a.shape, BF16) for a in rest_weights],
            compiler_params=small_grid,
        )(own, other, *rest_weights)

    project_own_pack = project_peaks()
    project_other_pack = exchange.core_swap(project_own_pack)
    project_own = clip_project(project_own_pack, project_other_pack)
    project_other = exchange.core_swap(project_own)
    tied, project_own = lax.optimization_barrier((rest_weights, project_own))
    own_pack = rest_peaks(tied)
    other_pack = exchange.core_swap(own_pack)
    other_pack, project_other = lax.optimization_barrier((other_pack, project_other))
    merge_own, up_own, down_own = clip_rest(own_pack, other_pack)
    merge_other = exchange.core_swap(merge_own)
    up_other = exchange.core_swap(up_own)
    down_other = exchange.core_swap(down_own)
    project_own, merge_own = lax.optimization_barrier((project_own, merge_own))

    head_shape = shaped((LANES, total), BF16)
    heads_out = [head_shape] * 4 + [shaped((8, total), F32)]
    mask_scratch = pltpu.VMEM((LONG, LONG), F32)
    xq, *own_heads = call(
        forward_first_body,
        [shaped((total, width), BF16)] + heads_out,
        (ids, row_lengths, clip_scales, inputs, project_own, project_own_pack),
        [mask_scratch],
        in_specs=[SMEM] * 3 + [VMEM] * 3,
        out_specs=[VMEM] * 6,
        limit=16 << 20,
    )
    other_heads = call(
        forward_second_body,
        heads_out,
        (ids, row_lengths, xq, project_other, project_other_pack),
        [mask_scratch],
        in_specs=[SMEM] * 2 + [VMEM] * 3,
        out_specs=[VMEM] * 5,
        limit=16 << 20,
    )

    vectors = jnp.concatenate([merge_bias[None], down_bias[None], norm_gains, norm_shifts], axis=0)
    rows_f32 = shaped((total, width), F32)
    rows_bf16 = shaped((total, width), BF16)
    wide = shaped((total, hidden), BF16)
    (
        unit,
        inverse,
        normed_q,
        active_own,
        active_other,
        factor_own,
        factor_other,
        output,
        grad_sum,
        grad_feed,
        sums,
    ) = call(
        middle_body,
        [
            rows_f32,
            shaped((total, 128), F32),
            rows_bf16,
            wide,
            wide,
            wide,
            wide,
            rows_bf16,
            rows_f32,
            rows_bf16,
            shaped((8, width), F32),
        ],
        (
            clip_scales,
            own_heads[3],
            other_heads[3],
            merge_own,
            merge_other,
            inputs,
            up_own,
            up_other,
            down_own,
            down_other,
            own_pack,
            other_pack,
            vectors,
            cotangent,
        ),
        [
            pltpu.VMEM((total, width), F32),
            pltpu.VMEM((total, 256), F32),
            pltpu.VMEM((total, 256), F32),
            pltpu.VMEM((3, 8, width), F32),
            pltpu.VMEM((3, 8, width), F32),
        ],
        in_specs=[SMEM] + [VMEM] * 13,
        out_specs=[VMEM] * 11,
        limit=32 << 20,
    )

    plan = Plan()
    chunk = shaped((blocks // 2, 2 * hidden // blocks, LANES), BF16)

    def down_half(which, half, active, grad):
        return call(
            partial(down_grad_body, which, half),
            chunk,
            (ids, active, grad),
            in_specs=[SMEM] + [VMEM] * 2,
            out_specs=VMEM,
            limit=9 << 20,
        )

    feed = plan.given("feed", grad_feed)
    down_tasks = {}
    for half, word in ((1, "high"), (0, "low")):
        for which, active in ((1, active_other), (0, active_own)):
            down_tasks[which, half] = plan.core(
                ("down.mine", "down.theirs")[which] + word,
                lambda grad, which=which, half=half, active=active: down_half(
                    which, half, active, grad
                ),
                [feed],
            )

    def take(index):
        return lambda values: values[index]

    def part(values, index):
        return values[index]

    def one(values, index):
        return [values[index]]

    down_out = plan.reduce(
        "down",
        exchange,
        (down_tasks[0, 1], down_tasks[0, 0]),
        (down_tasks[1, 1], down_tasks[1, 0]),
        lambda value, index: [value],
    )

    def up_half(body, which, grad, down, up, factor, *before):
        return call(
            partial(body, which),
            [chunk, chunk, shaped((1, hidden), F32), rows_f32],
            (ids, grad, down, up, factor, normed_q) + before,
            [pltpu.VMEM((total, hidden), BF16)],
            in_specs=[SMEM] + [VMEM] * (5 + len(before)),
            out_specs=[VMEM] * 4,
            limit=20 << 20,
        )

    up_theirs = plan.core(
        "up.theirs",
        lambda grad: up_half(
            up_grad_first_body, 1, grad, down_other, up_other, factor_other
        ),
        [feed],
    )
    up_mine = plan.core(
        "up.mine",
        lambda grad, before: up_half(
            up_grad_body, 0, grad, down_own, up_own, factor_own, before[3]
        ),
        [feed, up_theirs],
    )
    up_out = plan.reduce("up", exchange, (up_mine, up_mine), (up_theirs, up_theirs), one)

    small = shaped((16, width), F32)

    def norm_back(theirs, mine):
        ins = (clip_scales, mine[3], grad_sum, unit, inverse, vectors, sums, theirs[2], mine[2])
        return call(
            first_norm_back_body,
            [rows_f32, rows_bf16, small, small],
            ins,
            [pltpu.VMEM((3, 8, width), F32)],
            in_specs=[SMEM] + [VMEM] * 8,
            out_specs=[VMEM] * 4,
        )

    first_back = plan.core("norm", norm_back, [up_theirs, up_mine])

    def heads_back(which, back, heads, merge_q):
        count = (1, 4)[which]
        parts = [shaped((chunk.shape[0], chunk.shape[1] // count, LANES), BF16)] * count
        *outs, grads, row = call(
            partial(backward_heads_body, which),
            parts + parts + [shaped((3, LANES, total), BF16), shaped((8, 2 * LANES), F32)],
            (ids, row_lengths, xq, back[1]) + tuple(heads) + (merge_q,),
            [
                mask_scratch,
                pltpu.VMEM((LANES, total), BF16),
                pltpu.VMEM((width, total), BF16),
            ],
            in_specs=[SMEM] * 2 + [VMEM] * 8,
            out_specs=[VMEM] * (2 * count + 2),
            limit=18 << 20,
        )
        return outs[:count], outs[count:], grads, row

    heads_theirs = plan.core(
        "heads.theirs", lambda back: heads_back(1, back, other_heads, merge_other), [first_back]
    )
    heads_mine = plan.core(
        "heads.mine", lambda back: heads_back(0, back, own_heads, merge_own), [first_back]
    )
    rest_out = plan.reduce(
        "rest", exchange, (heads_mine, heads_mine), (heads_theirs, heads_theirs), part
    )

    def input_part(back, theirs, mine):
        return call(
            input_grad_body,
            rows_f32,
            (clip_scales, inputs, back[0], project_own, project_other, mine[2], theirs[2]),
            in_specs=[SMEM] + [VMEM] * 6,
            out_specs=VMEM,
            limit=16 << 20,
        )

    input_task = plan.core("input", input_part, [first_back, heads_theirs, heads_mine])

    def joined(sums_part, row):
        return jnp.concatenate([sums_part[:8], row[0:1], sums_part[12:15]], axis=0)

    small_row = lax.broadcasted_iota(jnp.int32, (12, width), 0)

    def merge_small(a, b):
        return jnp.where(small_row < 9, a + b, jnp.maximum(a, b))

    theirs_small = plan.core(
        "small.theirs", lambda back, heads: joined(back[2], heads[3]), [first_back, heads_theirs]
    )
    small_got = plan.send("small.got", theirs_small, exchange.core_swap)
    small_value = plan.core(
        "small.mine",
        lambda got, back, heads: merge_small(joined(back[3], heads[3]), got),
        [small_got, first_back, heads_mine],
    )
    for stage in range(exchange.bits):
        swap = partial(same_way.swap, stage=stage)
        small_in = plan.send(f"small.in{stage}", small_value, swap)
        small_value = plan.core(f"small.sum{stage}", merge_small, [small_value, small_in])

    final_steps = 4
    per = blocks // final_steps

    def final(body, parts, weights, specs):
        part_specs = [pl.BlockSpec(part.shape, lambda i, s: (0, 0, 0)) for part in parts]
        pack = pl.BlockSpec((16, hidden), lambda i, s: (0, 0))
        ins = (ids, own_pack, other_pack) + tuple(parts) + weights
        return pl.pallas_call(
            partial(body, per),
            grid_spec=pltpu.PrefetchScalarGridSpec(
                num_scalar_prefetch=1,
                grid=(final_steps,),
                in_specs=[pack, pack]
                + part_specs
                + specs,
                out_specs=specs,
            ),
            out_shape=[shaped(weight.shape, F32) for weight in weights],
            compiler_params=pltpu.CompilerParams(vmem_limit_bytes=10 << 20),
            cost_estimate=pl.CostEstimate(flops=1, bytes_accessed=1, transcendentals=0),
        )(*ins)

    down_spec = pl.BlockSpec((hidden // final_steps, width), lambda i, s: (i, 0))
    plan.core(
        "down.final",
        lambda *parts: final(down_final_body, parts, (down_weight,), [down_spec])[0],
        down_out,
    )
    up_spec = pl.BlockSpec((width // final_steps, hidden), lambda i, s: (i, 0))
    plan.core(
        "up.final",
        lambda *parts: final(up_final_body, parts, (up_weight,), [up_spec])[0],
        up_out,
    )

    def rest_final(half, chunk, *before):
        before = tuple(before[0]) if before else ()

        def place(i, s):
            return (half ^ (s[0] // (blocks // 2))) * (final_steps // 2) + i

        specs = [
            pl.BlockSpec((3, width // final_steps, LANES), lambda i, s: (0, place(i, s), 0)),
            pl.BlockSpec((LANES // final_steps, width), lambda i, s: (place(i, s), 0)),
        ]
        weights = (project, merge_weight)
        packs = (project_own_pack, project_other_pack)
        ins = (ids, own_pack, other_pack, chunk) + packs + weights
        pack = pl.BlockSpec((16, hidden), lambda i, s: (0, 0))
        narrow = pl.BlockSpec((16, LANES), lambda i, s: (0, 0))
        return pl.pallas_call(
            partial(rest_final_body, half, per),
            grid_spec=pltpu.PrefetchScalarGridSpec(
                num_scalar_prefetch=1,
                grid=(final_steps // 2,),
                in_specs=[pack, pack, pl.BlockSpec(chunk.shape, lambda i, s: (0, 0, 0))]
                + [narrow, narrow]
                + specs
                + [pl.BlockSpec(memory_space=pl.ANY)] * len(before),
                out_specs=specs,
            ),
            out_shape=[shaped(weight.shape, F32) for weight in weights],
            input_output_aliases={len(ins) + at: at for at in range(len(before))},
            compiler_params=pltpu.CompilerParams(vmem_limit_bytes=10 << 20),
            cost_estimate=pl.CostEstimate(flops=1, bytes_accessed=1, transcendentals=0),
        )(*ins, *before)

    plan.core("rest.half", partial(rest_final, 0), rest_out[:1])
    plan.core("rest.final", partial(rest_final, 1), [rest_out[1], "rest.half"])
    values = plan.run()
    small_all = values[small_value]
    project_grad, merge_grad = values["rest.final"]
    peaks = small_all[9:12, 0]
    return (
        output,
        values[input_task],
        jnp.transpose(project_grad, (1, 0, 2)),
        merge_grad,
        values["up.final"],
        values["down.final"],
        small_all[8].reshape(2, LANES),
        small_all[4],
        small_all[6:8].reshape(hidden),
        small_all[5],
        small_all[0:2],
        small_all[2:4],
        DECAY * clip_scales + (1.0 - DECAY) * peaks,
    )


def solution(mesh):
    return jax.shard_map(
        local,
        mesh=mesh,
        in_specs=(
            P(("dp", "tensor"), None),
            P("dp"),
            P(None, None, "tensor"),
            P("tensor", None),
            P(None, "tensor"),
            P("tensor", None),
            P(None, "tensor"),
            P(),
            P("tensor"),
            P(),
            P(),
            P(),
            P(),
            P(("dp", "tensor"), None),
        ),
        out_specs=(
            P(("dp", "tensor"), None),
            P(("dp", "tensor"), None),
            P(None, None, "tensor"),
            P("tensor", None),
            P(None, "tensor"),
            P("tensor", None),
            P(None, "tensor"),
            P(),
            P("tensor"),
            P(),
            P(),
            P(),
            P(),
        ),
        check_vma=False,
    )
```
